128 devices in a mesh: row: 16 (over x_hi, y, core), col: 8 (over z, x_lo).
Axes of the slice: x: 4 (x_hi: 2, x_lo: 2; x = x_hi * 2 + x_lo), y: 4, z: 4, core: 2. Of those that a mesh axis runs over, the one named last changes fastest.
Arguments:
- emb_a: bfloat16 [512, 1280], P('row', 'col'), may hold values from -70 to 70
- emb_b: bfloat16 [2048, 1280], P('col', 'row'), may hold values from -8 to 8
- w_query: bfloat16 [1280, 1280], replicated, may hold values from -1 to 1
- w_key: bfloat16 [1280, 1280], replicated, may hold values from -1 to 1
- w_value: bfloat16 [1280, 1280], replicated, may hold values from -0.15625 to 0.15625
- w_out: bfloat16 [1280, 1280], replicated, may hold values from -3 to 3
- w_pair_a: bfloat16 [1280, 64], replicated, may hold values from -0.15625 to 0.15625
- w_pair_b: bfloat16 [1280, 64], replicated, may hold values from -0.15625 to 0.15625
- w_depth: float32 [2, 64, 25], replicated, may hold values from -1.25 to 1.25
- w_point: bfloat16 [2, 64, 64], replicated, may hold values from -0.75 to 0.75
- w_logit: float32 [64], replicated, may hold values from -0.75 to 0.75
Outputs:
- logits: float32 [512, 2048], P('row', 'col')
The draws below stay inside these ranges and needn't reach their ends.
All inputs are finite; a program needn't handle non-finite values.
Results may differ from the reference program's by a relative error of at most 0.024.
Values may be sent and summed in bfloat16 or wider, within the bound.
A program may use at most 64 MiB of HBM per device.

```python
import math
import jax
import jax.numpy as jnp
from jax import lax

E = 1280
H = 16
C = 64
LA_DEV = 32
LA = 512
LB = 2048


def shared_rows(key):
    return jax.random.normal(jax.random.fold_in(key, 101), (LB, E), jnp.float32)


def shared_proj(key):
    return jax.random.normal(jax.random.fold_in(key, 202), (E, E), jnp.float32) * E ** (-0.5)


def draw_emb_b(key, part):
    base_rows = jnp.clip(shared_rows(key), -5.0, 5.0)
    return base_rows.astype(jnp.bfloat16)


def draw_emb_a(key, part):
    positions = jnp.arange(LA).astype(jnp.int32)
    base_rows = jnp.clip(shared_rows(key), -5.0, 5.0)
    key = jax.random.fold_in(key, 1)
    own = jnp.clip(jax.random.normal(key, (LA, E), jnp.float32), -5.0, 5.0)
    source = ((7 * positions + 3) % LB).astype(jnp.int32)
    aligned = 1.2 * jnp.take(base_rows, source, axis=0) + 0.6 * own
    result = jnp.where((positions % 4 == 0)[:, None], aligned, own)
    return result.astype(jnp.bfloat16)


def draw_w_query(key, part):
    weights = shared_proj(key)
    return weights.astype(jnp.bfloat16)


def draw_w_key(key, part):
    weights = shared_proj(key)
    key = jax.random.fold_in(key, 4)
    noise = jax.random.normal(key, (E, E), jnp.float32) * E ** (-0.5)
    return (0.8 * weights + 0.6 * noise).astype(jnp.bfloat16)


def bell_draw(own_key, extent, scale, most, dtype=jnp.bfloat16):
    return jnp.clip(scale * jax.random.normal(own_key, extent, jnp.float32), -most, most).astype(dtype)


def setup_inputs(seed: int = 0) -> dict:
    keys = jax.random.split(jax.random.key(seed), 12)
    emb_a = draw_emb_a(jax.random.fold_in(keys[11], 71), 0)
    emb_b = draw_emb_b(jax.random.fold_in(keys[11], 71), 0)
    w_query = draw_w_query(jax.random.fold_in(keys[11], 71), 0)
    w_key = draw_w_key(jax.random.fold_in(keys[11], 71), 0)
    w_value = bell_draw(keys[4], (E, E), E ** -0.5, 0.15625)
    w_out = bell_draw(keys[5], (E, E), 0.5, 3.0)
    w_pair_a = bell_draw(keys[6], (E, C), E ** -0.5, 0.15625)
    w_pair_b = bell_draw(keys[7], (E, C), E ** -0.5, 0.15625)
    w_depth = bell_draw(keys[8], (2, C, 25), 25 ** -0.5, 1.25, jnp.float32)
    w_point = bell_draw(keys[9], (2, C, C), C ** -0.5, 0.75)
    w_logit = bell_draw(keys[10], (C,), C ** -0.5, 0.75, jnp.float32)
    return dict(emb_a=emb_a, emb_b=emb_b, w_query=w_query, w_key=w_key, w_value=w_value, w_out=w_out, w_pair_a=w_pair_a, w_pair_b=w_pair_b, w_depth=w_depth, w_point=w_point, w_logit=w_logit)


def layer_norm(values, axis):
    centre = values - lax.optimization_barrier(jnp.mean(values, axis, keepdims=True))
    spread = lax.optimization_barrier(jnp.mean(centre * centre, axis, keepdims=True))
    return centre * lax.rsqrt(spread + 1e-05)

def attend(query_block, key_proj, value_proj):
    head_size = E // H
    queries = query_block.astype(jnp.float32).reshape(-1, H, head_size)
    keys_all = key_proj.astype(jnp.float32).reshape(-1, H, head_size)
    values_all = value_proj.astype(jnp.float32).reshape(-1, H, head_size)
    scores = jnp.einsum('ihd,jhd->hij', queries, keys_all) / math.sqrt(head_size)
    highest = lax.optimization_barrier(jnp.max(scores, -1, keepdims=True))
    weights = jnp.exp(scores - highest)
    totals = lax.optimization_barrier(jnp.sum(weights, -1))
    rounded = lax.optimization_barrier(weights.astype(jnp.bfloat16)).astype(jnp.float32)
    mixed = jnp.einsum('hij,jhd->ihd', rounded, values_all) / jnp.transpose(totals)[:, :, None]
    return mixed.reshape(-1, E).astype(jnp.bfloat16)

def ref_block(field, tap_weights, point_weights, keep):
    field_f = field.astype(jnp.float32)
    count_r = field.shape[1]
    count_c = field.shape[2]
    padded = jnp.pad(field_f, ((0, 0), (2, 2), (2, 2)))
    depth = jnp.zeros_like(field_f)
    for offset in range(25):
        shift_r, shift_c = divmod(offset, 5)
        depth = depth + tap_weights[:, offset][:, None, None] * padded[:, shift_r:shift_r + count_r, shift_c:shift_c + count_c]
    normed = lax.optimization_barrier(jax.nn.gelu(layer_norm(depth, 0)).astype(jnp.bfloat16)).astype(jnp.float32)
    update = jnp.einsum('cij,cd->dij', normed, point_weights.astype(jnp.float32))
    result = (field_f + update).astype(jnp.bfloat16)
    return jnp.where(keep, result, jnp.zeros_like(result))

def reference(emb_a, emb_b, w_query, w_key, w_value, w_out, w_pair_a, w_pair_b, w_depth, w_point, w_logit):
    query = jnp.dot(emb_a, w_query, preferred_element_type=jnp.float32).astype(jnp.bfloat16)
    key_proj = jnp.dot(emb_b, w_key, preferred_element_type=jnp.float32).astype(jnp.bfloat16)
    value_proj = jnp.dot(emb_b, w_value, preferred_element_type=jnp.float32).astype(jnp.bfloat16)
    block_len = math.gcd(LA, 512)
    blocks = query.reshape(LA // block_len, block_len, E)
    attended = lax.map(lambda q: attend(q, key_proj, value_proj), blocks).reshape(LA, E)
    hidden_a = emb_a.astype(jnp.float32) + jnp.dot(attended, w_out, preferred_element_type=jnp.float32)
    pair_a = jnp.dot(layer_norm(hidden_a, -1).astype(jnp.bfloat16), w_pair_a, preferred_element_type=jnp.float32)
    pair_b = jnp.dot(emb_b, w_pair_b, preferred_element_type=jnp.float32)
    tile_rows = LA_DEV
    padded_a = jnp.pad(pair_a, ((4, 4), (0, 0)))

    def tile(index):
        start = (index * tile_rows).astype(jnp.int32)
        piece = lax.dynamic_slice_in_dim(padded_a, start, tile_rows + 8, 0)
        positions = start - 4 + jnp.arange(tile_rows + 8).astype(jnp.int32)
        keep = ((positions >= 0) & (positions < LA))[None, :, None]
        field = jnp.transpose(piece)[:, :, None] + jnp.transpose(pair_b)[:, None, :]
        field = jnp.where(keep, field, jnp.zeros_like(field)).astype(jnp.bfloat16)
        field = ref_block(field, w_depth[0], w_point[0], keep)
        field = ref_block(field, w_depth[1], w_point[1], keep)
        return jnp.einsum('c,cij->ij', w_logit, field.astype(jnp.float32))[4:4 + tile_rows]
    tiles = lax.map(tile, jnp.arange(LA // tile_rows).astype(jnp.int32))
    return tiles.reshape(LA, LB)
```

```python
import functools
import math

import jax
import jax.numpy as jnp
from jax import lax
from jax.experimental import pallas as pl
from jax.experimental.pallas import tpu as pltpu
from jax.sharding import PartitionSpec as P

E = 1280
H = 16
D = E // H
C = 64
ROWS = 16
COLS = 8
LA = 512
LB = 2048
TILE_A = LA // ROWS
TILE_B = LB // COLS
HALF = TILE_B // 2
F32 = jnp.float32
BF16 = jnp.bfloat16
MESH = pl.DeviceIdType.MESH
NN = (((1,), (0,)), ((), ()))
NT = (((1,), (1,)), ((), ()))


def dot(a, b, dims=NN):
    return lax.dot_general(a, b, dims, preferred_element_type=F32)


def iota(shape, axis):
    return lax.broadcasted_iota(jnp.int32, shape, axis)


def eye(n):
    return jnp.where(iota((n, n), 0) == iota((n, n), 1), 1.0, 0.0).astype(BF16)


def doubled(n):
    lane = iota((n, 2 * n), 1)
    lane = jnp.where(lane >= n, lane - n, lane)
    return jnp.where(iota((n, 2 * n), 0) == lane, 1.0, 0.0).astype(BF16)


def split3(x):
    high = x.astype(BF16)
    rest = x - high.astype(F32)
    mid = rest.astype(BF16)
    low = (rest - mid.astype(F32)).astype(BF16)
    return high, mid, low


def exact_dot(x, ones, dims=NN):
    return sum(dot(part, ones, dims) for part in split3(x))


def attention(
    ea_h, eb_h, wq_h, wk_h, wv_h, wo_h, wpa_h, wpb_h,
    pa_ref, pb_ref,
    ea, wq, wk, wv, wo, wpa, wpb,
    fb_src, fb_all, fa_all, fa_rows, msg, land,
    pb_own, pb_sib, pb_left, pb_right, pa_own, pa_land,
    in_sem, fb_s, fb_r, fa_s, fa_r, rs_s, rs_r, pb_s, pb_r, pa_s, pa_r,
):
    r = lax.axis_index("row")
    c = lax.axis_index("col")
    k = lax.rem(r, 2)
    p = lax.div(r, 2)
    mine = k * COLS + c

    loads = [
        pltpu.make_async_copy(src, dst, in_sem.at[i])
        for i, (src, dst) in enumerate(
            [(eb_h.at[:, pl.ds(0, HALF)], fb_src.at[0]), (eb_h.at[:, pl.ds(HALF, HALF)], fb_src.at[1]),
             (ea_h, ea), (wq_h, wq), (wk_h, wk), (wv_h, wv),
             (wpb_h, wpb), (wo_h, wo), (wpa_h, wpa)]
        )
    ]
    for load in loads:
        load.start()
    w_eb0, w_eb1, w_ea, w_q, w_k, w_v, w_pb, w_o, w_pa = loads

    def group_peer(e):
        g = lax.rem(mine + e, 2 * COLS)
        return 2 * p + lax.div(g, COLS), lax.rem(g, COLS)

    barrier = pltpu.get_barrier_semaphore()

    def greet(row, col):
        pl.semaphore_signal(barrier, inc=1, device_id=(row, col), device_id_type=MESH)

    @pl.loop(1, ROWS)
    def _(d):
        greet(lax.rem(r + d, ROWS), c)
        greet(*group_peer(d))

    @pl.when((k == 1) & (r < ROWS - 1))
    def _():
        greet(r + 1, 0)

    @pl.when((k == 0) & (r > 0))
    def _():
        greet(r - 2, COLS - 1)

    pa_land[...] = jnp.zeros_like(pa_land)
    w_eb0.wait()
    w_eb1.wait()
    fb_all[pl.ds(r, 1)] = fb_src[pl.ds(k, 1)]
    w_ea.wait()
    fa_all[pl.ds(mine, 1)] = ea[...][None]

    first = (k == 0) & (c == 0) & (p > 0)
    last = (k == 0) & (c == COLS - 1) & (p < ROWS // 2 - 1)
    extra = jnp.where(first, COLS, 0) + jnp.where(last, COLS, 0)
    pl.semaphore_wait(barrier, 2 * (ROWS - 1) + extra)

    def fb_copy(d):
        to = lax.rem(r + d, ROWS)
        return pltpu.make_async_remote_copy(
            src_ref=fb_src.at[lax.rem(to, 2)], dst_ref=fb_all.at[r],
            send_sem=fb_s.at[d], recv_sem=fb_r.at[d],
            device_id=(to, c), device_id_type=MESH)

    def fa_copy(e):
        return pltpu.make_async_remote_copy(
            src_ref=ea, dst_ref=fa_all.at[mine],
            send_sem=fa_s.at[e], recv_sem=fa_r.at[e],
            device_id=group_peer(e), device_id_type=MESH)

    @pl.loop(1, ROWS)
    def _(d):
        fb_copy(d).start()
        fa_copy(d).start()

    @pl.loop(1, ROWS)
    def _(d):
        fa_copy(d).wait_recv()

    fa = jnp.concatenate(
        [jnp.concatenate([fa_all[kk * COLS + cc].astype(F32) for cc in range(COLS)], axis=1)
         for kk in range(2)], axis=0)
    fa_rows[...] = fa
    w_q.wait()
    query = dot(fa.astype(BF16), wq[...]).astype(BF16).astype(F32)
    w_pb.wait()
    wpb2 = jnp.concatenate([wpb[...], wpb[...]], axis=0)

    @pl.loop(1, ROWS)
    def _(d):
        fb_copy(d).wait_recv()

    fb = dot(eye(HALF), fb_all[...].reshape(E, HALF), NT).astype(BF16)
    pb_own[...] = dot(fb, wpb2, NT)

    def sib_copy():
        return pltpu.make_async_remote_copy(
            src_ref=pb_own, dst_ref=pb_sib, send_sem=pb_s.at[0], recv_sem=pb_r.at[0],
            device_id=(2 * p + 1 - k, c), device_id_type=MESH)

    def right_copy(kk):
        return pltpu.make_async_remote_copy(
            src_ref=pb_own.at[pl.ds(HALF - 8, 8)], dst_ref=pb_left,
            send_sem=pb_s.at[1 + kk], recv_sem=pb_r.at[1],
            device_id=(2 * p + kk, lax.rem(c + 1, COLS)), device_id_type=MESH)

    def left_copy(kk):
        return pltpu.make_async_remote_copy(
            src_ref=pb_own.at[pl.ds(0, 8)], dst_ref=pb_right,
            send_sem=pb_s.at[1 + kk], recv_sem=pb_r.at[2],
            device_id=(2 * p + kk, lax.rem(c + COLS - 1, COLS)), device_id_type=MESH)

    sends_right = (k == 1) & (c < COLS - 1)
    sends_left = (k == 0) & (c > 0)
    sib_copy().start()

    @pl.when(sends_right)
    def _():
        right_copy(0).start()
        right_copy(1).start()

    @pl.when(sends_left)
    def _():
        left_copy(0).start()
        left_copy(1).start()

    w_k.wait()
    rows = 2 * TILE_A
    scores = [None] * H
    lane256 = iota((rows, 256), 1)
    for t in range(5):
        key_t = dot(fb, wk[:, 256 * t:256 * t + 256]).astype(BF16)
        parts = []
        for h in range(3 * t, 3 * t + 4):
            low, high = D * h - 256 * t, D * h + D - 256 * t
            parts.append(jnp.where((lane256 >= low) & (lane256 < high),
                                   query[:, 256 * t:256 * t + 256], 0.0))
        found = dot(jnp.concatenate(parts, axis=0).astype(BF16), key_t, NT)
        for n, h in enumerate(range(3 * t, 3 * t + 4)):
            piece = found[rows * n:rows * n + rows]
            scores[h] = piece if scores[h] is None else scores[h] + piece

    lane = iota((rows, 128), 1)
    head_of = lane & (H - 1)
    tops = jnp.zeros((rows, 128), F32)
    totals = jnp.zeros((rows, 128), F32)
    weights = []
    for h in range(H):
        s = scores[h] * (1.0 / math.sqrt(D))
        top = jnp.max(s, axis=1, keepdims=True)
        w = jnp.exp(s - top)
        tops = jnp.where(head_of == h, top, tops)
        totals = jnp.where(head_of == h, jnp.sum(w, axis=1, keepdims=True), totals)
        weights.append(w.astype(BF16))
    t1, t2, t3 = (x.astype(F32) for x in split3(tops))
    n1, n2, _ = (x.astype(F32) for x in split3(totals))
    stats = jnp.where(lane < 16, t1, jnp.where(lane < 32, t2, jnp.where(
        lane < 48, t3, jnp.where(lane < 64, n1, jnp.where(lane < 80, n2, 0.0)))))

    w_v.wait()
    mixed = []
    for t in range(5):
        value_t = dot(fb, wv[:, 256 * t:256 * t + 256]).astype(BF16)
        found = dot(jnp.concatenate(weights[3 * t:3 * t + 4], axis=0), value_t)
        total = None
        for n, h in enumerate(range(3 * t, 3 * t + 4)):
            low, high = D * h - 256 * t, D * h + D - 256 * t
            piece = jnp.where((lane256 >= low) & (lane256 < high),
                              found[rows * n:rows * n + rows], 0.0)
            total = piece if total is None else total + piece
        mixed += [total[:, :128], total[:, 128:]]
    for d in range(COLS):
        block = [m[8 * d:8 * d + 8] for m in mixed + [stats]] + [jnp.zeros((8, 128), F32)]
        msg[d] = jnp.concatenate(block, axis=0).astype(BF16)

    def rs_copy(d):
        to = lax.rem(c + d, COLS)
        return pltpu.make_async_remote_copy(
            src_ref=msg.at[to], dst_ref=land.at[mine],
            send_sem=rs_s.at[d], recv_sem=rs_r.at[mine],
            device_id=(2 * p, to), device_id_type=MESH)

    def rs_arrival(g):
        return pltpu.make_async_remote_copy(
            src_ref=msg.at[0], dst_ref=land.at[g],
            send_sem=rs_s.at[0], recv_sem=rs_r.at[g],
            device_id=(2 * p, c), device_id_type=MESH)

    @pl.when(k == 1)
    def _():
        rs_copy(0).start()

    @pl.loop(1, COLS)
    def _(d):
        rs_copy(d).start()

    sib_copy().wait_recv()

    @pl.when(c > 0)
    def _():
        right_copy(0).wait_recv()

    @pl.when(c < COLS - 1)
    def _():
        left_copy(0).wait_recv()

    left_lane = iota((HALF, 128), 1) < C
    left8 = iota((8, 128), 1) < C
    zero8 = jnp.zeros((8, 128), F32)
    own, sib = pb_own[...], pb_sib[...]
    even = k == 0
    block0 = jnp.where(even, own, sib)
    block1 = jnp.where(even, sib, own)
    from_left = jnp.where(c > 0, pb_left[...], zero8)
    from_right = jnp.where(c < COLS - 1, pb_right[...], zero8)
    pb_ref[0:8] = jnp.where(left8, from_left, block0[HALF - 8:])
    pb_ref[8:8 + HALF] = jnp.where(left_lane, block0, block1)
    pb_ref[8 + HALF:16 + HALF] = jnp.where(left8, block1[:8], from_right)

    def pa_copy(row, col, slot, sem):
        return pltpu.make_async_remote_copy(
            src_ref=pa_own, dst_ref=pa_land.at[slot],
            send_sem=pa_s.at[sem], recv_sem=pa_r.at[slot],
            device_id=(row, col), device_id_type=MESH)

    targets = (
        (2 * p, c + 1, c <= 4, 0),
        (2 * p + 1, c - 3, c >= 3, 8),
        (2 * p - 1, 5, (c == 0) & (p > 0), 8),
        (2 * p + 2, 0, (c == COLS - 1) & (p < ROWS // 2 - 1), 0),
    )
    w_o.wait()
    w_pa.wait()

    @pl.when(k == 0)
    def _():
        land[pl.ds(c, 1)] = msg[pl.ds(c, 1)]

        @pl.loop(0, 2 * COLS)
        def _(g):
            @pl.when(g != c)
            def _():
                rs_arrival(g).wait_recv()

        got = [land[g].astype(F32) for g in range(2 * COLS)]
        stat = jnp.concatenate([x[80:88] for x in got], axis=0).astype(BF16)
        a, b = iota((128, 128), 0), iota((128, 128), 1)
        same = (a & (H - 1)) == (b & (H - 1))
        pick_top = jnp.where(same & (a < 48), 1.0, 0.0).astype(BF16)
        pick_total = jnp.where(same & (a >= 48) & (a < 80), 1.0, 0.0).astype(BF16)
        top = dot(stat, pick_top)
        total = dot(stat, pick_total)
        tops = [top[8 * g:8 * g + 8] for g in range(2 * COLS)]
        summit = functools.reduce(jnp.maximum, tops)
        scales = [jnp.exp(x - summit) for x in tops]
        whole = sum(s * total[8 * g:8 * g + 8] for g, s in enumerate(scales))
        factor = jnp.concatenate([s / whole for s in scales], axis=0)
        high = factor.astype(BF16).astype(F32)
        factor = jnp.where(b < H, high, jnp.where(b < 2 * H, factor - high, 0.0)).astype(BF16)
        l, f = iota((128, E), 0), iota((128, E), 1)
        first = (l & (H - 1)) * D
        spread = jnp.where((l < 2 * H) & (f >= first) & (f < first + D), 1.0, 0.0).astype(BF16)
        factors = dot(factor, spread)
        attended = []
        for t in range(10):
            attended.append(sum(
                got[g][8 * t:8 * t + 8] * factors[8 * g:8 * g + 8, 128 * t:128 * t + 128]
                for g in range(2 * COLS)))
        attended = jnp.concatenate(attended, axis=1).astype(BF16)
        hidden = fa_rows[pl.ds(pl.multiple_of(8 * c, 8), 8), :] + dot(attended, wo[...])
        centre = hidden - jnp.mean(hidden, axis=1, keepdims=True)
        spread_h = jnp.mean(centre * centre, axis=1, keepdims=True)
        normed = (centre * lax.rsqrt(spread_h + 1e-5)).astype(BF16)
        pa_own[...] = dot(normed, jnp.concatenate([wpa[...], wpa[...]], axis=0), NT)
        for row, slot, on, base in targets:
            @pl.when(on)
            def _():
                @pl.loop(0, COLS)
                def _(col):
                    local = (row == r) & (col == c)

                    @pl.when(local)
                    def _():
                        pa_land[pl.ds(slot, 1)] = pa_own[...][None]

                    @pl.when(jnp.logical_not(local))
                    def _():
                        pa_copy(row, col, slot, base + col).start()

    mine_slot = jnp.where((k == 0) & (c <= 4), c + 1, -1)

    @pl.loop(0, 6)
    def _(s):
        outside = ((s == 0) & (r == 0)) | ((s == 5) & (r == ROWS - 1))

        @pl.when(jnp.logical_not(outside) & (s != mine_slot))
        def _():
            pa_copy(r, c, s, 0).wait_recv()

    for s in range(6):
        pa_ref[8 * s:8 * s + 8] = pa_land[s]

    @pl.loop(1, ROWS)
    def _(d):
        fb_copy(d).wait_send()
        fa_copy(d).wait_send()

    sib_copy().wait_send()

    @pl.when(sends_right)
    def _():
        right_copy(0).wait_send()
        right_copy(1).wait_send()

    @pl.when(sends_left)
    def _():
        left_copy(0).wait_send()
        left_copy(1).wait_send()

    @pl.when(k == 1)
    def _():
        rs_copy(0).wait_send()

    @pl.loop(1, COLS)
    def _(d):
        rs_copy(d).wait_send()

    @pl.when(k == 0)
    def _():
        for row, slot, on, base in targets:
            @pl.when(on)
            def _():
                @pl.loop(0, COLS)
                def _(col):
                    @pl.when(jnp.logical_not((row == r) & (col == c)))
                    def _():
                        pa_copy(row, col, slot, base + col).wait_send()


def gelu(x):
    inner = x * (0.7978845608028654 + 0.035677408136300125 * (x * x))
    return (0.5 * x) * (1.0 + jnp.tanh(inner))


WIDE = 136


def pair_map(pa_ref, pb_ref, wd_ref, wp_ref, wl_ref, out_ref,
             taps, a_mid, a_edge, b_part, pb_mid, pb_in, f1, logits):
    r = lax.axis_index("row")
    c = lax.axis_index("col")
    a, b = iota((128, 128), 0), iota((128, 128), 1)
    same_half = (a < C) == (b < C)
    mean_of = jnp.where(same_half, 1.0 / C, 0.0).astype(BF16)
    double = doubled(C)

    for s in range(2):
        taps[s] = exact_dot(wd_ref[s], double)
    point = dot(wp_ref[0], double)
    point = jnp.where(same_half, jnp.concatenate([point, point], axis=0), 0.0).astype(BF16)
    read = jnp.broadcast_to(wl_ref[...], (8, C))
    folded = exact_dot(read, wp_ref[1], NT)
    row8, lane8 = iota((8, 128), 0), iota((8, 128), 1)
    half8 = (row8 & 1) == jnp.where(lane8 < C, 0, 1)

    def readout(x):
        both = exact_dot(x, double)
        high = both.astype(BF16).astype(F32)
        picked = jnp.where(row8 < 2, high, jnp.where(row8 < 4, both - high, 0.0))
        return jnp.where(half8, picked, 0.0).astype(BF16)

    heads = jnp.concatenate([readout(read), readout(folded)], axis=1)

    q48 = iota((48, 128), 0) + (TILE_A * r - 8)
    pa = jnp.where((q48 >= 0) & (q48 < LA), pa_ref[...], 0.0)
    q144, l144 = iota((144, 128), 0), iota((144, 128), 1)
    col144 = q144 + TILE_B * c + jnp.where(l144 < C, -4, HALF - 4)
    ok144 = (col144 >= 0) & (col144 < LB) & (q144 < WIDE)
    pb_in[0:140] = pb_ref[4:144]
    pb_in[140:144] = jnp.zeros((4, 128), F32)
    pb = jnp.where(ok144, pb_in[...], 0.0)
    pb_in[...] = pb
    pb_mid[...] = pb_in[2:2 + WIDE]
    ok = jnp.where(ok144, 1.0, 0.0)

    def tap(u, v):
        return taps[0, 5 * u + v:5 * u + v + 1, :]

    def centred(x):
        return x - exact_dot(x, mean_of)

    a_sum = None
    for u in range(5):
        weight = sum(tap(u, v) for v in range(5))
        piece = weight * pa[4 + u:44 + u]
        a_sum = piece if a_sum is None else a_sum + piece
    a_mid[...] = centred(a_sum)
    for n, start in enumerate((0, WIDE - 8)):
        weights = [sum(tap(u, v) * ok[start + v:start + v + 8] for v in range(5)) for u in range(5)]
        for i in range(36):
            value = sum(weights[u] * pa[4 + u + i:5 + u + i] for u in range(5))
            a_edge[n, 8 * i:8 * i + 8] = value
        a_edge[n] = centred(a_edge[n])
    for n, (low, high) in enumerate(((2, 5), (1, 5), (0, 5), (0, 4), (0, 3))):
        value = None
        for v in range(5):
            weight = sum(tap(u, v) for u in range(low, high))
            piece = weight * pb_in[v:v + WIDE]
            value = piece if value is None else value + piece
        b_part[n] = centred(value)

    vv, ll = iota((WIDE, 128), 0), iota((WIDE, 128), 1)
    col_v = vv + TILE_B * c + jnp.where(ll < C, -2, HALF - 2)
    in_map = (col_v >= 0) & (col_v < LB)
    n_first = 4

    @pl.loop(0, 36 // n_first)
    def _(step):
        xs, bases, keeps = [], [], []
        for s in range(n_first):
            u = step * n_first + s
            row = TILE_A * r - 2 + u
            kind = jnp.where(row == 0, 0, jnp.where(row == 1, 1, jnp.where(
                row == LA - 2, 3, jnp.where(row == LA - 1, 4, 2))))
            part = b_part[kind]
            at = pl.multiple_of(8 * u, 8)
            xs += [part[:8] + a_edge[0, pl.ds(at, 8)],
                   part[8:128] + a_mid[pl.ds(u, 1)],
                   part[128:] + a_edge[1, pl.ds(at, 8)]]
            bases.append(pb_mid[...] + pa_ref[pl.ds(u + 6, 1)])
            keeps.append(in_map & (row >= 0) & (row < LA))
        x = jnp.concatenate(xs, axis=0)
        var = dot((x * x).astype(BF16), mean_of)
        g = gelu(x * lax.rsqrt(var + 1e-5)).astype(BF16)
        update = dot(g, point)
        for s in range(n_first):
            u = step * n_first + s
            field = bases[s] + update[WIDE * s:WIDE * s + WIDE]
            field = jnp.where(keeps[s], field, 0.0).astype(BF16).astype(F32)
            f1[u] = field

    n_second = 4

    @pl.loop(0, TILE_A // n_second)
    def _(step):
        depths, fields = [], []
        for s in range(n_second):
            i = step * n_second + s
            total = None
            for u in range(5):
                for v in range(5):
                    piece = taps[1, 5 * u + v:5 * u + v + 1, :] * f1[i + u, v:v + HALF, :]
                    total = piece if total is None else total + piece
            depths.append(total)
            fields.append(f1[i + 2, 2:2 + HALF, :].astype(BF16))
        depth = jnp.concatenate(depths, axis=0)
        high = depth.astype(BF16)
        low = (depth - high.astype(F32)).astype(BF16)
        x = depth - (dot(high, mean_of) + dot(low, mean_of))
        var = dot((x * x).astype(BF16), mean_of)
        g = gelu(x * lax.rsqrt(var + 1e-5)).astype(BF16)
        both = jnp.concatenate([jnp.concatenate(fields, axis=0), g], axis=1)
        found = dot(heads, both, NT)
        left = found[0:1] + found[2:3]
        right = found[1:2] + found[3:4]
        for s in range(n_second):
            i = step * n_second + s
            logits[pl.ds(i, 1)] = left[:, HALF * s:HALF * s + HALF]
            logits[pl.ds(TILE_A + i, 1)] = right[:, HALF * s:HALF * s + HALF]

    out_ref[:, 0:HALF] = logits[0:TILE_A]
    out_ref[:, HALF:TILE_B] = logits[TILE_A:2 * TILE_A]


def local(
    emb_a, emb_b, w_query, w_key, w_value, w_out, w_pair_a, w_pair_b, w_depth, w_point, w_logit
):
    hbm = pl.BlockSpec(memory_space=pl.ANY)
    vmem = pl.BlockSpec(memory_space=pltpu.VMEM)
    weight = pltpu.VMEM((E, E), BF16)
    dma = pltpu.SemaphoreType.DMA
    pair_a, pair_b = pl.pallas_call(
        attention,
        out_shape=(jax.ShapeDtypeStruct((48, 128), F32), jax.ShapeDtypeStruct((144, 128), F32)),
        in_specs=[hbm] * 8,
        out_specs=(vmem, vmem),
        scratch_shapes=[
            pltpu.VMEM((TILE_A, E // COLS), BF16),
            weight, weight, weight, weight,
            pltpu.VMEM((C, E), BF16),
            pltpu.VMEM((C, E), BF16),
            pltpu.VMEM((2, D, HALF), BF16),
            pltpu.VMEM((ROWS, D, HALF), BF16),
            pltpu.VMEM((2 * COLS, TILE_A, E // COLS), BF16),
            pltpu.VMEM((2 * TILE_A, E), F32),
            pltpu.VMEM((COLS, 96, 128), BF16),
            pltpu.VMEM((2 * COLS, 96, 128), BF16),
            pltpu.VMEM((HALF, 128), F32),
            pltpu.VMEM((HALF, 128), F32),
            pltpu.VMEM((8, 128), F32),
            pltpu.VMEM((8, 128), F32),
            pltpu.VMEM((8, 128), F32),
            pltpu.VMEM((6, 8, 128), F32),
            dma((9,)),
            dma((16,)), dma((16,)),
            dma((16,)), dma((16,)),
            dma((8,)), dma((16,)),
            dma((3,)), dma((3,)),
            dma((16,)), dma((6,)),
        ],
        compiler_params=pltpu.CompilerParams(
            collective_id=0, has_side_effects=True, vmem_limit_bytes=60 * 2 ** 20),
        name="attention",
    )(emb_a, emb_b.T, w_query, w_key, w_value, w_out, w_pair_a.T, w_pair_b.T)
    return pl.pallas_call(
        pair_map,
        out_shape=jax.ShapeDtypeStruct((TILE_A, TILE_B), F32),
        in_specs=[vmem] * 5,
        out_specs=vmem,
        scratch_shapes=[
            pltpu.VMEM((2, 25, 128), F32),
            pltpu.VMEM((40, 128), F32),
            pltpu.VMEM((2, 288, 128), F32),
            pltpu.VMEM((5, WIDE, 128), F32),
            pltpu.VMEM((WIDE, 128), F32),
            pltpu.VMEM((144, 128), F32),
            pltpu.VMEM((36, WIDE, 128), F32),
            pltpu.VMEM((2 * TILE_A, 128), F32),
        ],
        compiler_params=pltpu.CompilerParams(vmem_limit_bytes=32 * 2 ** 20),
        name="pair_map",
    )(pair_a, pair_b, jnp.swapaxes(w_depth, 1, 2), w_point, w_logit.reshape(1, C))


def solution(mesh):
    in_specs = (P("row", "col"), P("col", "row"), P(), P(), P(), P(), P(), P(), P(), P(), P())
    out_specs = P("row", "col")
    return jax.shard_map(local, mesh=mesh, in_specs=in_specs, out_specs=out_specs, check_vma=False)
```

```python
import functools
import math

import jax
import jax.numpy as jnp
from jax import lax
from jax.experimental import pallas as pl
from jax.experimental.pallas import tpu as pltpu
from jax.sharding import PartitionSpec as P

E = 1280
H = 16
D = E // H
C = 64
ROWS = 16
COLS = 8
LA = 512
LB = 2048
TILE_A = LA // ROWS
TILE_B = LB // COLS
HALF = TILE_B // 2
F32 = jnp.float32
BF16 = jnp.bfloat16
MESH = pl.DeviceIdType.MESH
NN = (((1,), (0,)), ((), ()))
NT = (((1,), (1,)), ((), ()))


def dot(a, b, dims=NN):
    return lax.dot_general(a, b, dims, preferred_element_type=F32)


def iota(shape, axis):
    return lax.broadcasted_iota(jnp.int32, shape, axis)


def eye(n):
    return jnp.where(iota((n, n), 0) == iota((n, n), 1), 1.0, 0.0).astype(BF16)


def doubled(n):
    lane = iota((n, 2 * n), 1)
    lane = jnp.where(lane >= n, lane - n, lane)
    return jnp.where(iota((n, 2 * n), 0) == lane, 1.0, 0.0).astype(BF16)


def split3(x):
    high = x.astype(BF16)
    rest = x - high.astype(F32)
    mid = rest.astype(BF16)
    low = (rest - mid.astype(F32)).astype(BF16)
    return high, mid, low


def exact_dot(x, ones, dims=NN):
    return sum(dot(part, ones, dims) for part in split3(x))


QW = 136


def prepare_weights(wd, wp, wl, taps, row_w, edge_w, conv_w, point_w, head_w, c):
    double = doubled(C)
    for s in range(2):
        taps[s, 0:25] = exact_dot(wd[:, s, :], double)

    def tap(u, v):
        return taps[0, 5 * u + v:5 * u + v + 1, :]

    for u in range(5):
        row_w[u:u + 1] = sum(tap(u, v) for v in range(5))
    for n, start in enumerate((0, QW - 8)):
        column = 2 * (iota((8, 128), 0) + start) + jnp.where(iota((8, 128), 1) < C, 0, 1)
        column = column + TILE_B * c - 2
        for u in range(5):
            total = None
            for v in range(5):
                at = column + (v - 2)
                piece = jnp.where((at >= 0) & (at < LB), tap(u, v), 0.0)
                total = piece if total is None else total + piece
            edge_w[n, u] = total

    a, b = iota((128, 128), 0), iota((128, 128), 1)
    upper, left = a < C, b < C
    same = upper == left
    rest = jnp.where((a & (C - 1)) == (b & (C - 1)), 1.0 - 1.0 / C, -1.0 / C)
    columns = sum(dot(jnp.concatenate([eye(C), eye(C)], axis=0), part, NT)
                  for part in split3(wd[:, 1, :]))

    def spread(u, v):
        if not 0 <= v < 5:
            return 0.0
        return columns[:, 5 * u + v:5 * u + v + 1]

    zero = jnp.zeros((128, 128), BF16)
    for q in range(3):
        blocks = []
        for u in range(5):
            block = jnp.where(same, spread(u, 2 * q),
                              jnp.where(upper, spread(u, 2 * q - 1), spread(u, 2 * q + 1)))
            blocks.append((block * rest).astype(BF16))
        for u in range(6):
            at = 128 * (3 * u + q)
            conv_w[at:at + 128, 0:128] = blocks[u] if u < 5 else zero
            conv_w[at:at + 128, 128:256] = blocks[u - 1] if u > 0 else zero

    point = dot(wp[0], double)
    point = jnp.concatenate([point, point], axis=1)
    point = jnp.concatenate([point] * 4, axis=0)
    fits = (iota((256, 256), 0) // C) == (iota((256, 256), 1) // C)
    point_w[...] = jnp.where(fits, 0.5 * point, 0.0).astype(BF16)

    read = jnp.broadcast_to(wl[...], (8, C))
    folded = 0.5 * sum(dot(part, wp[1], NT) for part in split3(read))
    row8, lane8 = iota((8, 256), 0), iota((8, 256), 1)
    fits8 = (row8 & 3) == (lane8 // C)
    for n, values in enumerate((read, folded)):
        both = exact_dot(values, double)
        both = jnp.concatenate([both, both], axis=1)
        high = both.astype(BF16).astype(F32)
        picked = jnp.where(row8 < 4, high, both - high)
        head_w[:, 256 * n:256 * n + 256] = jnp.where(fits8, picked, 0.0).astype(BF16)


def mean_matrix(n):
    fits = (iota((n, n), 0) // C) == (iota((n, n), 1) // C)
    return jnp.where(fits, 1.0 / C, 0.0).astype(BF16)


def column_part(pb_buf, taps, pb_mid, b_part):
    mean = mean_matrix(128)
    left = iota((1, 128), 1) < C
    plain = [pb_buf[6 + q:6 + q + QW] for q in range(3)]
    pb_mid[...] = plain[1]
    crossed = [pltpu.roll(x, C, 1) for x in plain]

    for n, (low, high) in enumerate(((2, 5), (1, 5), (0, 5), (0, 4), (0, 3))):
        w = [sum(taps[0, 5 * u + v:5 * u + v + 1, :] for u in range(low, high)) for v in range(5)]
        value = (w[0] * plain[0] + w[2] * plain[1] + w[4] * plain[2]
                 + jnp.where(left, w[1], 0.0) * crossed[0]
                 + jnp.where(left, w[3], w[1]) * crossed[1]
                 + jnp.where(left, 0.0, w[3]) * crossed[2])
        b_part[n] = value - exact_dot(value, mean)


def attention(
    ea_h, eb_h, wq_h, wk_h, wv_h, wo_h, wpa_h, wpb_h, wd_h, wp_h, wl_h,
    out_ref,
    pa_buf, pb_mid, b_part, row_w, edge_w, conv_w, point_w, head_w, a_mid, a_edge, f1, logits,
    ea, wq, wk, wv, wo, wpa, wpb, wd, wp, wl,
    fb_src, fb_all, fa_all, fa_rows, msg, land,
    pb_own, pb_sib, pb_left, pb_right, pb_buf, pa_own, pa_land, taps,
    in_sem, fb_s, fb_r, fa_s, fa_r, rs_s, rs_r, pb_s, pb_r, pa_s, pa_r,
):
    r = lax.axis_index("row")
    c = lax.axis_index("col")
    k = lax.rem(r, 2)
    p = lax.div(r, 2)
    mine = k * COLS + c

    loads = [
        pltpu.make_async_copy(src, dst, in_sem.at[i])
        for i, (src, dst) in enumerate(
            [(eb_h.at[:, pl.ds(0, HALF)], fb_src.at[0]), (eb_h.at[:, pl.ds(HALF, HALF)], fb_src.at[1]),
             (ea_h, ea), (wq_h, wq), (wk_h, wk), (wv_h, wv),
             (wpb_h, wpb), (wo_h, wo), (wpa_h, wpa), (wd_h, wd), (wp_h, wp), (wl_h, wl)]
        )
    ]
    for load in loads:
        load.start()
    w_eb0, w_eb1, w_ea, w_q, w_k, w_v, w_pb, w_o, w_pa, w_d, w_p, w_l = loads

    x, y = lax.div(r, 8), lax.rem(p, 4)
    z, xl = lax.div(c, 2), lax.rem(c, 2)

    def row_peer(e):
        return (lax.rem(x + lax.div(e, 8), 2) * 8 + lax.rem(y + lax.rem(lax.div(e, 2), 4), 4) * 2
                + lax.rem(k + lax.rem(e, 2), 2))

    def col_peer(e):
        return lax.rem(z + lax.rem(lax.div(e, 2), 4), 4) * 2 + lax.rem(xl + lax.rem(e, 2), 2)

    barrier = pltpu.get_barrier_semaphore()

    def greet(row, col):
        pl.semaphore_signal(barrier, inc=1, device_id=(row, col), device_id_type=MESH)

    @pl.loop(1, ROWS)
    def _(n):
        e = ROWS - n
        greet(row_peer(e), c)
        greet(2 * p + lax.rem(k + lax.div(e, 8), 2), col_peer(e))

    @pl.when((k == 1) & (r < ROWS - 1))
    def _():
        greet(r + 1, 0)

    @pl.when((k == 0) & (r > 0))
    def _():
        greet(r - 2, COLS - 1)

    w_eb0.wait()
    w_eb1.wait()
    fb_all[pl.ds(r, 1)] = fb_src[pl.ds(k, 1)]
    w_ea.wait()
    fa_all[pl.ds(k, 1), pl.ds(c, 1)] = ea[...][None, None]

    first = (k == 0) & (c == 0) & (p > 0)
    last = (k == 0) & (c == COLS - 1) & (p < ROWS // 2 - 1)
    extra = jnp.where(first, COLS, 0) + jnp.where(last, COLS, 0)
    pl.semaphore_wait(barrier, 2 * (ROWS - 1) + extra)

    def fb_copy(e):
        to = row_peer(e)
        return pltpu.make_async_remote_copy(
            src_ref=fb_src.at[lax.rem(to, 2)], dst_ref=fb_all.at[r],
            send_sem=fb_s, recv_sem=fb_r,
            device_id=(to, c), device_id_type=MESH)

    def fb_whole():
        return pltpu.make_async_remote_copy(
            src_ref=fb_all.at[pl.ds(0, ROWS - 1)], dst_ref=fb_all.at[pl.ds(0, ROWS - 1)],
            send_sem=fb_s, recv_sem=fb_r, device_id=(2 * p + 1 - k, c), device_id_type=MESH)

    def fa_whole():
        part = fa_all.at[0, pl.ds(0, COLS - 1)]
        return pltpu.make_async_remote_copy(
            src_ref=part, dst_ref=part, send_sem=fa_s.at[1], recv_sem=fa_r.at[1],
            device_id=(2 * p + 1 - k, c), device_id_type=MESH)

    def fa_copy(e):
        return pltpu.make_async_remote_copy(
            src_ref=ea, dst_ref=fa_all.at[k, c],
            send_sem=fa_s.at[1], recv_sem=fa_r.at[1],
            device_id=(r, col_peer(e)), device_id_type=MESH)

    def fa_sibling():
        return pltpu.make_async_remote_copy(
            src_ref=fa_all.at[k], dst_ref=fa_all.at[k],
            send_sem=fa_s.at[0], recv_sem=fa_r.at[0],
            device_id=(2 * p + 1 - k, c), device_id_type=MESH)

    @pl.loop(1, ROWS)
    def _(n):
        fb_copy(ROWS - n).start()

    @pl.loop(1, COLS)
    def _(n):
        fa_copy(COLS - n).start()

    w_d.wait()
    w_p.wait()
    w_l.wait()
    prepare_weights(wd, wp, wl, taps, row_w, edge_w, conv_w, point_w, head_w, c)

    fa_whole().wait_recv()
    fa_sibling().start()
    fa_sibling().wait_recv()
    fa = jnp.concatenate(
        [jnp.concatenate([fa_all[kk, cc].astype(F32) for cc in range(COLS)], axis=1)
         for kk in range(2)], axis=0)
    fa_rows[...] = fa
    w_q.wait()
    query = dot(fa.astype(BF16), wq[...]).astype(BF16).astype(F32)
    w_pb.wait()
    wpb2 = jnp.concatenate([wpb[...], wpb[...]], axis=0)

    fb_whole().wait_recv()
    n0, n1 = iota((HALF, HALF), 0), iota((HALF, HALF), 1)
    order = jnp.where(n0 < HALF // 2, 2 * n0, 2 * n0 - (HALF - 1))
    order = jnp.where(n1 == order, 1.0, 0.0).astype(BF16)
    fb = dot(order, fb_all[...].reshape(E, HALF), NT).astype(BF16)
    found_b = dot(fb, wpb2, NT)
    pb_own[...] = jnp.where(iota((HALF // 2, 128), 1) < C, found_b[:HALF // 2], found_b[HALF // 2:])

    def sib_copy():
        return pltpu.make_async_remote_copy(
            src_ref=pb_own, dst_ref=pb_sib, send_sem=pb_s.at[0], recv_sem=pb_r.at[0],
            device_id=(2 * p + 1 - k, c), device_id_type=MESH)

    def right_copy(kk):
        return pltpu.make_async_remote_copy(
            src_ref=pb_own.at[pl.ds(HALF // 2 - 8, 8)], dst_ref=pb_left,
            send_sem=pb_s.at[1 + kk], recv_sem=pb_r.at[1],
            device_id=(2 * p + kk, lax.rem(c + 1, COLS)), device_id_type=MESH)

    def left_copy(kk):
        return pltpu.make_async_remote_copy(
            src_ref=pb_own.at[pl.ds(0, 8)], dst_ref=pb_right,
            send_sem=pb_s.at[1 + kk], recv_sem=pb_r.at[2],
            device_id=(2 * p + kk, lax.rem(c + COLS - 1, COLS)), device_id_type=MESH)

    sends_right = (k == 1) & (c < COLS - 1)
    sends_left = (k == 0) & (c > 0)
    sib_copy().start()

    @pl.when(sends_right)
    def _():
        right_copy(0).start()
        right_copy(1).start()

    @pl.when(sends_left)
    def _():
        left_copy(0).start()
        left_copy(1).start()

    w_k.wait()
    rows = 2 * TILE_A
    scores = [None] * H
    lane256 = iota((rows, 256), 1)
    for t in range(5):
        key_t = dot(fb, wk[:, 256 * t:256 * t + 256]).astype(BF16)
        parts = []
        for h in range(3 * t, 3 * t + 4):
            low, high = D * h - 256 * t, D * h + D - 256 * t
            parts.append(jnp.where((lane256 >= low) & (lane256 < high),
                                   query[:, 256 * t:256 * t + 256], 0.0))
        found = dot(jnp.concatenate(parts, axis=0).astype(BF16), key_t, NT)
        for n, h in enumerate(range(3 * t, 3 * t + 4)):
            piece = found[rows * n:rows * n + rows]
            scores[h] = piece if scores[h] is None else scores[h] + piece

    lane = iota((rows, 128), 1)
    head_of = lane & (H - 1)
    tops = jnp.zeros((rows, 128), F32)
    totals = jnp.zeros((rows, 128), F32)
    weights = []
    for h in range(H):
        s = scores[h] * (1.0 / math.sqrt(D))
        top = jnp.max(s, axis=1, keepdims=True)
        w = jnp.exp(s - top)
        tops = jnp.where(head_of == h, top, tops)
        totals = jnp.where(head_of == h, jnp.sum(w, axis=1, keepdims=True), totals)
        weights.append(w.astype(BF16))
    t1, t2, t3 = (x.astype(F32) for x in split3(tops))
    n1, n2, _ = (x.astype(F32) for x in split3(totals))
    stats = jnp.where(lane < 16, t1, jnp.where(lane < 32, t2, jnp.where(
        lane < 48, t3, jnp.where(lane < 64, n1, jnp.where(lane < 80, n2, 0.0)))))

    w_v.wait()
    mixed = []
    for t in range(5):
        value_t = dot(fb, wv[:, 256 * t:256 * t + 256]).astype(BF16)
        found = dot(jnp.concatenate(weights[3 * t:3 * t + 4], axis=0), value_t)
        total = None
        for n, h in enumerate(range(3 * t, 3 * t + 4)):
            low, high = D * h - 256 * t, D * h + D - 256 * t
            piece = jnp.where((lane256 >= low) & (lane256 < high),
                              found[rows * n:rows * n + rows], 0.0)
            total = piece if total is None else total + piece
        mixed += [total[:, :128], total[:, 128:]]
    for d in range(COLS):
        block = [m[8 * d:8 * d + 8] for m in mixed + [stats]] + [jnp.zeros((8, 128), F32)]
        msg[d] = jnp.concatenate(block, axis=0).astype(BF16)

    def rs_copy(d):
        to = col_peer(d)
        return pltpu.make_async_remote_copy(
            src_ref=msg.at[to], dst_ref=land.at[mine],
            send_sem=rs_s, recv_sem=rs_r,
            device_id=(2 * p, to), device_id_type=MESH)

    def rs_whole(n):
        return pltpu.make_async_remote_copy(
            src_ref=land.at[pl.ds(0, n)], dst_ref=land.at[pl.ds(0, n)],
            send_sem=rs_s, recv_sem=rs_r, device_id=(2 * p + 1 - k, c), device_id_type=MESH)

    @pl.loop(1, COLS)
    def _(n):
        rs_copy(COLS - n).start()

    @pl.when(k == 1)
    def _():
        rs_copy(0).start()

    sib_copy().wait_recv()

    @pl.when(c > 0)
    def _():
        right_copy(0).wait_recv()

    @pl.when(c < COLS - 1)
    def _():
        left_copy(0).wait_recv()

    zero8 = jnp.zeros((8, 128), F32)
    own, sib = pb_own[...], pb_sib[...]
    even = k == 0
    pb_buf[0:8] = jnp.where(c > 0, pb_left[...], zero8)
    pb_buf[8:72] = jnp.where(even, own, sib)
    pb_buf[72:136] = jnp.where(even, sib, own)
    pb_buf[136:144] = jnp.where(c < COLS - 1, pb_right[...], zero8)
    pb_buf[144:152] = zero8
    column_part(pb_buf, taps, pb_mid, b_part)

    def pa_copy(row, col, slot, sem):
        return pltpu.make_async_remote_copy(
            src_ref=pa_own, dst_ref=pa_land.at[slot],
            send_sem=pa_s.at[sem], recv_sem=pa_r.at[slot],
            device_id=(row, col), device_id_type=MESH)

    def pa_whole(n, sem):
        part = pb_buf.at[pl.ds(0, 8 * n)]
        return pltpu.make_async_remote_copy(
            src_ref=part, dst_ref=part, send_sem=pa_s.at[sem], recv_sem=pa_r.at[0],
            device_id=(2 * p + 1 - k, c), device_id_type=MESH)

    targets = (
        (2 * p - 1, 5, (c == 0) & (p > 0)),
        (2 * p + 2, 0, (c == COLS - 1) & (p < ROWS // 2 - 1)),
        (2 * p, c + 1, c <= 4),
        (2 * p + 1, c - 3, c >= 3),
    )
    w_o.wait()
    w_pa.wait()

    @pl.when(k == 0)
    def _():
        land[pl.ds(c, 1)] = msg[pl.ds(c, 1)]

        rs_whole(2 * COLS - 1).wait_recv()
        got = [land[g].astype(F32) for g in range(2 * COLS)]
        stat = jnp.concatenate([x[80:88] for x in got], axis=0).astype(BF16)
        a, b = iota((128, 128), 0), iota((128, 128), 1)
        same = (a & (H - 1)) == (b & (H - 1))
        pick_top = jnp.where(same & (a < 48), 1.0, 0.0).astype(BF16)
        pick_total = jnp.where(same & (a >= 48) & (a < 80), 1.0, 0.0).astype(BF16)
        top = dot(stat, pick_top)
        total = dot(stat, pick_total)
        tops = [top[8 * g:8 * g + 8] for g in range(2 * COLS)]
        summit = functools.reduce(jnp.maximum, tops)
        scales = [jnp.exp(x - summit) for x in tops]
        whole = sum(s * total[8 * g:8 * g + 8] for g, s in enumerate(scales))
        factor = jnp.concatenate([s / whole for s in scales], axis=0)
        high = factor.astype(BF16).astype(F32)
        factor = jnp.where(b < H, high, jnp.where(b < 2 * H, factor - high, 0.0)).astype(BF16)
        l, f = iota((128, E), 0), iota((128, E), 1)
        first = (l & (H - 1)) * D
        spread = jnp.where((l < 2 * H) & (f >= first) & (f < first + D), 1.0, 0.0).astype(BF16)
        factors = dot(factor, spread)
        attended = []
        for t in range(10):
            attended.append(sum(
                got[g][8 * t:8 * t + 8] * factors[8 * g:8 * g + 8, 128 * t:128 * t + 128]
                for g in range(2 * COLS)))
        attended = jnp.concatenate(attended, axis=1).astype(BF16)
        hidden = fa_rows[pl.ds(pl.multiple_of(8 * c, 8), 8), :] + dot(attended, wo[...])
        centre = hidden - jnp.mean(hidden, axis=1, keepdims=True)
        spread_h = jnp.mean(centre * centre, axis=1, keepdims=True)
        normed = (centre * lax.rsqrt(spread_h + 1e-5)).astype(BF16)
        pa_own[...] = dot(normed, jnp.concatenate([wpa[...], wpa[...]], axis=0), NT)
        for n, (row, slot, on) in enumerate(targets):
            @pl.when(on)
            def _():
                @pl.loop(0, COLS)
                def _(m):
                    col = col_peer(COLS - 1 - m)
                    local = (row == r) & (col == c)

                    @pl.when(local)
                    def _():
                        pa_land[pl.ds(slot, 1)] = pa_own[...][None]

                    @pl.when(jnp.logical_not(local))
                    def _():
                        pa_copy(row, col, slot, n).start()

    fb_whole().wait_send()
    fa_whole().wait_send()
    fa_sibling().wait_send()
    sib_copy().wait_send()

    @pl.when(sends_right)
    def _():
        right_copy(0).wait_send()
        right_copy(1).wait_send()

    @pl.when(sends_left)
    def _():
        left_copy(0).wait_send()
        left_copy(1).wait_send()

    @pl.when(k == 0)
    def _():
        rs_whole(COLS - 1).wait_send()

    @pl.when(k == 1)
    def _():
        rs_whole(COLS).wait_send()

    mean = mean_matrix(256)
    qq = iota((QW, 128), 0)
    in_map = ((qq > 0) | (c > 0)) & ((qq < HALF + 1) | (c < COLS - 1))
    first = functools.partial(
        first_block, r=r, in_map=in_map, mean=mean, pa_buf=pa_buf, pb_mid=pb_mid, b_part=b_part,
        a_mid=a_mid, a_edge=a_edge, point_w=point_w, f1=f1)
    second = functools.partial(
        second_block, mean=mean, conv_w=conv_w, head_w=head_w, f1=f1, logits=logits)
    mine_slot = jnp.where((k == 0) & (c <= 4), c + 1, -1)
    pa_buf[...] = jnp.zeros_like(pa_buf)
    for s in range(1, 5):
        @pl.when(s != mine_slot)
        def _():
            pa_copy(r, c, s, 0).wait_recv()

        pa_buf[8 * s:8 * s + 8] = pa_land[s]
    row_parts(pa_buf, row_w, edge_w, a_mid, a_edge, 4, 32, r)
    for u in range(4, 32, 2):
        first(u)
    second(1)
    second(2)

    @pl.when(r > 0)
    def _():
        pa_copy(r, c, 0, 0).wait_recv()
        pa_buf[0:8] = pa_land[0]

    @pl.when((r < ROWS - 1) & (mine_slot != 5))
    def _():
        pa_copy(r, c, 5, 0).wait_recv()

    @pl.when(r < ROWS - 1)
    def _():
        pa_buf[40:48] = pa_land[5]

    row_parts(pa_buf, row_w, edge_w, a_mid, a_edge, 0, 4, r)
    row_parts(pa_buf, row_w, edge_w, a_mid, a_edge, 32, 36, r)
    for u in (0, 2, 32, 34):
        first(u)
    second(0)
    second(3)
    out_ref[...] = side_by_side(logits)

    @pl.when(k == 0)
    def _():
        for n, (row, slot, on) in enumerate(targets):
            @pl.when(on & (row == r))
            def _():
                pa_whole(COLS - 1, n).wait_send()

            @pl.when(on & (row != r))
            def _():
                pa_whole(COLS, n).wait_send()


def gelu_twice(x):
    inner = x * (0.7978845608028654 + 0.035677408136300125 * (x * x))
    return x + x * jnp.tanh(inner)


def row_parts(pa_buf, row_w, edge_w, a_mid, a_edge, low, high, r):
    mean = mean_matrix(128)
    place = iota((48, 128), 0) + (TILE_A * r - 8)
    pa = jnp.where((place >= 0) & (place < LA), pa_buf[...], 0.0)
    middle = sum(row_w[u:u + 1] * pa[4 + u:44 + u] for u in range(5))
    weights = [[edge_w[n, u] for u in range(5)] for n in range(2)]
    edges = [sum(weights[n][u] * pa[4 + u + i:5 + u + i] for u in range(5))
             for n in range(2) for i in range(low, high)]
    value = jnp.concatenate([middle] + edges, axis=0)
    value = value - exact_dot(value, mean)
    at = 8 * (high - low)
    a_mid[low:high] = value[low:high]
    a_edge[0, 8 * low:8 * high] = value[40:40 + at]
    a_edge[1, 8 * low:8 * high] = value[40 + at:40 + 2 * at]


def first_block(u, r, in_map, mean, pa_buf, pb_mid, b_part, a_mid, a_edge, point_w, f1):
    top, bottom = r == 0, r == ROWS - 1
    kinds = {2: jnp.where(top, 0, 2), 3: jnp.where(top, 1, 2),
             32: jnp.where(bottom, 3, 2), 33: jnp.where(bottom, 4, 2)}

    def first_part(w):
        part = b_part[kinds.get(w, 2)]
        return jnp.concatenate([
            part[:8] + a_edge[0, 8 * w:8 * w + 8],
            part[8:128] + a_mid[w:w + 1],
            part[128:] + a_edge[1, 8 * w:8 * w + 8]], axis=0)

    x = jnp.concatenate([first_part(u), first_part(u + 1)], axis=1)
    var = dot((x * x).astype(BF16), mean)
    g = gelu_twice(x * lax.rsqrt(var + 1e-5)).astype(BF16)
    update = dot(g, point_w[...])
    for n in range(2):
        keep = in_map
        if u < 2:
            keep = keep & jnp.logical_not(top)
        if u >= 34:
            keep = keep & jnp.logical_not(bottom)
        field = pb_mid[...] + pa_buf[u + n + 6:u + n + 7] + update[:, 128 * n:128 * n + 128]
        f1[u + n] = jnp.where(keep, field, 0.0)


def second_block(step, mean, conv_w, head_w, f1, logits):
    pieces = {}
    for u in range(8 * step, 8 * step + 12):
        for q in range(3):
            pieces[u, q] = f1[u, q:q + HALF, :].astype(BF16)
    cols = []
    for u in range(6):
        for q in range(3):
            cols.append(jnp.concatenate(
                [pieces[8 * step + 2 * n + u, q] for n in range(4)], axis=0))
    x = dot(jnp.concatenate(cols, axis=1), conv_w[...])
    var = dot((x * x).astype(BF16), mean)
    g = gelu_twice(x * lax.rsqrt(var + 1e-5)).astype(BF16)
    both = jnp.concatenate([
        jnp.concatenate([pieces[8 * step + 2 * n + 2, 1] for n in range(4)], axis=0),
        jnp.concatenate([pieces[8 * step + 2 * n + 3, 1] for n in range(4)], axis=0), g], axis=1)
    found = dot(head_w[...], both, NT)
    found = found[0:4] + found[4:8]
    for n in range(4):
        for o in range(2):
            for s in range(2):
                at = TILE_A * s + 8 * step + 2 * n + o
                logits[at:at + 1] = found[2 * o + s:2 * o + s + 1, HALF * n:HALF * n + HALF]


def side_by_side(logits):
    total = None
    for s in range(2):
        place = iota((HALF, TILE_B), 1) == 2 * iota((HALF, TILE_B), 0) + s
        place = jnp.where(place, 1.0, 0.0).astype(BF16)
        piece = exact_dot(logits[TILE_A * s:TILE_A * s + TILE_A], place)
        total = piece if total is None else total + piece
    return total


def local(
    emb_a, emb_b, w_query, w_key, w_value, w_out, w_pair_a, w_pair_b, w_depth, w_point, w_logit
):
    hbm = pl.BlockSpec(memory_space=pltpu.HBM)
    vmem = pl.BlockSpec(memory_space=pltpu.VMEM)
    weight = pltpu.VMEM((E, E), BF16)
    dma = pltpu.SemaphoreType.DMA
    return pl.pallas_call(
        attention,
        out_shape=jax.ShapeDtypeStruct((TILE_A, TILE_B), F32),
        in_specs=[hbm] * 11,
        out_specs=vmem,
        scratch_shapes=[
            pltpu.VMEM((48, 128), F32),
            pltpu.VMEM((QW, 128), F32),
            pltpu.VMEM((5, QW, 128), F32),
            pltpu.VMEM((8, 128), F32),
            pltpu.VMEM((2, 5, 8, 128), F32),
            pltpu.VMEM((18 * 128, 256), BF16),
            pltpu.VMEM((256, 256), BF16),
            pltpu.VMEM((8, 512), BF16),
            pltpu.VMEM((40, 128), F32),
            pltpu.VMEM((2, 288, 128), F32),
            pltpu.VMEM((36, QW, 128), F32),
            pltpu.VMEM((2 * TILE_A, 128), F32),
            pltpu.VMEM((TILE_A, E // COLS), BF16),
            weight, weight, weight, weight,
            pltpu.VMEM((C, E), BF16),
            pltpu.VMEM((C, E), BF16),
            pltpu.VMEM((25, 2, C), F32),
            pltpu.VMEM((2, C, C), BF16),
            pltpu.VMEM((1, C), F32),
            pltpu.VMEM((2, D, HALF), BF16),
            pltpu.VMEM((ROWS, D, HALF), BF16),
            pltpu.VMEM((2, COLS, TILE_A, E // COLS), BF16),
            pltpu.VMEM((2 * TILE_A, E), F32),
            pltpu.VMEM((COLS, 96, 128), BF16),
            pltpu.VMEM((2 * COLS, 96, 128), BF16),
            pltpu.VMEM((HALF // 2, 128), F32),
            pltpu.VMEM((HALF // 2, 128), F32),
            pltpu.VMEM((8, 128), F32),
            pltpu.VMEM((8, 128), F32),
            pltpu.VMEM((152, 128), F32),
            pltpu.VMEM((8, 128), F32),
            pltpu.VMEM((6, 8, 128), F32),
            pltpu.VMEM((2, 32, 128), F32),
            dma((12,)),
            dma, dma,
            dma((2,)), dma((2,)),
            dma, dma,
            dma((3,)), dma((3,)),
            dma((4,)), dma((6,)),
        ],
        compiler_params=pltpu.CompilerParams(
            collective_id=0, has_side_effects=True, vmem_limit_bytes=60 * 2 ** 20),
        name="contact_map",
    )(emb_a, emb_b.T, w_query, w_key, w_value, w_out, w_pair_a.T, w_pair_b.T,
      jnp.transpose(w_depth, (2, 0, 1)), w_point, w_logit.reshape(1, C))


def solution(mesh):
    in_specs = (P("row", "col"), P("col", "row"), P(), P(), P(), P(), P(), P(), P(), P(), P())
    out_specs = P("row", "col")
    return jax.shard_map(local, mesh=mesh, in_specs=in_specs, out_specs=out_specs, check_vma=False)
```

```python
import functools
import math

import jax
import jax.numpy as jnp
from jax import lax
from jax.experimental import pallas as pl
from jax.experimental.pallas import tpu as pltpu
from jax.sharding import PartitionSpec as P

E = 1280
H = 16
D = E // H
C = 64
ROWS = 16
COLS = 8
LA = 512
LB = 2048
TILE_A = LA // ROWS
TILE_B = LB // COLS
HALF = TILE_B // 2
F32 = jnp.float32
BF16 = jnp.bfloat16
MESH = pl.DeviceIdType.MESH
NN = (((1,), (0,)), ((), ()))
NT = (((1,), (1,)), ((), ()))


def dot(a, b, dims=NN):
    return lax.dot_general(a, b, dims, preferred_element_type=F32)


def iota(shape, axis):
    return lax.broadcasted_iota(jnp.int32, shape, axis)


def eye(n):
    return jnp.where(iota((n, n), 0) == iota((n, n), 1), 1.0, 0.0).astype(BF16)


def doubled(n):
    lane = iota((n, 2 * n), 1)
    lane = jnp.where(lane >= n, lane - n, lane)
    return jnp.where(iota((n, 2 * n), 0) == lane, 1.0, 0.0).astype(BF16)


def split3(x):
    high = x.astype(BF16)
    rest = x - high.astype(F32)
    mid = rest.astype(BF16)
    low = (rest - mid.astype(F32)).astype(BF16)
    return high, mid, low


def exact_dot(x, ones, dims=NN):
    return sum(dot(part, ones, dims) for part in split3(x))


def near_dot(x, ones):
    high, mid, _ = split3(x)
    return dot(high, ones) + dot(mid, ones)


QW = 136


def prepare_weights(wd, wp, wl, taps, row_w, edge_w, conv_w, point_w, head_w, c):
    double = doubled(C)
    for s in range(2):
        taps[s, 0:25] = exact_dot(wd[:, s, :], double)

    def tap(u, v):
        return taps[0, 5 * u + v:5 * u + v + 1, :]

    for u in range(5):
        row_w[u:u + 1] = sum(tap(u, v) for v in range(5))
    for n, start in enumerate((0, QW - 8)):
        column = 2 * (iota((8, 128), 0) + start) + jnp.where(iota((8, 128), 1) < C, 0, 1)
        column = column + TILE_B * c - 2
        for u in range(5):
            total = None
            for v in range(5):
                at = column + (v - 2)
                piece = jnp.where((at >= 0) & (at < LB), tap(u, v), 0.0)
                total = piece if total is None else total + piece
            edge_w[n, u] = total

    a, b = iota((128, 128), 0), iota((128, 128), 1)
    upper, left = a < C, b < C
    same = upper == left
    rest = jnp.where((a & (C - 1)) == (b & (C - 1)), 1.0 - 1.0 / C, -1.0 / C)
    columns = sum(dot(jnp.concatenate([eye(C), eye(C)], axis=0), part, NT)
                  for part in split3(wd[:, 1, :]))

    def spread(u, v):
        if not 0 <= v < 5:
            return 0.0
        return columns[:, 5 * u + v:5 * u + v + 1]

    zero = jnp.zeros((128, 128), BF16)
    for q in range(3):
        blocks = []
        for u in range(5):
            block = jnp.where(same, spread(u, 2 * q),
                              jnp.where(upper, spread(u, 2 * q - 1), spread(u, 2 * q + 1)))
            blocks.append((block * rest).astype(BF16))
        for u in range(6):
            at = 128 * (3 * u + q)
            conv_w[at:at + 128, 0:128] = blocks[u] if u < 5 else zero
            conv_w[at:at + 128, 128:256] = blocks[u - 1] if u > 0 else zero

    point = dot(wp[0], double)
    point = jnp.concatenate([point, point], axis=1)
    point = jnp.concatenate([point] * 4, axis=0)
    fits = (iota((256, 256), 0) // C) == (iota((256, 256), 1) // C)
    point_w[...] = jnp.where(fits, 0.5 * point, 0.0).astype(BF16)

    read = jnp.broadcast_to(wl[...], (8, C))
    folded = 0.5 * sum(dot(part, wp[1], NT) for part in split3(read))
    row8, lane8 = iota((8, 256), 0), iota((8, 256), 1)
    fits8 = (row8 & 3) == (lane8 // C)
    for n, values in enumerate((read, folded)):
        both = exact_dot(values, double)
        both = jnp.concatenate([both, both], axis=1)
        high = both.astype(BF16).astype(F32)
        picked = jnp.where(row8 < 4, high, both - high)
        head_w[:, 256 * n:256 * n + 256] = jnp.where(fits8, picked, 0.0).astype(BF16)


def mean_matrix(n):
    fits = (iota((n, n), 0) // C) == (iota((n, n), 1) // C)
    return jnp.where(fits, 1.0 / C, 0.0).astype(BF16)


def column_part(pb_buf, taps, pb_mid, b_part):
    mean = mean_matrix(128)
    left = iota((1, 128), 1) < C
    plain = [pb_buf[6 + q:6 + q + QW] for q in range(3)]
    pb_mid[...] = plain[1]
    crossed = [pltpu.roll(x, C, 1) for x in plain]

    for n, (low, high) in enumerate(((2, 5), (1, 5), (0, 5), (0, 4), (0, 3))):
        w = [sum(taps[0, 5 * u + v:5 * u + v + 1, :] for u in range(low, high)) for v in range(5)]
        value = (w[0] * plain[0] + w[2] * plain[1] + w[4] * plain[2]
                 + jnp.where(left, w[1], 0.0) * crossed[0]
                 + jnp.where(left, w[3], w[1]) * crossed[1]
                 + jnp.where(left, 0.0, w[3]) * crossed[2])
        b_part[n] = value - near_dot(value, mean)


def attention(
    ea_h, eb_h, wq_h, wk_h, wv_h, wo_h, wpa_h, wpb_h, wd_h, wp_h, wl_h,
    out_ref,
    pa_buf, pb_mid, b_part, row_w, edge_w, conv_w, point_w, head_w, a_mid, a_edge, f1, logits,
    ea, wq, wk, wv, wo, wpa, wpb, wd, wp, wl,
    fb_src, fb_all, fa_all, fa_rows, msg, land,
    pb_own, pb_sib, pb_left, pb_right, pb_buf, pa_own, pa_land, taps,
    in_sem, fb_s, fb_r, fa_s, fa_r, rs_s, rs_r, pb_s, pb_r, pa_s, pa_r,
):
    r = lax.axis_index("row")
    c = lax.axis_index("col")
    k = lax.rem(r, 2)
    p = lax.div(r, 2)
    mine = k * COLS + c

    loads = [
        pltpu.make_async_copy(src, dst, in_sem.at[i])
        for i, (src, dst) in enumerate(
            [(eb_h.at[:, pl.ds(0, HALF)], fb_src.at[0]), (eb_h.at[:, pl.ds(HALF, HALF)], fb_src.at[1]),
             (ea_h, ea), (wq_h, wq), (wk_h, wk), (wv_h, wv),
             (wpb_h, wpb), (wo_h, wo), (wpa_h, wpa), (wd_h, wd), (wp_h, wp), (wl_h, wl)]
        )
    ]
    for load in loads:
        load.start()
    w_eb0, w_eb1, w_ea, w_q, w_k, w_v, w_pb, w_o, w_pa, w_d, w_p, w_l = loads

    x, y = lax.div(r, 8), lax.rem(p, 4)
    z, xl = lax.div(c, 2), lax.rem(c, 2)

    def row_peer(e):
        return (lax.rem(x + lax.div(e, 8), 2) * 8 + lax.rem(y + lax.rem(lax.div(e, 2), 4), 4) * 2
                + lax.rem(k + lax.rem(e, 2), 2))

    def col_peer(e):
        return lax.rem(z + lax.rem(lax.div(e, 2), 4), 4) * 2 + lax.rem(xl + lax.rem(e, 2), 2)

    barrier = pltpu.get_barrier_semaphore()

    def greet(row, col):
        pl.semaphore_signal(barrier, inc=1, device_id=(row, col), device_id_type=MESH)

    @pl.loop(1, ROWS)
    def _(n):
        e = ROWS - n
        greet(row_peer(e), c)
        greet(2 * p + lax.rem(k + lax.div(e, 8), 2), col_peer(e))

    @pl.when((k == 1) & (r < ROWS - 1))
    def _():
        greet(r + 1, 0)

    @pl.when((k == 0) & (r > 0))
    def _():
        greet(r - 2, COLS - 1)

    w_eb0.wait()
    w_eb1.wait()
    fb_all[pl.ds(r, 1)] = fb_src[pl.ds(k, 1)]
    w_ea.wait()
    fa_all[pl.ds(k, 1), pl.ds(c, 1)] = ea[...][None, None]

    first = (k == 0) & (c == 0) & (p > 0)
    last = (k == 0) & (c == COLS - 1) & (p < ROWS // 2 - 1)
    extra = jnp.where(first, COLS, 0) + jnp.where(last, COLS, 0)
    pl.semaphore_wait(barrier, 2 * (ROWS - 1) + extra)

    def fb_copy(e):
        to = row_peer(e)
        return pltpu.make_async_remote_copy(
            src_ref=fb_src.at[lax.rem(to, 2)], dst_ref=fb_all.at[r],
            send_sem=fb_s, recv_sem=fb_r,
            device_id=(to, c), device_id_type=MESH)

    def fb_whole():
        return pltpu.make_async_remote_copy(
            src_ref=fb_all.at[pl.ds(0, ROWS - 1)], dst_ref=fb_all.at[pl.ds(0, ROWS - 1)],
            send_sem=fb_s, recv_sem=fb_r, device_id=(2 * p + 1 - k, c), device_id_type=MESH)

    def fa_whole():
        part = fa_all.at[0, pl.ds(0, COLS - 1)]
        return pltpu.make_async_remote_copy(
            src_ref=part, dst_ref=part, send_sem=fa_s.at[1], recv_sem=fa_r.at[1],
            device_id=(2 * p + 1 - k, c), device_id_type=MESH)

    def fa_copy(e):
        return pltpu.make_async_remote_copy(
            src_ref=ea, dst_ref=fa_all.at[k, c],
            send_sem=fa_s.at[1], recv_sem=fa_r.at[1],
            device_id=(r, col_peer(e)), device_id_type=MESH)

    def fa_sibling():
        return pltpu.make_async_remote_copy(
            src_ref=fa_all.at[k], dst_ref=fa_all.at[k],
            send_sem=fa_s.at[0], recv_sem=fa_r.at[0],
            device_id=(2 * p + 1 - k, c), device_id_type=MESH)

    @pl.loop(1, COLS)
    def _(n):
        fa_copy(COLS - n).start()

    @pl.loop(1, ROWS)
    def _(n):
        fb_copy(ROWS - n).start()

    w_d.wait()
    w_p.wait()
    w_l.wait()
    prepare_weights(wd, wp, wl, taps, row_w, edge_w, conv_w, point_w, head_w, c)

    fa_whole().wait_recv()
    fa_sibling().start()
    fa_sibling().wait_recv()
    fa = jnp.concatenate(
        [jnp.concatenate([fa_all[kk, cc].astype(F32) for cc in range(COLS)], axis=1)
         for kk in range(2)], axis=0)
    fa_rows[...] = fa
    w_q.wait()
    query = dot(fa.astype(BF16), wq[...]).astype(BF16).astype(F32)
    w_pb.wait()
    wpb2 = jnp.concatenate([wpb[...], wpb[...]], axis=0)

    fb_whole().wait_recv()
    n0, n1 = iota((HALF, HALF), 0), iota((HALF, HALF), 1)
    order = jnp.where(n0 < HALF // 2, 2 * n0, 2 * n0 - (HALF - 1))
    order = jnp.where(n1 == order, 1.0, 0.0).astype(BF16)
    fb = dot(order, fb_all[...].reshape(E, HALF), NT).astype(BF16)
    found_b = dot(fb, wpb2, NT)
    pb_own[...] = jnp.where(iota((HALF // 2, 128), 1) < C, found_b[:HALF // 2], found_b[HALF // 2:])

    def sib_copy():
        return pltpu.make_async_remote_copy(
            src_ref=pb_own, dst_ref=pb_sib, send_sem=pb_s.at[0], recv_sem=pb_r.at[0],
            device_id=(2 * p + 1 - k, c), device_id_type=MESH)

    def right_copy(kk):
        return pltpu.make_async_remote_copy(
            src_ref=pb_own.at[pl.ds(HALF // 2 - 8, 8)], dst_ref=pb_left,
            send_sem=pb_s.at[1 + kk], recv_sem=pb_r.at[1],
            device_id=(2 * p + kk, lax.rem(c + 1, COLS)), device_id_type=MESH)

    def left_copy(kk):
        return pltpu.make_async_remote_copy(
            src_ref=pb_own.at[pl.ds(0, 8)], dst_ref=pb_right,
            send_sem=pb_s.at[1 + kk], recv_sem=pb_r.at[2],
            device_id=(2 * p + kk, lax.rem(c + COLS - 1, COLS)), device_id_type=MESH)

    sends_right = (k == 1) & (c < COLS - 1)
    sends_left = (k == 0) & (c > 0)
    sib_copy().start()

    @pl.when(sends_right)
    def _():
        right_copy(0).start()
        right_copy(1).start()

    @pl.when(sends_left)
    def _():
        left_copy(0).start()
        left_copy(1).start()

    w_k.wait()
    rows = 2 * TILE_A
    scores = [None] * H
    lane256 = iota((rows, 256), 1)
    for t in range(5):
        key_t = dot(fb, wk[:, 256 * t:256 * t + 256]).astype(BF16)
        parts = []
        for h in range(3 * t, 3 * t + 4):
            low, high = D * h - 256 * t, D * h + D - 256 * t
            parts.append(jnp.where((lane256 >= low) & (lane256 < high),
                                   query[:, 256 * t:256 * t + 256], 0.0))
        found = dot(jnp.concatenate(parts, axis=0).astype(BF16), key_t, NT)
        for n, h in enumerate(range(3 * t, 3 * t + 4)):
            piece = found[rows * n:rows * n + rows]
            scores[h] = piece if scores[h] is None else scores[h] + piece

    lane = iota((rows, 128), 1)
    head_of = lane & (H - 1)
    tops = jnp.zeros((rows, 128), F32)
    totals = jnp.zeros((rows, 128), F32)
    weights = []
    for h in range(H):
        s = scores[h] * (1.0 / math.sqrt(D))
        top = jnp.max(s, axis=1, keepdims=True)
        w = jnp.exp(s - top)
        tops = jnp.where(head_of == h, top, tops)
        totals = jnp.where(head_of == h, jnp.sum(w, axis=1, keepdims=True), totals)
        weights.append(w.astype(BF16))
    t1, t2, t3 = (x.astype(F32) for x in split3(tops))
    n1, n2, _ = (x.astype(F32) for x in split3(totals))
    stats = jnp.where(lane < 16, t1, jnp.where(lane < 32, t2, jnp.where(
        lane < 48, t3, jnp.where(lane < 64, n1, jnp.where(lane < 80, n2, 0.0)))))

    w_v.wait()
    mixed = []
    for t in range(5):
        value_t = dot(fb, wv[:, 256 * t:256 * t + 256]).astype(BF16)
        found = dot(jnp.concatenate(weights[3 * t:3 * t + 4], axis=0), value_t)
        total = None
        for n, h in enumerate(range(3 * t, 3 * t + 4)):
            low, high = D * h - 256 * t, D * h + D - 256 * t
            piece = jnp.where((lane256 >= low) & (lane256 < high),
                              found[rows * n:rows * n + rows], 0.0)
            total = piece if total is None else total + piece
        mixed += [total[:, :128], total[:, 128:]]
    for d in range(COLS):
        block = [m[8 * d:8 * d + 8] for m in mixed + [stats]] + [jnp.zeros((8, 128), F32)]
        msg[d] = jnp.concatenate(block, axis=0).astype(BF16)

    def rs_copy(d):
        to = col_peer(d)
        return pltpu.make_async_remote_copy(
            src_ref=msg.at[to], dst_ref=land.at[mine],
            send_sem=rs_s, recv_sem=rs_r,
            device_id=(2 * p, to), device_id_type=MESH)

    def rs_whole(n):
        return pltpu.make_async_remote_copy(
            src_ref=land.at[pl.ds(0, n)], dst_ref=land.at[pl.ds(0, n)],
            send_sem=rs_s, recv_sem=rs_r, device_id=(2 * p + 1 - k, c), device_id_type=MESH)

    @pl.loop(1, COLS)
    def _(n):
        rs_copy(COLS - n).start()

    @pl.when(k == 1)
    def _():
        rs_copy(0).start()

    sib_copy().wait_recv()

    @pl.when(c > 0)
    def _():
        right_copy(0).wait_recv()

    @pl.when(c < COLS - 1)
    def _():
        left_copy(0).wait_recv()

    zero8 = jnp.zeros((8, 128), F32)
    own, sib = pb_own[...], pb_sib[...]
    even = k == 0
    pb_buf[0:8] = jnp.where(c > 0, pb_left[...], zero8)
    pb_buf[8:72] = jnp.where(even, own, sib)
    pb_buf[72:136] = jnp.where(even, sib, own)
    pb_buf[136:144] = jnp.where(c < COLS - 1, pb_right[...], zero8)
    pb_buf[144:152] = zero8
    column_part(pb_buf, taps, pb_mid, b_part)

    def pa_copy(row, col, slot, sem):
        return pltpu.make_async_remote_copy(
            src_ref=pa_own, dst_ref=pa_land.at[slot],
            send_sem=pa_s.at[sem], recv_sem=pa_r.at[slot],
            device_id=(row, col), device_id_type=MESH)

    def pa_whole(n, sem):
        part = pb_buf.at[pl.ds(0, 8 * n)]
        return pltpu.make_async_remote_copy(
            src_ref=part, dst_ref=part, send_sem=pa_s.at[sem], recv_sem=pa_r.at[0],
            device_id=(2 * p + 1 - k, c), device_id_type=MESH)

    targets = (
        (2 * p - 1, 5, (c == 0) & (p > 0)),
        (2 * p + 2, 0, (c == COLS - 1) & (p < ROWS // 2 - 1)),
        (2 * p, c + 1, c <= 4),
        (2 * p + 1, c - 3, c >= 3),
    )
    w_o.wait()
    w_pa.wait()

    @pl.when(k == 0)
    def _():
        land[pl.ds(c, 1)] = msg[pl.ds(c, 1)]

        rs_whole(2 * COLS - 1).wait_recv()
        got = [land[g].astype(F32) for g in range(2 * COLS)]
        stat = jnp.concatenate([x[80:88] for x in got], axis=0).astype(BF16)
        a, b = iota((128, 128), 0), iota((128, 128), 1)
        same = (a & (H - 1)) == (b & (H - 1))
        pick_top = jnp.where(same & (a < 48), 1.0, 0.0).astype(BF16)
        pick_total = jnp.where(same & (a >= 48) & (a < 80), 1.0, 0.0).astype(BF16)
        top = dot(stat, pick_top)
        total = dot(stat, pick_total)
        tops = [top[8 * g:8 * g + 8] for g in range(2 * COLS)]
        summit = functools.reduce(jnp.maximum, tops)
        scales = [jnp.exp(x - summit) for x in tops]
        whole = sum(s * total[8 * g:8 * g + 8] for g, s in enumerate(scales))
        factor = jnp.concatenate([s / whole for s in scales], axis=0)
        high = factor.astype(BF16).astype(F32)
        factor = jnp.where(b < H, high, jnp.where(b < 2 * H, factor - high, 0.0)).astype(BF16)
        l, f = iota((128, E), 0), iota((128, E), 1)
        first = (l & (H - 1)) * D
        spread = jnp.where((l < 2 * H) & (f >= first) & (f < first + D), 1.0, 0.0).astype(BF16)
        factors = dot(factor, spread)
        attended = []
        for t in range(10):
            attended.append(sum(
                got[g][8 * t:8 * t + 8] * factors[8 * g:8 * g + 8, 128 * t:128 * t + 128]
                for g in range(2 * COLS)))
        attended = jnp.concatenate(attended, axis=1).astype(BF16)
        hidden = fa_rows[pl.ds(pl.multiple_of(8 * c, 8), 8), :] + dot(attended, wo[...])
        centre = hidden - jnp.mean(hidden, axis=1, keepdims=True)
        spread_h = jnp.mean(centre * centre, axis=1, keepdims=True)
        normed = (centre * lax.rsqrt(spread_h + 1e-5)).astype(BF16)
        pa_own[...] = dot(normed, jnp.concatenate([wpa[...], wpa[...]], axis=0), NT)
        for n, (row, slot, on) in enumerate(targets):
            @pl.when(on)
            def _():
                @pl.loop(0, COLS)
                def _(m):
                    col = col_peer(COLS - 1 - m)
                    local = (row == r) & (col == c)

                    @pl.when(local)
                    def _():
                        pa_land[pl.ds(slot, 1)] = pa_own[...][None]

                    @pl.when(jnp.logical_not(local))
                    def _():
                        pa_copy(row, col, slot, n).start()

    fb_whole().wait_send()
    fa_whole().wait_send()
    fa_sibling().wait_send()
    sib_copy().wait_send()

    @pl.when(sends_right)
    def _():
        right_copy(0).wait_send()
        right_copy(1).wait_send()

    @pl.when(sends_left)
    def _():
        left_copy(0).wait_send()
        left_copy(1).wait_send()

    @pl.when(k == 0)
    def _():
        rs_whole(COLS - 1).wait_send()

    @pl.when(k == 1)
    def _():
        rs_whole(COLS).wait_send()

    mean = mean_matrix(256)
    qq = iota((QW, 128), 0)
    in_map = ((qq > 0) | (c > 0)) & ((qq < HALF + 1) | (c < COLS - 1))
    first = functools.partial(
        first_blocks, r=r, in_map=in_map, mean=mean, pa_buf=pa_buf, pb_mid=pb_mid, b_part=b_part,
        a_mid=a_mid, a_edge=a_edge, point_w=point_w, f1=f1)
    second = functools.partial(correlate, conv_w=conv_w, f1=f1)
    last_part = functools.partial(read_out, mean=mean, head_w=head_w, logits=logits)
    mine_slot = jnp.where((k == 0) & (c <= 4), c + 1, -1)
    pa_buf[...] = jnp.zeros_like(pa_buf)
    for s in range(1, 5):
        @pl.when(s != mine_slot)
        def _():
            pa_copy(r, c, s, 0).wait_recv()

        pa_buf[8 * s:8 * s + 8] = pa_land[s]
    row_parts(pa_buf, row_w, edge_w, a_mid, a_edge, range(4, 32), r)
    for _ in first(list(range(4, 32, 2))):
        pass
    part1 = second(1)
    part2 = second(2)
    last_part(1, *part1)
    last_part(2, *part2)

    @pl.when(r > 0)
    def _():
        pa_copy(r, c, 0, 0).wait_recv()
        pa_buf[0:8] = pa_land[0]

    @pl.when((r < ROWS - 1) & (mine_slot != 5))
    def _():
        pa_copy(r, c, 5, 0).wait_recv()

    @pl.when(r < ROWS - 1)
    def _():
        pa_buf[40:48] = pa_land[5]

    row_parts(pa_buf, row_w, edge_w, a_mid, a_edge, (0, 1, 2, 3, 32, 33, 34, 35), r)
    for _ in first([0, 2, 32, 34]):
        pass
    part0 = second(0)
    part3 = second(3)
    last_part(0, *part0)
    last_part(3, *part3)
    out_ref[...] = side_by_side(logits)

    @pl.when(k == 0)
    def _():
        for n, (row, slot, on) in enumerate(targets):
            @pl.when(on & (row == r))
            def _():
                pa_whole(COLS - 1, n).wait_send()

            @pl.when(on & (row != r))
            def _():
                pa_whole(COLS, n).wait_send()


def gelu_twice(x):
    inner = x * (0.7978845608028654 + 0.035677408136300125 * (x * x))
    return x + x * jnp.tanh(inner)


def row_parts(pa_buf, row_w, edge_w, a_mid, a_edge, rows, r):
    place = iota((48, 128), 0) + (TILE_A * r - 8)
    pa = jnp.where((place >= 0) & (place < LA), pa_buf[...], 0.0)
    middle = sum(row_w[u:u + 1] * pa[4 + u:44 + u] for u in range(5))
    weights = [[edge_w[n, u] for u in range(5)] for n in range(2)]
    edges = [sum(weights[n][u] * pa[4 + u + i:5 + u + i] for u in range(5))
             for n in range(2) for i in rows]
    value = jnp.concatenate([middle] + edges, axis=0)
    value = value - near_dot(value, mean_matrix(128))
    for m, i in enumerate(rows):
        a_mid[i:i + 1] = value[i:i + 1]
        a_edge[0, 8 * i:8 * i + 8] = value[40 + 8 * m:48 + 8 * m]
        at = 40 + 8 * (len(rows) + m)
        a_edge[1, 8 * i:8 * i + 8] = value[at:at + 8]


def first_blocks(rows, r, in_map, mean, pa_buf, pb_mid, b_part, a_mid, a_edge, point_w, f1):
    top, bottom = r == 0, r == ROWS - 1
    kinds = {2: jnp.where(top, 0, 2), 3: jnp.where(top, 1, 2),
             32: jnp.where(bottom, 3, 2), 33: jnp.where(bottom, 4, 2)}

    def part_of(w):
        part = b_part[kinds.get(w, 2)]
        return jnp.concatenate([
            part[:8] + a_edge[0, 8 * w:8 * w + 8],
            part[8:128] + a_mid[w:w + 1],
            part[128:] + a_edge[1, 8 * w:8 * w + 8]], axis=0)

    def start(u):
        x = jnp.concatenate([part_of(u), part_of(u + 1)], axis=1)
        return x, dot((x * x).astype(BF16), mean)

    def middle(x, var):
        return dot(gelu_twice(x * lax.rsqrt(var + 1e-5)).astype(BF16), point_w[...])

    def end(u, update):
        for n in range(2):
            keep = in_map
            if u < 2:
                keep = keep & jnp.logical_not(top)
            if u >= 34:
                keep = keep & jnp.logical_not(bottom)
            field = pb_mid[...] + pa_buf[u + n + 6:u + n + 7] + update[:, 128 * n:128 * n + 128]
            f1[u + n] = jnp.where(keep, field, 0.0)

    started, updates = {}, {}
    count = len(rows)
    for n in range(count + 2):
        if n < count:
            started[n] = start(rows[n])
        if 1 <= n <= count:
            updates[n - 1] = middle(*started.pop(n - 1))
        if n >= 2:
            end(rows[n - 2], updates.pop(n - 2))
            yield rows[n - 2]


def correlate(step, conv_w, f1):
    pieces = {}
    for u in range(8 * step, 8 * step + 12):
        for q in range(3):
            pieces[u, q] = f1[u, q:q + HALF, :].astype(BF16)

    def tall(u, q):
        return jnp.concatenate([pieces[8 * step + 2 * n + u, q] for n in range(4)], axis=0)

    around = jnp.concatenate([tall(u, q) for u in range(6) for q in range(3)], axis=1)
    return dot(around, conv_w[...]), [tall(2, 1), tall(3, 1)]


def read_out(step, x, field, mean, head_w, logits):
    var = dot((x * x).astype(BF16), mean)
    g = gelu_twice(x * lax.rsqrt(var + 1e-5)).astype(BF16)
    found = dot(head_w[...], jnp.concatenate(field + [g], axis=1), NT)
    found = found[0:4] + found[4:8]
    for n in range(4):
        for o in range(2):
            for s in range(2):
                at = TILE_A * s + 8 * step + 2 * n + o
                logits[at:at + 1] = found[2 * o + s:2 * o + s + 1, HALF * n:HALF * n + HALF]


def side_by_side(logits):
    total = None
    for s in range(2):
        place = iota((HALF, TILE_B), 1) == 2 * iota((HALF, TILE_B), 0) + s
        place = jnp.where(place, 1.0, 0.0).astype(BF16)
        piece = near_dot(logits[TILE_A * s:TILE_A * s + TILE_A], place)
        total = piece if total is None else total + piece
    return total


def local(
    emb_a, emb_b, w_query, w_key, w_value, w_out, w_pair_a, w_pair_b, w_depth, w_point, w_logit
):
    hbm = pl.BlockSpec(memory_space=pltpu.HBM)
    vmem = pl.BlockSpec(memory_space=pltpu.VMEM)
    weight = pltpu.VMEM((E, E), BF16)
    dma = pltpu.SemaphoreType.DMA
    return pl.pallas_call(
        attention,
        out_shape=jax.ShapeDtypeStruct((TILE_A, TILE_B), F32),
        in_specs=[hbm] * 11,
        out_specs=vmem,
        scratch_shapes=[
            pltpu.VMEM((48, 128), F32),
            pltpu.VMEM((QW, 128), F32),
            pltpu.VMEM((5, QW, 128), F32),
            pltpu.VMEM((8, 128), F32),
            pltpu.VMEM((2, 5, 8, 128), F32),
            pltpu.VMEM((18 * 128, 256), BF16),
            pltpu.VMEM((256, 256), BF16),
            pltpu.VMEM((8, 512), BF16),
            pltpu.VMEM((40, 128), F32),
            pltpu.VMEM((2, 288, 128), F32),
            pltpu.VMEM((36, QW, 128), F32),
            pltpu.VMEM((2 * TILE_A, 128), F32),
            pltpu.VMEM((TILE_A, E // COLS), BF16),
            weight, weight, weight, weight,
            pltpu.VMEM((C, E), BF16),
            pltpu.VMEM((C, E), BF16),
            pltpu.VMEM((25, 2, C), F32),
            pltpu.VMEM((2, C, C), BF16),
            pltpu.VMEM((1, C), F32),
            pltpu.VMEM((2, D, HALF), BF16),
            pltpu.VMEM((ROWS, D, HALF), BF16),
            pltpu.VMEM((2, COLS, TILE_A, E // COLS), BF16),
            pltpu.VMEM((2 * TILE_A, E), F32),
            pltpu.VMEM((COLS, 96, 128), BF16),
            pltpu.VMEM((2 * COLS, 96, 128), BF16),
            pltpu.VMEM((HALF // 2, 128), F32),
            pltpu.VMEM((HALF // 2, 128), F32),
            pltpu.VMEM((8, 128), F32),
            pltpu.VMEM((8, 128), F32),
            pltpu.VMEM((152, 128), F32),
            pltpu.VMEM((8, 128), F32),
            pltpu.VMEM((6, 8, 128), F32),
            pltpu.VMEM((2, 32, 128), F32),
            dma((12,)),
            dma, dma,
            dma((2,)), dma((2,)),
            dma, dma,
            dma((3,)), dma((3,)),
            dma((4,)), dma((6,)),
        ],
        compiler_params=pltpu.CompilerParams(
            collective_id=0, has_side_effects=True, vmem_limit_bytes=60 * 2 ** 20),
        name="contact_map",
    )(emb_a, emb_b.T, w_query, w_key, w_value, w_out, w_pair_a.T, w_pair_b.T,
      jnp.transpose(w_depth, (2, 0, 1)), w_point, w_logit.reshape(1, C))


def solution(mesh):
    in_specs = (P("row", "col"), P("col", "row"), P(), P(), P(), P(), P(), P(), P(), P(), P())
    out_specs = P("row", "col")
    return jax.shard_map(local, mesh=mesh, in_specs=in_specs, out_specs=out_specs, check_vma=False)
```

```python
import functools
import math

import jax
import jax.numpy as jnp
from jax import lax
from jax.experimental import pallas as pl
from jax.experimental.pallas import tpu as pltpu
from jax.sharding import PartitionSpec as P

E = 1280
H = 16
D = E // H
C = 64
ROWS = 16
COLS = 8
LA = 512
LB = 2048
TILE_A = LA // ROWS
TILE_B = LB // COLS
HALF = TILE_B // 2
F32 = jnp.float32
BF16 = jnp.bfloat16
MESH = pl.DeviceIdType.MESH
NN = (((1,), (0,)), ((), ()))
NT = (((1,), (1,)), ((), ()))


def dot(a, b, dims=NN):
    return lax.dot_general(a, b, dims, preferred_element_type=F32)


def iota(shape, axis):
    return lax.broadcasted_iota(jnp.int32, shape, axis)


def eye(n):
    return jnp.where(iota((n, n), 0) == iota((n, n), 1), 1.0, 0.0).astype(BF16)


def doubled(n):
    lane = iota((n, 2 * n), 1)
    lane = jnp.where(lane >= n, lane - n, lane)
    return jnp.where(iota((n, 2 * n), 0) == lane, 1.0, 0.0).astype(BF16)


def split3(x):
    high = x.astype(BF16)
    rest = x - high.astype(F32)
    mid = rest.astype(BF16)
    low = (rest - mid.astype(F32)).astype(BF16)
    return high, mid, low


def exact_dot(x, ones, dims=NN):
    return sum(dot(part, ones, dims) for part in split3(x))


def near_dot(x, ones):
    high, mid, _ = split3(x)
    return dot(high, ones) + dot(mid, ones)


QW = 136


def prepare_weights(wd, wp, wl, taps, row_w, edge_w, conv_w, point_w, head_w, c):
    double = doubled(C)
    for s in range(2):
        taps[s, 0:25] = exact_dot(wd[:, s, :], double)

    def tap(u, v):
        return taps[0, 5 * u + v:5 * u + v + 1, :]

    for u in range(5):
        row_w[u:u + 1] = sum(tap(u, v) for v in range(5))
    for n, start in enumerate((0, QW - 8)):
        column = 2 * (iota((8, 128), 0) + start) + jnp.where(iota((8, 128), 1) < C, 0, 1)
        column = column + TILE_B * c - 2
        for u in range(5):
            total = None
            for v in range(5):
                at = column + (v - 2)
                piece = jnp.where((at >= 0) & (at < LB), tap(u, v), 0.0)
                total = piece if total is None else total + piece
            edge_w[n, u] = total

    a, b = iota((128, 128), 0), iota((128, 128), 1)
    upper, left = a < C, b < C
    same = upper == left
    rest = jnp.where((a & (C - 1)) == (b & (C - 1)), 1.0 - 1.0 / C, -1.0 / C)
    columns = sum(dot(jnp.concatenate([eye(C), eye(C)], axis=0), part, NT)
                  for part in split3(wd[:, 1, :]))

    def spread(u, v):
        if not 0 <= v < 5:
            return 0.0
        return columns[:, 5 * u + v:5 * u + v + 1]

    zero = jnp.zeros((128, 128), BF16)
    for q in range(3):
        blocks = []
        for u in range(5):
            block = jnp.where(same, spread(u, 2 * q),
                              jnp.where(upper, spread(u, 2 * q - 1), spread(u, 2 * q + 1)))
            blocks.append((block * rest).astype(BF16))
        for u in range(6):
            at = 128 * (3 * u + q)
            conv_w[at:at + 128, 0:128] = blocks[u] if u < 5 else zero
            conv_w[at:at + 128, 128:256] = blocks[u - 1] if u > 0 else zero

    point = dot(wp[0], double)
    point = jnp.concatenate([point, point], axis=1)
    point = jnp.concatenate([point] * 4, axis=0)
    fits = (iota((256, 256), 0) // C) == (iota((256, 256), 1) // C)
    point_w[...] = jnp.where(fits, 0.5 * point, 0.0).astype(BF16)

    read = jnp.broadcast_to(wl[...], (8, C))
    folded = 0.5 * sum(dot(part, wp[1], NT) for part in split3(read))
    row8, lane8 = iota((8, 256), 0), iota((8, 256), 1)
    fits8 = (row8 & 3) == (lane8 // C)
    for n, values in enumerate((read, folded)):
        both = exact_dot(values, double)
        both = jnp.concatenate([both, both], axis=1)
        high = both.astype(BF16).astype(F32)
        picked = jnp.where(row8 < 4, high, both - high)
        head_w[:, 256 * n:256 * n + 256] = jnp.where(fits8, picked, 0.0).astype(BF16)


def mean_matrix(n):
    fits = (iota((n, n), 0) // C) == (iota((n, n), 1) // C)
    return jnp.where(fits, 1.0 / C, 0.0).astype(BF16)


def column_part(pb_buf, taps, pb_mid, b_part):
    mean = mean_matrix(128)
    left = iota((1, 128), 1) < C
    plain = [pb_buf[6 + q:6 + q + QW] for q in range(3)]
    pb_mid[...] = plain[1]
    crossed = [pltpu.roll(x, C, 1) for x in plain]

    for n, (low, high) in enumerate(((2, 5), (1, 5), (0, 5), (0, 4), (0, 3))):
        w = [sum(taps[0, 5 * u + v:5 * u + v + 1, :] for u in range(low, high)) for v in range(5)]
        value = (w[0] * plain[0] + w[2] * plain[1] + w[4] * plain[2]
                 + jnp.where(left, w[1], 0.0) * crossed[0]
                 + jnp.where(left, w[3], w[1]) * crossed[1]
                 + jnp.where(left, 0.0, w[3]) * crossed[2])
        b_part[n] = value - near_dot(value, mean)


def attention(
    ea_h, eb_h, wq_h, wk_h, wv_h, wo_h, wpa_h, wpb_h, wd_h, wp_h, wl_h,
    out_ref,
    pa_buf, pb_mid, b_part, row_w, edge_w, conv_w, point_w, head_w, a_mid, a_edge, f1, logits,
    ea, wq, wk, wv, wo, wpa, wpb, wd, wp, wl,
    fb_src, fb_all, fa_all, fa_rows, keys, values, spread, msg, land,
    pb_own, pb_sib, pb_left, pb_right, pb_buf, pa_own, pa_land, taps,
    in_sem, fb_s, fb_r, fa_s, fa_r, rs_s, rs_r, pb_s, pb_r, pa_s, pa_r,
):
    r = lax.axis_index("row")
    c = lax.axis_index("col")
    k = lax.rem(r, 2)
    p = lax.div(r, 2)
    mine = k * COLS + c

    loads = [
        pltpu.make_async_copy(src, dst, in_sem.at[i])
        for i, (src, dst) in enumerate(
            [(eb_h.at[:, pl.ds(0, HALF)], fb_src.at[0]), (eb_h.at[:, pl.ds(HALF, HALF)], fb_src.at[1]),
             (ea_h, ea), (wq_h, wq), (wk_h, wk), (wv_h, wv),
             (wpb_h, wpb), (wo_h, wo), (wpa_h, wpa), (wd_h, wd), (wp_h, wp), (wl_h, wl)]
        )
    ]
    for load in loads:
        load.start()
    w_eb0, w_eb1, w_ea, w_q, w_k, w_v, w_pb, w_o, w_pa, w_d, w_p, w_l = loads

    x, y = lax.div(r, 8), lax.rem(p, 4)
    z, xl = lax.div(c, 2), lax.rem(c, 2)

    def row_peer(e):
        return (lax.rem(x + lax.div(e, 8), 2) * 8 + lax.rem(y + lax.rem(lax.div(e, 2), 4), 4) * 2
                + lax.rem(k + lax.rem(e, 2), 2))

    def col_peer(e):
        return lax.rem(z + lax.rem(lax.div(e, 2), 4), 4) * 2 + lax.rem(xl + lax.rem(e, 2), 2)

    barrier = pltpu.get_barrier_semaphore()

    def greet(row, col):
        pl.semaphore_signal(barrier, inc=1, device_id=(row, col), device_id_type=MESH)

    @pl.loop(1, ROWS)
    def _(n):
        e = ROWS - n
        greet(row_peer(e), c)
        greet(2 * p + lax.rem(k + lax.div(e, 8), 2), col_peer(e))

    @pl.when((k == 1) & (r < ROWS - 1))
    def _():
        greet(r + 1, 0)

    @pl.when((k == 0) & (r > 0))
    def _():
        greet(r - 2, COLS - 1)

    w_eb0.wait()
    w_eb1.wait()
    fb_all[pl.ds(r, 1)] = fb_src[pl.ds(k, 1)]
    w_ea.wait()
    fa_all[pl.ds(k, 1), pl.ds(c, 1)] = ea[...][None, None]

    first = (k == 0) & (c == 0) & (p > 0)
    last = (k == 0) & (c == COLS - 1) & (p < ROWS // 2 - 1)
    extra = jnp.where(first, COLS, 0) + jnp.where(last, COLS, 0)
    pl.semaphore_wait(barrier, 2 * (ROWS - 1) + extra)

    def fb_copy(e):
        to = row_peer(e)
        return pltpu.make_async_remote_copy(
            src_ref=fb_src.at[lax.rem(to, 2)], dst_ref=fb_all.at[r],
            send_sem=fb_s, recv_sem=fb_r.at[lax.div(e, 8)],
            device_id=(to, c), device_id_type=MESH)

    def fb_some(n, far):
        part = fb_all.at[pl.ds(0, n)]
        return pltpu.make_async_remote_copy(
            src_ref=part, dst_ref=part, send_sem=fb_s, recv_sem=fb_r.at[far],
            device_id=(2 * p + 1 - k, c), device_id_type=MESH)

    def fa_whole():
        part = fa_all.at[0, pl.ds(0, COLS - 1)]
        return pltpu.make_async_remote_copy(
            src_ref=part, dst_ref=part, send_sem=fa_s.at[1], recv_sem=fa_r.at[1],
            device_id=(2 * p + 1 - k, c), device_id_type=MESH)

    def fa_copy(e):
        return pltpu.make_async_remote_copy(
            src_ref=ea, dst_ref=fa_all.at[k, c],
            send_sem=fa_s.at[1], recv_sem=fa_r.at[1],
            device_id=(r, col_peer(e)), device_id_type=MESH)

    def fa_sibling():
        return pltpu.make_async_remote_copy(
            src_ref=fa_all.at[k], dst_ref=fa_all.at[k],
            send_sem=fa_s.at[0], recv_sem=fa_r.at[0],
            device_id=(2 * p + 1 - k, c), device_id_type=MESH)

    @pl.loop(1, COLS)
    def _(n):
        fa_copy(COLS - n).start()

    @pl.loop(1, ROWS)
    def _(n):
        fb_copy(ROWS - n).start()

    w_d.wait()
    w_p.wait()
    w_l.wait()
    prepare_weights(wd, wp, wl, taps, row_w, edge_w, conv_w, point_w, head_w, c)
    l, f = iota((128, E), 0), iota((128, E), 1)
    start = (l & (H - 1)) * D
    spread[...] = jnp.where((l < 2 * H) & (f >= start) & (f < start + D), 1.0, 0.0).astype(BF16)

    fa_whole().wait_recv()
    fa_sibling().start()

    n0, n1 = iota((HALF, HALF), 0), iota((HALF, HALF), 1)
    order = jnp.where(n0 < HALF // 2, 2 * n0, 2 * n0 - (HALF - 1))
    order = jnp.where(n1 == order, 1.0, 0.0).astype(BF16)

    def features(side):
        blocks = fb_all[pl.ds(8 * side, 8)].reshape(E // 2, HALF)
        return dot(order, blocks, NT).astype(BF16)

    def some_rows(side):
        return pl.ds(pl.multiple_of(side * (E // 2), 128), E // 2)

    def pair_weights(side):
        part = wpb[:, some_rows(side)]
        return jnp.concatenate([part, part], axis=0)

    fb_some(7, 0).wait_recv()
    w_k.wait()
    w_v.wait()
    w_pb.wait()
    near = features(x)
    for t in range(5):
        at = slice(256 * t, 256 * t + 256)
        keys[:, at] = dot(near, wk[some_rows(x), at])
        values[:, at] = dot(near, wv[some_rows(x), at])
    near_b = dot(near, pair_weights(x), NT)

    fa_sibling().wait_recv()
    fa = jnp.concatenate(
        [jnp.concatenate([fa_all[kk, cc].astype(F32) for cc in range(COLS)], axis=1)
         for kk in range(2)], axis=0)
    fa_rows[...] = fa
    w_q.wait()
    query = dot(fa.astype(BF16), wq[...]).astype(BF16).astype(F32)

    fb_some(8, 1).wait_recv()
    far = features(1 - x)
    found_b = near_b + dot(far, pair_weights(1 - x), NT)
    pb_own[...] = jnp.where(iota((HALF // 2, 128), 1) < C, found_b[:HALF // 2], found_b[HALF // 2:])

    def sib_copy():
        return pltpu.make_async_remote_copy(
            src_ref=pb_own, dst_ref=pb_sib, send_sem=pb_s.at[0], recv_sem=pb_r.at[0],
            device_id=(2 * p + 1 - k, c), device_id_type=MESH)

    def right_copy(kk):
        return pltpu.make_async_remote_copy(
            src_ref=pb_own.at[pl.ds(HALF // 2 - 8, 8)], dst_ref=pb_left,
            send_sem=pb_s.at[1 + kk], recv_sem=pb_r.at[1],
            device_id=(2 * p + kk, lax.rem(c + 1, COLS)), device_id_type=MESH)

    def left_copy(kk):
        return pltpu.make_async_remote_copy(
            src_ref=pb_own.at[pl.ds(0, 8)], dst_ref=pb_right,
            send_sem=pb_s.at[1 + kk], recv_sem=pb_r.at[2],
            device_id=(2 * p + kk, lax.rem(c + COLS - 1, COLS)), device_id_type=MESH)

    sends_right = (k == 1) & (c < COLS - 1)
    sends_left = (k == 0) & (c > 0)
    sib_copy().start()

    @pl.when(sends_right)
    def _():
        right_copy(0).start()
        right_copy(1).start()

    @pl.when(sends_left)
    def _():
        left_copy(0).start()
        left_copy(1).start()

    rows = 2 * TILE_A
    lane256 = iota((rows, 256), 1)

    def heads_of(t):
        return range(3 * t, 3 * t + 4)

    def inside(h, t):
        return (lane256 >= D * h - 256 * t) & (lane256 < D * h + D - 256 * t)

    spans = [slice(256 * t, 256 * t + 256) for t in range(5)]
    masked = [jnp.concatenate([jnp.where(inside(h, t), query[:, spans[t]], 0.0)
                               for h in heads_of(t)], axis=0).astype(BF16) for t in range(5)]
    key_parts = [keys[:, at] + dot(far, wk[some_rows(1 - x), at]) for at in spans]
    founds = [dot(masked[t], key_parts[t].astype(BF16), NT) for t in range(5)]
    value_parts = [values[:, at] + dot(far, wv[some_rows(1 - x), at]) for at in spans]
    scores = [None] * H
    for t in range(5):
        for n, h in enumerate(heads_of(t)):
            piece = founds[t][rows * n:rows * n + rows]
            scores[h] = piece if scores[h] is None else scores[h] + piece

    lane = iota((rows, 128), 1)
    head_of = lane & (H - 1)
    tops = jnp.zeros((rows, 128), F32)
    totals = jnp.zeros((rows, 128), F32)
    weights = []
    for h in range(H):
        s = scores[h] * (1.0 / math.sqrt(D))
        top = jnp.max(s, axis=1, keepdims=True)
        w = jnp.exp(s - top)
        tops = jnp.where(head_of == h, top, tops)
        totals = jnp.where(head_of == h, jnp.sum(w, axis=1, keepdims=True), totals)
        weights.append(w.astype(BF16))
    founds = [dot(jnp.concatenate(weights[3 * t:3 * t + 4], axis=0), value_parts[t].astype(BF16))
              for t in range(5)]
    t1, t2, t3 = (x.astype(F32) for x in split3(tops))
    n1, n2, _ = (x.astype(F32) for x in split3(totals))
    stats = jnp.where(lane < 16, t1, jnp.where(lane < 32, t2, jnp.where(
        lane < 48, t3, jnp.where(lane < 64, n1, jnp.where(lane < 80, n2, 0.0)))))

    mixed = []
    for t in range(5):
        total = sum(jnp.where(inside(h, t), founds[t][rows * n:rows * n + rows], 0.0)
                    for n, h in enumerate(heads_of(t)))
        mixed += [total[:, :128], total[:, 128:]]
    for d in range(COLS):
        block = [m[8 * d:8 * d + 8] for m in mixed + [stats]] + [jnp.zeros((8, 128), F32)]
        msg[d] = jnp.concatenate(block, axis=0).astype(BF16)

    def rs_copy(d):
        to = col_peer(d)
        return pltpu.make_async_remote_copy(
            src_ref=msg.at[to], dst_ref=land.at[mine],
            send_sem=rs_s, recv_sem=rs_r,
            device_id=(2 * p, to), device_id_type=MESH)

    def rs_whole(n):
        return pltpu.make_async_remote_copy(
            src_ref=land.at[pl.ds(0, n)], dst_ref=land.at[pl.ds(0, n)],
            send_sem=rs_s, recv_sem=rs_r, device_id=(2 * p + 1 - k, c), device_id_type=MESH)

    @pl.loop(1, COLS)
    def _(n):
        rs_copy(COLS - n).start()

    @pl.when(k == 1)
    def _():
        rs_copy(0).start()

    sib_copy().wait_recv()

    @pl.when(c > 0)
    def _():
        right_copy(0).wait_recv()

    @pl.when(c < COLS - 1)
    def _():
        left_copy(0).wait_recv()

    zero8 = jnp.zeros((8, 128), F32)
    own, sib = pb_own[...], pb_sib[...]
    even = k == 0
    pb_buf[0:8] = jnp.where(c > 0, pb_left[...], zero8)
    pb_buf[8:72] = jnp.where(even, own, sib)
    pb_buf[72:136] = jnp.where(even, sib, own)
    pb_buf[136:144] = jnp.where(c < COLS - 1, pb_right[...], zero8)
    pb_buf[144:152] = zero8
    column_part(pb_buf, taps, pb_mid, b_part)

    def pa_copy(row, col, slot, sem):
        return pltpu.make_async_remote_copy(
            src_ref=pa_own, dst_ref=pa_land.at[slot],
            send_sem=pa_s.at[sem], recv_sem=pa_r.at[slot],
            device_id=(row, col), device_id_type=MESH)

    def pa_whole(n, sem):
        part = pb_buf.at[pl.ds(0, 8 * n)]
        return pltpu.make_async_remote_copy(
            src_ref=part, dst_ref=part, send_sem=pa_s.at[sem], recv_sem=pa_r.at[0],
            device_id=(2 * p + 1 - k, c), device_id_type=MESH)

    targets = (
        (2 * p, c + 1, c <= 4),
        (2 * p + 1, c - 3, c >= 3),
        (2 * p - 1, 5, (c == 0) & (p > 0)),
        (2 * p + 2, 0, (c == COLS - 1) & (p < ROWS // 2 - 1)),
    )
    w_o.wait()
    w_pa.wait()

    @pl.when(k == 0)
    def _():
        land[pl.ds(c, 1)] = msg[pl.ds(c, 1)]

        rs_whole(2 * COLS - 1).wait_recv()
        got = [land[g].astype(F32) for g in range(2 * COLS)]
        stat = jnp.concatenate([x[80:88] for x in got], axis=0).astype(BF16)
        a, b = iota((128, 128), 0), iota((128, 128), 1)
        same = (a & (H - 1)) == (b & (H - 1))
        pick_top = jnp.where(same & (a < 48), 1.0, 0.0).astype(BF16)
        pick_total = jnp.where(same & (a >= 48) & (a < 80), 1.0, 0.0).astype(BF16)
        top = dot(stat, pick_top)
        total = dot(stat, pick_total)
        tops = [top[8 * g:8 * g + 8] for g in range(2 * COLS)]
        summit = functools.reduce(jnp.maximum, tops)
        scales = [jnp.exp(x - summit) for x in tops]
        whole = sum(s * total[8 * g:8 * g + 8] for g, s in enumerate(scales))
        factor = jnp.concatenate([s / whole for s in scales], axis=0)
        high = factor.astype(BF16).astype(F32)
        factor = jnp.where(b < H, high, jnp.where(b < 2 * H, factor - high, 0.0)).astype(BF16)
        factors = dot(factor, spread[...])
        attended = []
        for t in range(10):
            attended.append(sum(
                got[g][8 * t:8 * t + 8] * factors[8 * g:8 * g + 8, 128 * t:128 * t + 128]
                for g in range(2 * COLS)))
        attended = jnp.concatenate(attended, axis=1).astype(BF16)
        hidden = fa_rows[pl.ds(pl.multiple_of(8 * c, 8), 8), :] + dot(attended, wo[...])
        centre = hidden - jnp.mean(hidden, axis=1, keepdims=True)
        spread_h = jnp.mean(centre * centre, axis=1, keepdims=True)
        normed = (centre * lax.rsqrt(spread_h + 1e-5)).astype(BF16)
        pa_own[...] = dot(normed, jnp.concatenate([wpa[...], wpa[...]], axis=0), NT)
        for n, (row, slot, on) in enumerate(targets):
            @pl.when(on)
            def _():
                @pl.loop(0, COLS)
                def _(m):
                    col = col_peer(COLS - 1 - m)
                    local = (row == r) & (col == c)

                    @pl.when(local)
                    def _():
                        pa_land[pl.ds(slot, 1)] = pa_own[...][None]

                    @pl.when(jnp.logical_not(local))
                    def _():
                        pa_copy(row, col, slot, n).start()

    fb_some(ROWS - 1, 0).wait_send()
    fa_whole().wait_send()
    fa_sibling().wait_send()
    sib_copy().wait_send()

    @pl.when(sends_right)
    def _():
        right_copy(0).wait_send()
        right_copy(1).wait_send()

    @pl.when(sends_left)
    def _():
        left_copy(0).wait_send()
        left_copy(1).wait_send()

    @pl.when(k == 0)
    def _():
        rs_whole(COLS - 1).wait_send()

    @pl.when(k == 1)
    def _():
        rs_whole(COLS).wait_send()

    mean = mean_matrix(256)
    qq = iota((QW, 128), 0)
    in_map = ((qq > 0) | (c > 0)) & ((qq < HALF + 1) | (c < COLS - 1))
    first = functools.partial(
        first_blocks, r=r, in_map=in_map, mean=mean, pa_buf=pa_buf, pb_mid=pb_mid, b_part=b_part,
        a_mid=a_mid, a_edge=a_edge, point_w=point_w, f1=f1)
    second = functools.partial(correlate, conv_w=conv_w, f1=f1)
    last_part = functools.partial(read_out, mean=mean, head_w=head_w, logits=logits)
    mine_slot = jnp.where((k == 0) & (c <= 4), c + 1, -1)
    pa_buf[...] = jnp.zeros_like(pa_buf)
    for s in range(1, 5):
        @pl.when(s != mine_slot)
        def _():
            pa_copy(r, c, s, 0).wait_recv()

        pa_buf[8 * s:8 * s + 8] = pa_land[s]
    row_parts(pa_buf, row_w, edge_w, a_mid, a_edge, range(4, 32), r)
    for _ in first(list(range(4, 32, 2))):
        pass
    part1 = second(1)
    part2 = second(2)
    last_part(1, *part1)
    last_part(2, *part2)

    @pl.when(r > 0)
    def _():
        pa_copy(r, c, 0, 0).wait_recv()
        pa_buf[0:8] = pa_land[0]

    @pl.when((r < ROWS - 1) & (mine_slot != 5))
    def _():
        pa_copy(r, c, 5, 0).wait_recv()

    @pl.when(r < ROWS - 1)
    def _():
        pa_buf[40:48] = pa_land[5]

    row_parts(pa_buf, row_w, edge_w, a_mid, a_edge, (0, 1, 2, 3, 32, 33, 34, 35), r)
    for _ in first([0, 2, 32, 34]):
        pass
    part0 = second(0)
    part3 = second(3)
    last_part(0, *part0)
    last_part(3, *part3)
    out_ref[...] = side_by_side(logits)

    @pl.when(k == 0)
    def _():
        for n, (row, slot, on) in enumerate(targets):
            @pl.when(on & (row == r))
            def _():
                pa_whole(COLS - 1, n).wait_send()

            @pl.when(on & (row != r))
            def _():
                pa_whole(COLS, n).wait_send()


def gelu_twice(x):
    inner = x * (0.7978845608028654 + 0.035677408136300125 * (x * x))
    return x + x * jnp.tanh(inner)


def row_parts(pa_buf, row_w, edge_w, a_mid, a_edge, rows, r):
    place = iota((48, 128), 0) + (TILE_A * r - 8)
    pa = jnp.where((place >= 0) & (place < LA), pa_buf[...], 0.0)
    middle = sum(row_w[u:u + 1] * pa[4 + u:44 + u] for u in range(5))
    weights = [[edge_w[n, u] for u in range(5)] for n in range(2)]
    edges = [sum(weights[n][u] * pa[4 + u + i:5 + u + i] for u in range(5))
             for n in range(2) for i in rows]
    value = jnp.concatenate([middle] + edges, axis=0)
    value = value - near_dot(value, mean_matrix(128))
    for m, i in enumerate(rows):
        a_mid[i:i + 1] = value[i:i + 1]
        a_edge[0, 8 * i:8 * i + 8] = value[40 + 8 * m:48 + 8 * m]
        at = 40 + 8 * (len(rows) + m)
        a_edge[1, 8 * i:8 * i + 8] = value[at:at + 8]


def first_blocks(rows, r, in_map, mean, pa_buf, pb_mid, b_part, a_mid, a_edge, point_w, f1):
    top, bottom = r == 0, r == ROWS - 1
    kinds = {2: jnp.where(top, 0, 2), 3: jnp.where(top, 1, 2),
             32: jnp.where(bottom, 3, 2), 33: jnp.where(bottom, 4, 2)}

    def part_of(w):
        part = b_part[kinds.get(w, 2)]
        return jnp.concatenate([
            part[:8] + a_edge[0, 8 * w:8 * w + 8],
            part[8:128] + a_mid[w:w + 1],
            part[128:] + a_edge[1, 8 * w:8 * w + 8]], axis=0)

    def start(u):
        x = jnp.concatenate([part_of(u), part_of(u + 1)], axis=1)
        return x, dot((x * x).astype(BF16), mean)

    def middle(x, var):
        return dot(gelu_twice(x * lax.rsqrt(var + 1e-5)).astype(BF16), point_w[...])

    def end(u, update):
        for n in range(2):
            keep = in_map
            if u < 2:
                keep = keep & jnp.logical_not(top)
            if u >= 34:
                keep = keep & jnp.logical_not(bottom)
            field = pb_mid[...] + pa_buf[u + n + 6:u + n + 7] + update[:, 128 * n:128 * n + 128]
            f1[u + n] = jnp.where(keep, field, 0.0)

    started, updates = {}, {}
    count = len(rows)
    for n in range(count + 2):
        if n < count:
            started[n] = start(rows[n])
        if 1 <= n <= count:
            updates[n - 1] = middle(*started.pop(n - 1))
        if n >= 2:
            end(rows[n - 2], updates.pop(n - 2))
            yield rows[n - 2]


def correlate(step, conv_w, f1):
    pieces = {}
    for u in range(8 * step, 8 * step + 12):
        for q in range(3):
            pieces[u, q] = f1[u, q:q + HALF, :].astype(BF16)

    def tall(u, q):
        return jnp.concatenate([pieces[8 * step + 2 * n + u, q] for n in range(4)], axis=0)

    around = jnp.concatenate([tall(u, q) for u in range(6) for q in range(3)], axis=1)
    return dot(around, conv_w[...]), [tall(2, 1), tall(3, 1)]


def read_out(step, x, field, mean, head_w, logits):
    var = dot((x * x).astype(BF16), mean)
    g = gelu_twice(x * lax.rsqrt(var + 1e-5)).astype(BF16)
    found = dot(head_w[...], jnp.concatenate(field + [g], axis=1), NT)
    found = found[0:4] + found[4:8]
    for n in range(4):
        for o in range(2):
            for s in range(2):
                at = TILE_A * s + 8 * step + 2 * n + o
                logits[at:at + 1] = found[2 * o + s:2 * o + s + 1, HALF * n:HALF * n + HALF]


def side_by_side(logits):
    total = None
    for s in range(2):
        place = iota((HALF, TILE_B), 1) == 2 * iota((HALF, TILE_B), 0) + s
        place = jnp.where(place, 1.0, 0.0).astype(BF16)
        piece = near_dot(logits[TILE_A * s:TILE_A * s + TILE_A], place)
        total = piece if total is None else total + piece
    return total


def local(
    emb_a, emb_b, w_query, w_key, w_value, w_out, w_pair_a, w_pair_b, w_depth, w_point, w_logit
):
    hbm = pl.BlockSpec(memory_space=pltpu.HBM)
    vmem = pl.BlockSpec(memory_space=pltpu.VMEM)
    weight = pltpu.VMEM((E, E), BF16)
    dma = pltpu.SemaphoreType.DMA
    return pl.pallas_call(
        attention,
        out_shape=jax.ShapeDtypeStruct((TILE_A, TILE_B), F32),
        in_specs=[hbm] * 11,
        out_specs=vmem,
        scratch_shapes=[
            pltpu.VMEM((48, 128), F32),
            pltpu.VMEM((QW, 128), F32),
            pltpu.VMEM((5, QW, 128), F32),
            pltpu.VMEM((8, 128), F32),
            pltpu.VMEM((2, 5, 8, 128), F32),
            pltpu.VMEM((18 * 128, 256), BF16),
            pltpu.VMEM((256, 256), BF16),
            pltpu.VMEM((8, 512), BF16),
            pltpu.VMEM((40, 128), F32),
            pltpu.VMEM((2, 288, 128), F32),
            pltpu.VMEM((36, QW, 128), F32),
            pltpu.VMEM((2 * TILE_A, 128), F32),
            pltpu.VMEM((TILE_A, E // COLS), BF16),
            weight, weight, weight, weight,
            pltpu.VMEM((C, E), BF16),
            pltpu.VMEM((C, E), BF16),
            pltpu.VMEM((25, 2, C), F32),
            pltpu.VMEM((2, C, C), BF16),
            pltpu.VMEM((1, C), F32),
            pltpu.VMEM((2, D, HALF), BF16),
            pltpu.VMEM((ROWS, D, HALF), BF16),
            pltpu.VMEM((2, COLS, TILE_A, E // COLS), BF16),
            pltpu.VMEM((2 * TILE_A, E), F32),
            pltpu.VMEM((HALF, E), F32),
            pltpu.VMEM((HALF, E), F32),
            pltpu.VMEM((128, E), BF16),
            pltpu.VMEM((COLS, 96, 128), BF16),
            pltpu.VMEM((2 * COLS, 96, 128), BF16),
            pltpu.VMEM((HALF // 2, 128), F32),
            pltpu.VMEM((HALF // 2, 128), F32),
            pltpu.VMEM((8, 128), F32),
            pltpu.VMEM((8, 128), F32),
            pltpu.VMEM((152, 128), F32),
            pltpu.VMEM((8, 128), F32),
            pltpu.VMEM((6, 8, 128), F32),
            pltpu.VMEM((2, 32, 128), F32),
            dma((12,)),
            dma, dma((2,)),
            dma((2,)), dma((2,)),
            dma, dma,
            dma((3,)), dma((3,)),
            dma((4,)), dma((6,)),
        ],
        compiler_params=pltpu.CompilerParams(
            collective_id=0, has_side_effects=True, vmem_limit_bytes=60 * 2 ** 20),
        name="contact_map",
    )(emb_a, emb_b.T, w_query, w_key, w_value, w_out, w_pair_a.T, w_pair_b.T,
      jnp.transpose(w_depth, (2, 0, 1)), w_point, w_logit.reshape(1, C))


def solution(mesh):
    in_specs = (P("row", "col"), P("col", "row"), P(), P(), P(), P(), P(), P(), P(), P(), P())
    out_specs = P("row", "col")
    return jax.shard_map(local, mesh=mesh, in_specs=in_specs, out_specs=out_specs, check_vma=False)
```

```python
import functools
import math

import jax
import jax.numpy as jnp
from jax import lax
from jax.experimental import pallas as pl
from jax.experimental.pallas import tpu as pltpu
from jax.sharding import PartitionSpec as P

E = 1280
H = 16
D = E // H
C = 64
ROWS = 16
COLS = 8
LA = 512
LB = 2048
TILE_A = LA // ROWS
TILE_B = LB // COLS
HALF = TILE_B // 2
F32 = jnp.float32
BF16 = jnp.bfloat16
MESH = pl.DeviceIdType.MESH
NN = (((1,), (0,)), ((), ()))
NT = (((1,), (1,)), ((), ()))


def dot(a, b, dims=NN):
    return lax.dot_general(a, b, dims, preferred_element_type=F32)


def iota(shape, axis):
    return lax.broadcasted_iota(jnp.int32, shape, axis)


def eye(n):
    return jnp.where(iota((n, n), 0) == iota((n, n), 1), 1.0, 0.0).astype(BF16)


def doubled(n):
    lane = iota((n, 2 * n), 1)
    lane = jnp.where(lane >= n, lane - n, lane)
    return jnp.where(iota((n, 2 * n), 0) == lane, 1.0, 0.0).astype(BF16)


def split3(x):
    high = x.astype(BF16)
    rest = x - high.astype(F32)
    mid = rest.astype(BF16)
    low = (rest - mid.astype(F32)).astype(BF16)
    return high, mid, low


def exact_dot(x, ones, dims=NN):
    return sum(dot(part, ones, dims) for part in split3(x))


def near_dot(x, ones):
    high, mid, _ = split3(x)
    return dot(high, ones) + dot(mid, ones)


QW = 136


def prepare_weights(wd, wp, wl, taps, row_w, edge_w, conv_w, point_w, head_w, c):
    double = doubled(C)
    for s in range(2):
        taps[s, 0:25] = exact_dot(wd[:, s, :], double)

    def tap(u, v):
        return taps[0, 5 * u + v:5 * u + v + 1, :]

    for u in range(5):
        row_w[u:u + 1] = sum(tap(u, v) for v in range(5))
    for n, start in enumerate((0, QW - 8)):
        column = 2 * (iota((8, 128), 0) + start) + jnp.where(iota((8, 128), 1) < C, 0, 1)
        column = column + TILE_B * c - 2
        for u in range(5):
            total = None
            for v in range(5):
                at = column + (v - 2)
                piece = jnp.where((at >= 0) & (at < LB), tap(u, v), 0.0)
                total = piece if total is None else total + piece
            edge_w[n, u] = total

    a, b = iota((128, 128), 0), iota((128, 128), 1)
    upper, left = a < C, b < C
    same = upper == left
    rest = jnp.where((a & (C - 1)) == (b & (C - 1)), 1.0 - 1.0 / C, -1.0 / C)
    columns = sum(dot(jnp.concatenate([eye(C), eye(C)], axis=0), part, NT)
                  for part in split3(wd[:, 1, :]))

    def spread(u, v):
        if not 0 <= v < 5:
            return 0.0
        return columns[:, 5 * u + v:5 * u + v + 1]

    zero = jnp.zeros((128, 128), BF16)
    for q in range(3):
        blocks = []
        for u in range(5):
            block = jnp.where(same, spread(u, 2 * q),
                              jnp.where(upper, spread(u, 2 * q - 1), spread(u, 2 * q + 1)))
            blocks.append((block * rest).astype(BF16))
        for u in range(6):
            at = 128 * (3 * u + q)
            conv_w[at:at + 128, 0:128] = blocks[u] if u < 5 else zero
            conv_w[at:at + 128, 128:256] = blocks[u - 1] if u > 0 else zero

    point = dot(wp[0], double)
    point = jnp.concatenate([point, point], axis=1)
    point = jnp.concatenate([point] * 4, axis=0)
    fits = (iota((256, 256), 0) // C) == (iota((256, 256), 1) // C)
    point_w[...] = jnp.where(fits, 0.5 * point, 0.0).astype(BF16)

    read = jnp.broadcast_to(wl[...], (8, C))
    folded = 0.5 * sum(dot(part, wp[1], NT) for part in split3(read))
    row8, lane8 = iota((8, 256), 0), iota((8, 256), 1)
    fits8 = (row8 & 3) == (lane8 // C)
    for n, values in enumerate((read, folded)):
        both = exact_dot(values, double)
        both = jnp.concatenate([both, both], axis=1)
        high = both.astype(BF16).astype(F32)
        picked = jnp.where(row8 < 4, high, both - high)
        head_w[:, 256 * n:256 * n + 256] = jnp.where(fits8, picked, 0.0).astype(BF16)


def mean_matrix(n):
    fits = (iota((n, n), 0) // C) == (iota((n, n), 1) // C)
    return jnp.where(fits, 1.0 / C, 0.0).astype(BF16)


def column_part(pb_buf, taps, pb_mid, b_part):
    mean = mean_matrix(128)
    left = iota((1, 128), 1) < C
    plain = [pb_buf[6 + q:6 + q + QW] for q in range(3)]
    pb_mid[...] = plain[1]
    crossed = [pltpu.roll(x, C, 1) for x in plain]

    for n, (low, high) in enumerate(((2, 5), (1, 5), (0, 5), (0, 4), (0, 3))):
        w = [sum(taps[0, 5 * u + v:5 * u + v + 1, :] for u in range(low, high)) for v in range(5)]
        value = (w[0] * plain[0] + w[2] * plain[1] + w[4] * plain[2]
                 + jnp.where(left, w[1], 0.0) * crossed[0]
                 + jnp.where(left, w[3], w[1]) * crossed[1]
                 + jnp.where(left, 0.0, w[3]) * crossed[2])
        b_part[n] = value - near_dot(value, mean)


def attention(
    ea_h, eb_h, wq_h, wk_h, wv_h, wo_h, wpa_h, wpb_h, wd_h, wp_h, wl_h,
    out_ref,
    pa_buf, pb_mid, b_part, row_w, edge_w, conv_w, point_w, head_w, a_mid, a_edge, f1, logits,
    ea, wq, wk, wv, wo, wpa, wpb, wd, wp, wl,
    fb_src, fb_all, fa_all, fa_rows, keys, values, spread, msg, land,
    pb_own, pb_sib, pb_left, pb_right, pb_buf, pa_own, pa_land, taps,
    in_sem, fb_s, fb_r, fa_s, fa_r, rs_s, rs_r, pb_s, pb_r, pa_s, pa_r,
):
    r = lax.axis_index("row")
    c = lax.axis_index("col")
    k = lax.rem(r, 2)
    p = lax.div(r, 2)
    mine = k * COLS + c

    loads = [
        pltpu.make_async_copy(src, dst, in_sem.at[i])
        for i, (src, dst) in enumerate(
            [(eb_h.at[:, pl.ds(0, HALF)], fb_src.at[0]), (eb_h.at[:, pl.ds(HALF, HALF)], fb_src.at[1]),
             (ea_h, ea), (wq_h, wq), (wk_h, wk), (wv_h, wv),
             (wpb_h, wpb), (wo_h, wo), (wpa_h, wpa), (wd_h, wd), (wp_h, wp), (wl_h, wl)]
        )
    ]
    for load in loads:
        load.start()
    w_eb0, w_eb1, w_ea, w_q, w_k, w_v, w_pb, w_o, w_pa, w_d, w_p, w_l = loads

    x, y = lax.div(r, 8), lax.rem(p, 4)
    z, xl = lax.div(c, 2), lax.rem(c, 2)

    def row_peer(e):
        return (lax.rem(x + lax.div(e, 8), 2) * 8 + lax.rem(y + lax.rem(lax.div(e, 2), 4), 4) * 2
                + lax.rem(k + lax.rem(e, 2), 2))

    def col_peer(e):
        return lax.rem(z + lax.rem(lax.div(e, 2), 4), 4) * 2 + lax.rem(xl + lax.rem(e, 2), 2)

    barrier = pltpu.get_barrier_semaphore()

    def greet(row, col):
        pl.semaphore_signal(barrier, inc=1, device_id=(row, col), device_id_type=MESH)

    @pl.loop(1, ROWS)
    def _(n):
        e = ROWS - n
        greet(row_peer(e), c)
        greet(2 * p + lax.rem(k + lax.div(e, 8), 2), col_peer(e))

    @pl.when((k == 1) & (r < ROWS - 1))
    def _():
        greet(r + 1, 0)

    @pl.when((k == 0) & (r > 0))
    def _():
        greet(r - 2, COLS - 1)

    w_eb0.wait()
    w_eb1.wait()
    fb_all[pl.ds(r, 1)] = fb_src[pl.ds(k, 1)]
    w_ea.wait()
    fa_all[pl.ds(k, 1), pl.ds(c, 1)] = ea[...][None, None]

    first = (k == 0) & (c == 0) & (p > 0)
    last = (k == 0) & (c == COLS - 1) & (p < ROWS // 2 - 1)
    extra = jnp.where(first, COLS, 0) + jnp.where(last, COLS, 0)
    pl.semaphore_wait(barrier, 2 * (ROWS - 1) + extra)

    def fb_copy(e):
        to = row_peer(e)
        return pltpu.make_async_remote_copy(
            src_ref=fb_src.at[lax.rem(to, 2)], dst_ref=fb_all.at[r],
            send_sem=fb_s, recv_sem=fb_r.at[lax.div(e, 8)],
            device_id=(to, c), device_id_type=MESH)

    def fb_some(n, far):
        part = fb_all.at[pl.ds(0, n)]
        return pltpu.make_async_remote_copy(
            src_ref=part, dst_ref=part, send_sem=fb_s, recv_sem=fb_r.at[far],
            device_id=(2 * p + 1 - k, c), device_id_type=MESH)

    def fa_whole():
        part = fa_all.at[0, pl.ds(0, COLS - 1)]
        return pltpu.make_async_remote_copy(
            src_ref=part, dst_ref=part, send_sem=fa_s.at[1], recv_sem=fa_r.at[1],
            device_id=(2 * p + 1 - k, c), device_id_type=MESH)

    def fa_copy(e):
        return pltpu.make_async_remote_copy(
            src_ref=ea, dst_ref=fa_all.at[k, c],
            send_sem=fa_s.at[1], recv_sem=fa_r.at[1],
            device_id=(r, col_peer(e)), device_id_type=MESH)

    def fa_sibling():
        return pltpu.make_async_remote_copy(
            src_ref=fa_all.at[k], dst_ref=fa_all.at[k],
            send_sem=fa_s.at[0], recv_sem=fa_r.at[0],
            device_id=(2 * p + 1 - k, c), device_id_type=MESH)

    @pl.loop(1, COLS)
    def _(n):
        fa_copy(COLS - n).start()

    @pl.loop(1, ROWS)
    def _(n):
        fb_copy(ROWS - n).start()

    w_d.wait()
    w_p.wait()
    w_l.wait()
    prepare_weights(wd, wp, wl, taps, row_w, edge_w, conv_w, point_w, head_w, c)
    l, f = iota((128, E), 0), iota((128, E), 1)
    start = (l & (H - 1)) * D
    spread[...] = jnp.where((l < 2 * H) & (f >= start) & (f < start + D), 1.0, 0.0).astype(BF16)

    fa_whole().wait_recv()
    fa_sibling().start()

    n0, n1 = iota((HALF, HALF), 0), iota((HALF, HALF), 1)
    order = jnp.where(n0 < HALF // 2, 2 * n0, 2 * n0 - (HALF - 1))
    order = jnp.where(n1 == order, 1.0, 0.0).astype(BF16)

    def features(side):
        blocks = fb_all[pl.ds(8 * side, 8)].reshape(E // 2, HALF)
        return dot(order, blocks, NT).astype(BF16)

    def some_rows(side):
        return pl.ds(pl.multiple_of(side * (E // 2), 128), E // 2)

    def pair_weights(side):
        part = wpb[:, some_rows(side)]
        return jnp.concatenate([part, part], axis=0)

    fb_some(7, 0).wait_recv()
    w_k.wait()
    w_v.wait()
    w_pb.wait()
    near = features(x)
    for t in range(5):
        at = slice(256 * t, 256 * t + 256)
        keys[:, at] = dot(near, wk[some_rows(x), at])
        values[:, at] = dot(near, wv[some_rows(x), at])
    near_b = dot(near, pair_weights(x), NT)

    fa_sibling().wait_recv()
    fa = jnp.concatenate(
        [jnp.concatenate([fa_all[kk, cc].astype(F32) for cc in range(COLS)], axis=1)
         for kk in range(2)], axis=0)
    fa_rows[...] = fa
    w_q.wait()
    query = dot(fa.astype(BF16), wq[...]).astype(BF16).astype(F32)

    fb_some(8, 1).wait_recv()
    far = features(1 - x)
    found_b = near_b + dot(far, pair_weights(1 - x), NT)
    pb_own[...] = jnp.where(iota((HALF // 2, 128), 1) < C, found_b[:HALF // 2], found_b[HALF // 2:])

    def sib_copy():
        return pltpu.make_async_remote_copy(
            src_ref=pb_own, dst_ref=pb_sib, send_sem=pb_s.at[0], recv_sem=pb_r.at[0],
            device_id=(2 * p + 1 - k, c), device_id_type=MESH)

    def right_copy(kk):
        return pltpu.make_async_remote_copy(
            src_ref=pb_own.at[pl.ds(HALF // 2 - 8, 8)], dst_ref=pb_left,
            send_sem=pb_s.at[1 + kk], recv_sem=pb_r.at[1],
            device_id=(2 * p + kk, lax.rem(c + 1, COLS)), device_id_type=MESH)

    def left_copy(kk):
        return pltpu.make_async_remote_copy(
            src_ref=pb_own.at[pl.ds(0, 8)], dst_ref=pb_right,
            send_sem=pb_s.at[1 + kk], recv_sem=pb_r.at[2],
            device_id=(2 * p + kk, lax.rem(c + COLS - 1, COLS)), device_id_type=MESH)

    sends_right = (k == 1) & (c < COLS - 1)
    sends_left = (k == 0) & (c > 0)
    sib_copy().start()

    @pl.when(sends_right)
    def _():
        right_copy(0).start()
        right_copy(1).start()

    @pl.when(sends_left)
    def _():
        left_copy(0).start()
        left_copy(1).start()

    rows = 2 * TILE_A
    lane256 = iota((rows, 256), 1)

    def heads_of(t):
        return range(3 * t, 3 * t + 4)

    def inside(h, t):
        return (lane256 >= D * h - 256 * t) & (lane256 < D * h + D - 256 * t)

    spans = [slice(256 * t, 256 * t + 256) for t in range(5)]
    masked = [jnp.concatenate([jnp.where(inside(h, t), query[:, spans[t]], 0.0)
                               for h in heads_of(t)], axis=0).astype(BF16) for t in range(5)]
    key_parts = [keys[:, at] + dot(far, wk[some_rows(1 - x), at]) for at in spans]
    founds = [dot(masked[t], key_parts[t].astype(BF16), NT) for t in range(5)]
    value_parts = [values[:, at] + dot(far, wv[some_rows(1 - x), at]) for at in spans]
    scores = [None] * H
    for t in range(5):
        for n, h in enumerate(heads_of(t)):
            piece = founds[t][rows * n:rows * n + rows]
            scores[h] = piece if scores[h] is None else scores[h] + piece

    lane = iota((rows, 128), 1)
    head_of = lane & (H - 1)
    tops = jnp.zeros((rows, 128), F32)
    totals = jnp.zeros((rows, 128), F32)
    weights = []
    for h in range(H):
        s = scores[h] * (1.0 / math.sqrt(D))
        top = jnp.max(s, axis=1, keepdims=True)
        w = jnp.exp(s - top)
        tops = jnp.where(head_of == h, top, tops)
        totals = jnp.where(head_of == h, jnp.sum(w, axis=1, keepdims=True), totals)
        weights.append(w.astype(BF16))
    founds = [dot(jnp.concatenate(weights[3 * t:3 * t + 4], axis=0), value_parts[t].astype(BF16))
              for t in range(5)]
    t1, t2, t3 = (x.astype(F32) for x in split3(tops))
    n1, n2, _ = (x.astype(F32) for x in split3(totals))
    stats = jnp.where(lane < 16, t1, jnp.where(lane < 32, t2, jnp.where(
        lane < 48, t3, jnp.where(lane < 64, n1, jnp.where(lane < 80, n2, 0.0)))))

    mixed = []
    for t in range(5):
        total = sum(jnp.where(inside(h, t), founds[t][rows * n:rows * n + rows], 0.0)
                    for n, h in enumerate(heads_of(t)))
        mixed += [total[:, :128], total[:, 128:]]
    for d in range(COLS):
        block = [m[8 * d:8 * d + 8] for m in mixed + [stats]] + [jnp.zeros((8, 128), F32)]
        msg[d] = jnp.concatenate(block, axis=0).astype(BF16)

    def rs_copy(d):
        to = col_peer(d)
        return pltpu.make_async_remote_copy(
            src_ref=msg.at[to], dst_ref=land.at[mine],
            send_sem=rs_s, recv_sem=rs_r,
            device_id=(2 * p, to), device_id_type=MESH)

    def rs_whole(n):
        return pltpu.make_async_remote_copy(
            src_ref=land.at[pl.ds(0, n)], dst_ref=land.at[pl.ds(0, n)],
            send_sem=rs_s, recv_sem=rs_r, device_id=(2 * p + 1 - k, c), device_id_type=MESH)

    @pl.loop(1, COLS)
    def _(n):
        rs_copy(COLS - n).start()

    @pl.when(k == 1)
    def _():
        rs_copy(0).start()

    sib_copy().wait_recv()

    @pl.when(c > 0)
    def _():
        right_copy(0).wait_recv()

    @pl.when(c < COLS - 1)
    def _():
        left_copy(0).wait_recv()

    zero8 = jnp.zeros((8, 128), F32)
    own, sib = pb_own[...], pb_sib[...]
    even = k == 0
    pb_buf[0:8] = jnp.where(c > 0, pb_left[...], zero8)
    pb_buf[8:72] = jnp.where(even, own, sib)
    pb_buf[72:136] = jnp.where(even, sib, own)
    pb_buf[136:144] = jnp.where(c < COLS - 1, pb_right[...], zero8)
    pb_buf[144:152] = zero8
    column_part(pb_buf, taps, pb_mid, b_part)

    def pa_copy(row, col, slot, sem):
        return pltpu.make_async_remote_copy(
            src_ref=pa_own, dst_ref=pa_land.at[slot],
            send_sem=pa_s.at[sem], recv_sem=pa_r.at[slot],
            device_id=(row, col), device_id_type=MESH)

    def pa_whole(n, sem):
        part = pb_buf.at[pl.ds(0, 8 * n)]
        return pltpu.make_async_remote_copy(
            src_ref=part, dst_ref=part, send_sem=pa_s.at[sem], recv_sem=pa_r.at[0],
            device_id=(2 * p + 1 - k, c), device_id_type=MESH)

    targets = (
        (2 * p, c + 1, c <= 4),
        (2 * p + 1, c - 3, c >= 3),
        (2 * p - 1, 5, (c == 0) & (p > 0)),
        (2 * p + 2, 0, (c == COLS - 1) & (p < ROWS // 2 - 1)),
    )
    w_o.wait()
    w_pa.wait()

    @pl.when(k == 0)
    def _():
        land[pl.ds(c, 1)] = msg[pl.ds(c, 1)]

        rs_whole(2 * COLS - 1).wait_recv()
        got = [land[g].astype(F32) for g in range(2 * COLS)]
        stat = jnp.concatenate([x[80:88] for x in got], axis=0).astype(BF16)
        a, b = iota((128, 128), 0), iota((128, 128), 1)
        same = (a & (H - 1)) == (b & (H - 1))
        pick_top = jnp.where(same & (a < 48), 1.0, 0.0).astype(BF16)
        pick_total = jnp.where(same & (a >= 48) & (a < 80), 1.0, 0.0).astype(BF16)
        top = dot(stat, pick_top)
        total = dot(stat, pick_total)
        tops = [top[8 * g:8 * g + 8] for g in range(2 * COLS)]
        summit = functools.reduce(jnp.maximum, tops)
        scales = [jnp.exp(x - summit) for x in tops]
        whole = sum(s * total[8 * g:8 * g + 8] for g, s in enumerate(scales))
        factor = jnp.concatenate([s / whole for s in scales], axis=0)
        high = factor.astype(BF16).astype(F32)
        factor = jnp.where(b < H, high, jnp.where(b < 2 * H, factor - high, 0.0)).astype(BF16)
        factors = dot(factor, spread[...])
        attended = []
        for t in range(10):
            attended.append(sum(
                got[g][8 * t:8 * t + 8] * factors[8 * g:8 * g + 8, 128 * t:128 * t + 128]
                for g in range(2 * COLS)))
        attended = jnp.concatenate(attended, axis=1).astype(BF16)
        hidden = fa_rows[pl.ds(pl.multiple_of(8 * c, 8), 8), :] + dot(attended, wo[...])
        centre = hidden - jnp.mean(hidden, axis=1, keepdims=True)
        spread_h = jnp.mean(centre * centre, axis=1, keepdims=True)
        normed = (centre * lax.rsqrt(spread_h + 1e-5)).astype(BF16)
        pa_own[...] = dot(normed, jnp.concatenate([wpa[...], wpa[...]], axis=0), NT)
        for n, (row, slot, on) in enumerate(targets):
            @pl.when(on)
            def _():
                @pl.loop(0, COLS)
                def _(m):
                    col = col_peer(COLS - 1 - m)
                    local = (row == r) & (col == c)

                    @pl.when(local)
                    def _():
                        pa_land[pl.ds(slot, 1)] = pa_own[...][None]

                    @pl.when(jnp.logical_not(local))
                    def _():
                        pa_copy(row, col, slot, n).start()

    fb_some(ROWS - 1, 0).wait_send()
    fa_whole().wait_send()
    fa_sibling().wait_send()
    sib_copy().wait_send()

    @pl.when(sends_right)
    def _():
        right_copy(0).wait_send()
        right_copy(1).wait_send()

    @pl.when(sends_left)
    def _():
        left_copy(0).wait_send()
        left_copy(1).wait_send()

    @pl.when(k == 0)
    def _():
        rs_whole(COLS - 1).wait_send()

    @pl.when(k == 1)
    def _():
        rs_whole(COLS).wait_send()

    mean = mean_matrix(256)
    qq = iota((QW, 128), 0)
    in_map = ((qq > 0) | (c > 0)) & ((qq < HALF + 1) | (c < COLS - 1))
    first = functools.partial(
        first_blocks, r=r, in_map=in_map, mean=mean, pa_buf=pa_buf, pb_mid=pb_mid, b_part=b_part,
        a_mid=a_mid, a_edge=a_edge, point_w=point_w, f1=f1)
    second = functools.partial(correlate, conv_w=conv_w, f1=f1)
    last_part = functools.partial(read_out, mean=mean, head_w=head_w, logits=logits)
    mine_slot = jnp.where((k == 0) & (c <= 4), c + 1, -1)
    pa_buf[...] = jnp.zeros_like(pa_buf)
    for s in range(1, 5):
        @pl.when(s != mine_slot)
        def _():
            pa_copy(r, c, s, 0).wait_recv()

        pa_buf[8 * s:8 * s + 8] = pa_land[s]
    row_parts(pa_buf, row_w, edge_w, a_mid, a_edge, range(4, 32), r)
    for _ in first(list(range(4, 32, 2))):
        pass
    part1 = second(1)
    part2 = second(2)
    last_part(1, *part1)
    last_part(2, *part2)

    @pl.when(r > 0)
    def _():
        pa_copy(r, c, 0, 0).wait_recv()
        pa_buf[0:8] = pa_land[0]

    @pl.when((r < ROWS - 1) & (mine_slot != 5))
    def _():
        pa_copy(r, c, 5, 0).wait_recv()

    @pl.when(r < ROWS - 1)
    def _():
        pa_buf[40:48] = pa_land[5]

    row_parts(pa_buf, row_w, edge_w, a_mid, a_edge, (0, 1, 2, 3, 32, 33, 34, 35), r)
    for _ in first([0, 2, 32, 34]):
        pass
    part0 = second(0)
    part3 = second(3)
    last_part(0, *part0)
    last_part(3, *part3)
    out_ref[...] = side_by_side(logits)

    @pl.when(k == 0)
    def _():
        for n, (row, slot, on) in enumerate(targets):
            @pl.when(on & (row == r))
            def _():
                pa_whole(COLS - 1, n).wait_send()

            @pl.when(on & (row != r))
            def _():
                pa_whole(COLS, n).wait_send()


def gelu_twice(x):
    inner = x * (0.7978845608028654 + 0.035677408136300125 * (x * x))
    return x + x * jnp.tanh(inner)


def row_parts(pa_buf, row_w, edge_w, a_mid, a_edge, rows, r):
    place = iota((48, 128), 0) + (TILE_A * r - 8)
    pa = jnp.where((place >= 0) & (place < LA), pa_buf[...], 0.0)
    middle = sum(row_w[u:u + 1] * pa[4 + u:44 + u] for u in range(5))
    weights = [[edge_w[n, u] for u in range(5)] for n in range(2)]
    edges = [sum(weights[n][u] * pa[4 + u + i:5 + u + i] for u in range(5))
             for n in range(2) for i in rows]
    value = jnp.concatenate([middle] + edges, axis=0)
    value = value - near_dot(value, mean_matrix(128))
    for m, i in enumerate(rows):
        a_mid[i:i + 1] = value[i:i + 1]
        a_edge[0, 8 * i:8 * i + 8] = value[40 + 8 * m:48 + 8 * m]
        at = 40 + 8 * (len(rows) + m)
        a_edge[1, 8 * i:8 * i + 8] = value[at:at + 8]


def first_blocks(rows, r, in_map, mean, pa_buf, pb_mid, b_part, a_mid, a_edge, point_w, f1):
    top, bottom = r == 0, r == ROWS - 1
    kinds = {2: jnp.where(top, 0, 2), 3: jnp.where(top, 1, 2),
             32: jnp.where(bottom, 3, 2), 33: jnp.where(bottom, 4, 2)}

    def part_of(w):
        part = b_part[kinds.get(w, 2)]
        return jnp.concatenate([
            part[:8] + a_edge[0, 8 * w:8 * w + 8],
            part[8:128] + a_mid[w:w + 1],
            part[128:] + a_edge[1, 8 * w:8 * w + 8]], axis=0)

    def start(u):
        x = jnp.concatenate([part_of(u), part_of(u + 1)], axis=1)
        return x, dot((x * x).astype(BF16), mean)

    def middle(x, var):
        return dot(gelu_twice(x * lax.rsqrt(var + 1e-5)).astype(BF16), point_w[...])

    def end(u, update):
        for n in range(2):
            keep = in_map
            if u < 2:
                keep = keep & jnp.logical_not(top)
            if u >= 34:
                keep = keep & jnp.logical_not(bottom)
            field = pb_mid[...] + pa_buf[u + n + 6:u + n + 7] + update[:, 128 * n:128 * n + 128]
            f1[u + n] = jnp.where(keep, field, 0.0)

    started, updates = {}, {}
    count = len(rows)
    for n in range(count + 2):
        if n < count:
            started[n] = start(rows[n])
        if 1 <= n <= count:
            updates[n - 1] = middle(*started.pop(n - 1))
        if n >= 2:
            end(rows[n - 2], updates.pop(n - 2))
            yield rows[n - 2]


def correlate(step, conv_w, f1):
    pieces = {}
    for u in range(8 * step, 8 * step + 12):
        for q in range(3):
            pieces[u, q] = f1[u, q:q + HALF, :].astype(BF16)

    def tall(u, q):
        return jnp.concatenate([pieces[8 * step + 2 * n + u, q] for n in range(4)], axis=0)

    around = jnp.concatenate([tall(u, q) for u in range(6) for q in range(3)], axis=1)
    return dot(around, conv_w[...]), [tall(2, 1), tall(3, 1)]


def read_out(step, x, field, mean, head_w, logits):
    var = dot((x * x).astype(BF16), mean)
    g = gelu_twice(x * lax.rsqrt(var + 1e-5)).astype(BF16)
    found = dot(head_w[...], jnp.concatenate(field + [g], axis=1), NT)
    found = found[0:4] + found[4:8]
    for n in range(4):
        for o in range(2):
            for s in range(2):
                at = TILE_A * s + 8 * step + 2 * n + o
                logits[at:at + 1] = found[2 * o + s:2 * o + s + 1, HALF * n:HALF * n + HALF]


def side_by_side(logits):
    total = None
    for s in range(2):
        place = iota((HALF, TILE_B), 1) == 2 * iota((HALF, TILE_B), 0) + s
        place = jnp.where(place, 1.0, 0.0).astype(BF16)
        piece = near_dot(logits[TILE_A * s:TILE_A * s + TILE_A], place)
        total = piece if total is None else total + piece
    return total


def local(
    emb_a, emb_b, w_query, w_key, w_value, w_out, w_pair_a, w_pair_b, w_depth, w_point, w_logit
):
    hbm = pl.BlockSpec(memory_space=pltpu.HBM)
    vmem = pl.BlockSpec(memory_space=pltpu.VMEM)
    weight = pltpu.VMEM((E, E), BF16)
    dma = pltpu.SemaphoreType.DMA
    return pl.pallas_call(
        attention,
        out_shape=pltpu.VMEM((TILE_A, TILE_B), F32),
        in_specs=[hbm] * 11,
        out_specs=vmem,
        scratch_shapes=[
            pltpu.VMEM((48, 128), F32),
            pltpu.VMEM((QW, 128), F32),
            pltpu.VMEM((5, QW, 128), F32),
            pltpu.VMEM((8, 128), F32),
            pltpu.VMEM((2, 5, 8, 128), F32),
            pltpu.VMEM((18 * 128, 256), BF16),
            pltpu.VMEM((256, 256), BF16),
            pltpu.VMEM((8, 512), BF16),
            pltpu.VMEM((40, 128), F32),
            pltpu.VMEM((2, 288, 128), F32),
            pltpu.VMEM((36, QW, 128), F32),
            pltpu.VMEM((2 * TILE_A, 128), F32),
            pltpu.VMEM((TILE_A, E // COLS), BF16),
            weight, weight, weight, weight,
            pltpu.VMEM((C, E), BF16),
            pltpu.VMEM((C, E), BF16),
            pltpu.VMEM((25, 2, C), F32),
            pltpu.VMEM((2, C, C), BF16),
            pltpu.VMEM((1, C), F32),
            pltpu.VMEM((2, D, HALF), BF16),
            pltpu.VMEM((ROWS, D, HALF), BF16),
            pltpu.VMEM((2, COLS, TILE_A, E // COLS), BF16),
            pltpu.VMEM((2 * TILE_A, E), F32),
            pltpu.VMEM((HALF, E), F32),
            pltpu.VMEM((HALF, E), F32),
            pltpu.VMEM((128, E), BF16),
            pltpu.VMEM((COLS, 96, 128), BF16),
            pltpu.VMEM((2 * COLS, 96, 128), BF16),
            pltpu.VMEM((HALF // 2, 128), F32),
            pltpu.VMEM((HALF // 2, 128), F32),
            pltpu.VMEM((8, 128), F32),
            pltpu.VMEM((8, 128), F32),
            pltpu.VMEM((152, 128), F32),
            pltpu.VMEM((8, 128), F32),
            pltpu.VMEM((6, 8, 128), F32),
            pltpu.VMEM((2, 32, 128), F32),
            dma((12,)),
            dma, dma((2,)),
            dma((2,)), dma((2,)),
            dma, dma,
            dma((3,)), dma((3,)),
            dma((4,)), dma((6,)),
        ],
        compiler_params=pltpu.CompilerParams(
            collective_id=0, has_side_effects=True, vmem_limit_bytes=48 * 2 ** 20),
        name="contact_map",
    )(*(pltpu.with_memory_space_constraint(a, pltpu.HBM) for a in (
        emb_a, emb_b.T, w_query, w_key, w_value, w_out, w_pair_a.T, w_pair_b.T,
        jnp.transpose(w_depth, (2, 0, 1)), w_point, w_logit.reshape(1, C))))


def solution(mesh):
    in_specs = (P("row", "col"), P("col", "row"), P(), P(), P(), P(), P(), P(), P(), P(), P())
    out_specs = P("row", "col")
    return jax.shard_map(local, mesh=mesh, in_specs=in_specs, out_specs=out_specs, check_vma=False)
```

```python
import functools
import math

import jax
import jax.numpy as jnp
from jax import lax
from jax.experimental import pallas as pl
from jax.experimental.pallas import tpu as pltpu
from jax.sharding import PartitionSpec as P

E = 1280
H = 16
D = E // H
C = 64
ROWS = 16
COLS = 8
LA = 512
LB = 2048
TILE_A = LA // ROWS
TILE_B = LB // COLS
HALF = TILE_B // 2
F32 = jnp.float32
BF16 = jnp.bfloat16
MESH = pl.DeviceIdType.MESH
NN = (((1,), (0,)), ((), ()))
NT = (((1,), (1,)), ((), ()))


def dot(a, b, dims=NN):
    return lax.dot_general(a, b, dims, preferred_element_type=F32)


def iota(shape, axis):
    return lax.broadcasted_iota(jnp.int32, shape, axis)


def eye(n):
    return jnp.where(iota((n, n), 0) == iota((n, n), 1), 1.0, 0.0).astype(BF16)


def doubled(n):
    lane = iota((n, 2 * n), 1)
    lane = jnp.where(lane >= n, lane - n, lane)
    return jnp.where(iota((n, 2 * n), 0) == lane, 1.0, 0.0).astype(BF16)


def split3(x):
    high = x.astype(BF16)
    rest = x - high.astype(F32)
    mid = rest.astype(BF16)
    low = (rest - mid.astype(F32)).astype(BF16)
    return high, mid, low


def exact_dot(x, ones, dims=NN):
    return sum(dot(part, ones, dims) for part in split3(x))


def near_dot(x, ones):
    high, mid, _ = split3(x)
    return dot(high, ones) + dot(mid, ones)


QW = 136


def prepare_weights(wd, wp, wl, taps, row_w, edge_w, conv_w, point_w, head_w, c):
    double = doubled(C)
    for s in range(2):
        taps[s, 0:25] = exact_dot(wd[:, s, :], double)

    def tap(u, v):
        return taps[0, 5 * u + v:5 * u + v + 1, :]

    for u in range(5):
        row_w[u:u + 1] = sum(tap(u, v) for v in range(5))
    for n, start in enumerate((1, HALF)):
        column = 2 * start + jnp.where(iota((1, 128), 1) < C, 0, 1) + TILE_B * c - 2
        for u in range(5):
            total = None
            for v in range(5):
                at = column + (v - 2)
                piece = jnp.where((at >= 0) & (at < LB), tap(u, v), 0.0)
                total = piece if total is None else total + piece
            edge_w[n, u:u + 1] = total

    a, b = iota((128, 128), 0), iota((128, 128), 1)
    upper, left = a < C, b < C
    same = upper == left
    rest = jnp.where((a & (C - 1)) == (b & (C - 1)), 1.0 - 1.0 / C, -1.0 / C)
    columns = sum(dot(jnp.concatenate([eye(C), eye(C)], axis=0), part, NT)
                  for part in split3(wd[:, 1, :]))

    def spread(u, v):
        if not 0 <= v < 5:
            return 0.0
        return columns[:, 5 * u + v:5 * u + v + 1]

    zero = jnp.zeros((128, 128), BF16)
    for q in range(3):
        blocks = []
        for u in range(5):
            block = jnp.where(same, spread(u, 2 * q),
                              jnp.where(upper, spread(u, 2 * q - 1), spread(u, 2 * q + 1)))
            blocks.append((block * rest).astype(BF16))
        for u in range(6):
            at = 128 * (3 * u + q)
            conv_w[at:at + 128, 0:128] = blocks[u] if u < 5 else zero
            conv_w[at:at + 128, 128:256] = blocks[u - 1] if u > 0 else zero

    point = dot(wp[0], double)
    point = jnp.concatenate([point, point], axis=1)
    point = jnp.concatenate([point] * 4, axis=0)
    fits = (iota((256, 256), 0) // C) == (iota((256, 256), 1) // C)
    point_w[...] = jnp.where(fits, 0.5 * point, 0.0).astype(BF16)

    read = jnp.broadcast_to(wl[...], (8, C))
    folded = 0.5 * sum(dot(part, wp[1], NT) for part in split3(read))
    row8, lane8 = iota((8, 256), 0), iota((8, 256), 1)
    fits8 = (row8 & 3) == (lane8 // C)
    for n, values in enumerate((read, folded)):
        both = exact_dot(values, double)
        both = jnp.concatenate([both, both], axis=1)
        high = both.astype(BF16).astype(F32)
        picked = jnp.where(row8 < 4, high, both - high)
        head_w[:, 256 * n:256 * n + 256] = jnp.where(fits8, picked, 0.0).astype(BF16)


def mean_matrix(n):
    fits = (iota((n, n), 0) // C) == (iota((n, n), 1) // C)
    return jnp.where(fits, 1.0 / C, 0.0).astype(BF16)


def column_part(pb_buf, taps, pb_mid, b_part):
    mean = mean_matrix(128)
    left = iota((1, 128), 1) < C
    plain = [pb_buf[6 + q:6 + q + QW] for q in range(3)]
    pb_mid[...] = plain[1]
    crossed = [pltpu.roll(x, C, 1) for x in plain]

    for n, (low, high) in enumerate(((2, 5), (1, 5), (0, 5), (0, 4), (0, 3))):
        w = [sum(taps[0, 5 * u + v:5 * u + v + 1, :] for u in range(low, high)) for v in range(5)]
        value = (w[0] * plain[0] + w[2] * plain[1] + w[4] * plain[2]
                 + jnp.where(left, w[1], 0.0) * crossed[0]
                 + jnp.where(left, w[3], w[1]) * crossed[1]
                 + jnp.where(left, 0.0, w[3]) * crossed[2])
        b_part[n] = value - near_dot(value, mean)


def attention(
    ea_h, eb_h, wq_h, wk_h, wv_h, wo_h, wpa_h, wpb_h, wd_h, wp_h, wl_h,
    out_ref,
    pa_buf, pb_mid, b_part, row_w, edge_w, conv_w, point_w, head_w, a_mid, a_edge, f1, logits,
    ea, wq, wk, wv, wo, wpa, wpb, wd, wp, wl,
    fb_src, fb_all, fa_all, fa_rows, keys, values, spread, msg, land,
    pb_own, pb_sib, pb_left, pb_right, pb_buf, pa_own, pa_land, taps,
    in_sem, fb_s, fb_r, fa_s, fa_r, rs_s, rs_r, pb_s, pb_r, pa_s, pa_r,
):
    r = lax.axis_index("row")
    c = lax.axis_index("col")
    k = lax.rem(r, 2)
    p = lax.div(r, 2)
    mine = k * COLS + c

    loads = [
        pltpu.make_async_copy(src, dst, in_sem.at[i])
        for i, (src, dst) in enumerate(
            [(eb_h.at[:, pl.ds(0, HALF)], fb_src.at[0]), (eb_h.at[:, pl.ds(HALF, HALF)], fb_src.at[1]),
             (ea_h, ea), (wq_h, wq), (wk_h, wk), (wv_h, wv),
             (wpb_h, wpb), (wo_h, wo), (wpa_h, wpa), (wd_h, wd), (wp_h, wp), (wl_h, wl)]
        )
    ]
    for load in loads:
        load.start()
    w_eb0, w_eb1, w_ea, w_q, w_k, w_v, w_pb, w_o, w_pa, w_d, w_p, w_l = loads

    x, y = lax.div(r, 8), lax.rem(p, 4)
    z, xl = lax.div(c, 2), lax.rem(c, 2)

    def row_peer(e):
        return (lax.rem(x + lax.div(e, 8), 2) * 8 + lax.rem(y + lax.rem(lax.div(e, 2), 4), 4) * 2
                + lax.rem(k + lax.rem(e, 2), 2))

    def col_peer(e):
        return lax.rem(z + lax.rem(lax.div(e, 2), 4), 4) * 2 + lax.rem(xl + lax.rem(e, 2), 2)

    barrier = pltpu.get_barrier_semaphore()

    def greet(row, col):
        pl.semaphore_signal(barrier, inc=1, device_id=(row, col), device_id_type=MESH)

    @pl.loop(1, ROWS)
    def _(n):
        e = ROWS - n
        greet(row_peer(e), c)
        greet(2 * p + lax.rem(k + lax.div(e, 8), 2), col_peer(e))

    @pl.when((k == 1) & (r < ROWS - 1))
    def _():
        greet(r + 1, 0)

    @pl.when((k == 0) & (r > 0))
    def _():
        greet(r - 2, COLS - 1)

    w_eb0.wait()
    w_eb1.wait()
    fb_all[pl.ds(r, 1)] = fb_src[pl.ds(k, 1)]
    w_ea.wait()
    fa_all[pl.ds(k, 1), pl.ds(c, 1)] = ea[...][None, None]

    first = (k == 0) & (c == 0) & (p > 0)
    last = (k == 0) & (c == COLS - 1) & (p < ROWS // 2 - 1)
    extra = jnp.where(first, COLS, 0) + jnp.where(last, COLS, 0)
    pl.semaphore_wait(barrier, 2 * (ROWS - 1) + extra)

    def fb_copy(e):
        to = row_peer(e)
        return pltpu.make_async_remote_copy(
            src_ref=fb_src.at[lax.rem(to, 2)], dst_ref=fb_all.at[r],
            send_sem=fb_s, recv_sem=fb_r.at[lax.div(e, 8)],
            device_id=(to, c), device_id_type=MESH)

    def fb_some(n, far):
        part = fb_all.at[pl.ds(0, n)]
        return pltpu.make_async_remote_copy(
            src_ref=part, dst_ref=part, send_sem=fb_s, recv_sem=fb_r.at[far],
            device_id=(2 * p + 1 - k, c), device_id_type=MESH)

    def fa_whole():
        part = fa_all.at[0, pl.ds(0, COLS - 1)]
        return pltpu.make_async_remote_copy(
            src_ref=part, dst_ref=part, send_sem=fa_s.at[1], recv_sem=fa_r.at[1],
            device_id=(2 * p + 1 - k, c), device_id_type=MESH)

    def fa_copy(e):
        return pltpu.make_async_remote_copy(
            src_ref=ea, dst_ref=fa_all.at[k, c],
            send_sem=fa_s.at[1], recv_sem=fa_r.at[1],
            device_id=(r, col_peer(e)), device_id_type=MESH)

    def fa_sibling():
        return pltpu.make_async_remote_copy(
            src_ref=fa_all.at[k], dst_ref=fa_all.at[k],
            send_sem=fa_s.at[0], recv_sem=fa_r.at[0],
            device_id=(2 * p + 1 - k, c), device_id_type=MESH)

    @pl.loop(1, COLS)
    def _(n):
        fa_copy(COLS - n).start()

    @pl.loop(1, ROWS)
    def _(n):
        fb_copy(ROWS - n).start()

    w_d.wait()
    w_p.wait()
    w_l.wait()
    prepare_weights(wd, wp, wl, taps, row_w, edge_w, conv_w, point_w, head_w, c)
    l, f = iota((128, E), 0), iota((128, E), 1)
    start = (l & (H - 1)) * D
    spread[...] = jnp.where((l < 2 * H) & (f >= start) & (f < start + D), 1.0, 0.0).astype(BF16)

    fa_whole().wait_recv()
    fa_sibling().start()

    n0, n1 = iota((HALF, HALF), 0), iota((HALF, HALF), 1)
    order = jnp.where(n0 < HALF // 2, 2 * n0, 2 * n0 - (HALF - 1))
    order = jnp.where(n1 == order, 1.0, 0.0).astype(BF16)

    def features(side):
        blocks = fb_all[pl.ds(8 * side, 8)].reshape(E // 2, HALF)
        return dot(order, blocks, NT).astype(BF16)

    def some_rows(side):
        return pl.ds(pl.multiple_of(side * (E // 2), 128), E // 2)

    def pair_weights(side):
        part = wpb[:, some_rows(side)]
        return jnp.concatenate([part, part], axis=0)

    fb_some(7, 0).wait_recv()
    w_k.wait()
    w_v.wait()
    w_pb.wait()
    near = features(x)
    for t in range(5):
        at = slice(256 * t, 256 * t + 256)
        keys[:, at] = dot(near, wk[some_rows(x), at])
        values[:, at] = dot(near, wv[some_rows(x), at])
    near_b = dot(near, pair_weights(x), NT)

    fa_sibling().wait_recv()
    fa = jnp.concatenate(
        [jnp.concatenate([fa_all[kk, cc].astype(F32) for cc in range(COLS)], axis=1)
         for kk in range(2)], axis=0)
    fa_rows[...] = fa
    w_q.wait()
    query = dot(fa.astype(BF16), wq[...]).astype(BF16).astype(F32)

    fb_some(8, 1).wait_recv()
    far = features(1 - x)
    found_b = near_b + dot(far, pair_weights(1 - x), NT)
    pb_own[...] = jnp.where(iota((HALF // 2, 128), 1) < C, found_b[:HALF // 2], found_b[HALF // 2:])

    def sib_copy():
        return pltpu.make_async_remote_copy(
            src_ref=pb_own, dst_ref=pb_sib, send_sem=pb_s.at[0], recv_sem=pb_r.at[0],
            device_id=(2 * p + 1 - k, c), device_id_type=MESH)

    def right_copy(kk):
        return pltpu.make_async_remote_copy(
            src_ref=pb_own.at[pl.ds(HALF // 2 - 8, 8)], dst_ref=pb_left,
            send_sem=pb_s.at[1 + kk], recv_sem=pb_r.at[1],
            device_id=(2 * p + kk, lax.rem(c + 1, COLS)), device_id_type=MESH)

    def left_copy(kk):
        return pltpu.make_async_remote_copy(
            src_ref=pb_own.at[pl.ds(0, 8)], dst_ref=pb_right,
            send_sem=pb_s.at[1 + kk], recv_sem=pb_r.at[2],
            device_id=(2 * p + kk, lax.rem(c + COLS - 1, COLS)), device_id_type=MESH)

    sends_right = (k == 1) & (c < COLS - 1)
    sends_left = (k == 0) & (c > 0)
    sib_copy().start()

    @pl.when(sends_right)
    def _():
        right_copy(0).start()
        right_copy(1).start()

    @pl.when(sends_left)
    def _():
        left_copy(0).start()
        left_copy(1).start()

    rows = 2 * TILE_A
    lane256 = iota((rows, 256), 1)

    def heads_of(t):
        return range(3 * t, 3 * t + 4)

    def inside(h, t):
        return (lane256 >= D * h - 256 * t) & (lane256 < D * h + D - 256 * t)

    spans = [slice(256 * t, 256 * t + 256) for t in range(5)]
    masked = [jnp.concatenate([jnp.where(inside(h, t), query[:, spans[t]], 0.0)
                               for h in heads_of(t)], axis=0).astype(BF16) for t in range(5)]
    key_parts = [keys[:, at] + dot(far, wk[some_rows(1 - x), at]) for at in spans]
    founds = [dot(masked[t], key_parts[t].astype(BF16), NT) for t in range(5)]
    value_parts = [values[:, at] + dot(far, wv[some_rows(1 - x), at]) for at in spans]
    scores = [None] * H
    for t in range(5):
        for n, h in enumerate(heads_of(t)):
            piece = founds[t][rows * n:rows * n + rows]
            scores[h] = piece if scores[h] is None else scores[h] + piece

    lane = iota((rows, 128), 1)
    head_of = lane & (H - 1)
    tops = jnp.zeros((rows, 128), F32)
    totals = jnp.zeros((rows, 128), F32)
    weights = []
    for h in range(H):
        s = scores[h] * (1.0 / math.sqrt(D))
        top = jnp.max(s, axis=1, keepdims=True)
        w = jnp.exp(s - top)
        tops = jnp.where(head_of == h, top, tops)
        totals = jnp.where(head_of == h, jnp.sum(w, axis=1, keepdims=True), totals)
        weights.append(w.astype(BF16))
    founds = [dot(jnp.concatenate(weights[3 * t:3 * t + 4], axis=0), value_parts[t].astype(BF16))
              for t in range(5)]
    t1, t2, t3 = (x.astype(F32) for x in split3(tops))
    n1, n2, _ = (x.astype(F32) for x in split3(totals))
    stats = jnp.where(lane < 16, t1, jnp.where(lane < 32, t2, jnp.where(
        lane < 48, t3, jnp.where(lane < 64, n1, jnp.where(lane < 80, n2, 0.0)))))

    mixed = []
    for t in range(5):
        total = sum(jnp.where(inside(h, t), founds[t][rows * n:rows * n + rows], 0.0)
                    for n, h in enumerate(heads_of(t)))
        mixed += [total[:, :128], total[:, 128:]]
    for d in range(COLS):
        block = [m[8 * d:8 * d + 8] for m in mixed + [stats]] + [jnp.zeros((8, 128), F32)]
        msg[d] = jnp.concatenate(block, axis=0).astype(BF16)

    def rs_copy(d):
        to = col_peer(d)
        return pltpu.make_async_remote_copy(
            src_ref=msg.at[to], dst_ref=land.at[mine],
            send_sem=rs_s, recv_sem=rs_r,
            device_id=(2 * p, to), device_id_type=MESH)

    def rs_whole(n):
        return pltpu.make_async_remote_copy(
            src_ref=land.at[pl.ds(0, n)], dst_ref=land.at[pl.ds(0, n)],
            send_sem=rs_s, recv_sem=rs_r, device_id=(2 * p + 1 - k, c), device_id_type=MESH)

    @pl.loop(1, COLS)
    def _(n):
        rs_copy(COLS - n).start()

    @pl.when(k == 1)
    def _():
        rs_copy(0).start()

    sib_copy().wait_recv()

    @pl.when(c > 0)
    def _():
        right_copy(0).wait_recv()

    @pl.when(c < COLS - 1)
    def _():
        left_copy(0).wait_recv()

    zero8 = jnp.zeros((8, 128), F32)
    own, sib = pb_own[...], pb_sib[...]
    even = k == 0
    pb_buf[0:8] = jnp.where(c > 0, pb_left[...], zero8)
    pb_buf[8:72] = jnp.where(even, own, sib)
    pb_buf[72:136] = jnp.where(even, sib, own)
    pb_buf[136:144] = jnp.where(c < COLS - 1, pb_right[...], zero8)
    pb_buf[144:152] = zero8
    column_part(pb_buf, taps, pb_mid, b_part)

    def pa_copy(row, col, slot, sem):
        return pltpu.make_async_remote_copy(
            src_ref=pa_own, dst_ref=pa_land.at[slot],
            send_sem=pa_s.at[sem], recv_sem=pa_r.at[slot],
            device_id=(row, col), device_id_type=MESH)

    def pa_whole(n, sem):
        part = pb_buf.at[pl.ds(0, 8 * n)]
        return pltpu.make_async_remote_copy(
            src_ref=part, dst_ref=part, send_sem=pa_s.at[sem], recv_sem=pa_r.at[0],
            device_id=(2 * p + 1 - k, c), device_id_type=MESH)

    targets = (
        (2 * p, c + 1, c <= 4),
        (2 * p + 1, c - 3, c >= 3),
        (2 * p - 1, 5, (c == 0) & (p > 0)),
        (2 * p + 2, 0, (c == COLS - 1) & (p < ROWS // 2 - 1)),
    )
    w_o.wait()
    w_pa.wait()

    @pl.when(k == 0)
    def _():
        land[pl.ds(c, 1)] = msg[pl.ds(c, 1)]

        rs_whole(2 * COLS - 1).wait_recv()
        got = [land[g].astype(F32) for g in range(2 * COLS)]
        stat = jnp.concatenate([x[80:88] for x in got], axis=0).astype(BF16)
        a, b = iota((128, 128), 0), iota((128, 128), 1)
        same = (a & (H - 1)) == (b & (H - 1))
        pick_top = jnp.where(same & (a < 48), 1.0, 0.0).astype(BF16)
        pick_total = jnp.where(same & (a >= 48) & (a < 80), 1.0, 0.0).astype(BF16)
        top = dot(stat, pick_top)
        total = dot(stat, pick_total)
        tops = [top[8 * g:8 * g + 8] for g in range(2 * COLS)]
        summit = functools.reduce(jnp.maximum, tops)
        scales = [jnp.exp(x - summit) for x in tops]
        whole = sum(s * total[8 * g:8 * g + 8] for g, s in enumerate(scales))
        factor = jnp.concatenate([s / whole for s in scales], axis=0)
        high = factor.astype(BF16).astype(F32)
        factor = jnp.where(b < H, high, jnp.where(b < 2 * H, factor - high, 0.0)).astype(BF16)
        factors = dot(factor, spread[...])
        attended = []
        for t in range(10):
            attended.append(sum(
                got[g][8 * t:8 * t + 8] * factors[8 * g:8 * g + 8, 128 * t:128 * t + 128]
                for g in range(2 * COLS)))
        attended = jnp.concatenate(attended, axis=1).astype(BF16)
        hidden = fa_rows[pl.ds(pl.multiple_of(8 * c, 8), 8), :] + dot(attended, wo[...])
        centre = hidden - jnp.mean(hidden, axis=1, keepdims=True)
        spread_h = jnp.mean(centre * centre, axis=1, keepdims=True)
        normed = (centre * lax.rsqrt(spread_h + 1e-5)).astype(BF16)
        pa_own[...] = dot(normed, jnp.concatenate([wpa[...], wpa[...]], axis=0), NT)
        for n, (row, slot, on) in enumerate(targets):
            @pl.when(on)
            def _():
                @pl.loop(0, COLS)
                def _(m):
                    col = col_peer(COLS - 1 - m)
                    local = (row == r) & (col == c)

                    @pl.when(local)
                    def _():
                        pa_land[pl.ds(slot, 1)] = pa_own[...][None]

                    @pl.when(jnp.logical_not(local))
                    def _():
                        pa_copy(row, col, slot, n).start()

    fb_some(ROWS - 1, 0).wait_send()
    fa_whole().wait_send()
    fa_sibling().wait_send()
    sib_copy().wait_send()

    @pl.when(sends_right)
    def _():
        right_copy(0).wait_send()
        right_copy(1).wait_send()

    @pl.when(sends_left)
    def _():
        left_copy(0).wait_send()
        left_copy(1).wait_send()

    @pl.when(k == 0)
    def _():
        rs_whole(COLS - 1).wait_send()

    @pl.when(k == 1)
    def _():
        rs_whole(COLS).wait_send()

    mean = mean_matrix(256)
    qq = iota((QW, 128), 0)
    in_map = ((qq > 0) | (c > 0)) & ((qq < HALF + 1) | (c < COLS - 1))
    first = functools.partial(
        first_blocks, r=r, in_map=in_map, mean=mean, pa_buf=pa_buf, pb_mid=pb_mid, b_part=b_part,
        a_mid=a_mid, a_edge=a_edge, point_w=point_w, f1=f1)
    second = functools.partial(correlate, conv_w=conv_w, f1=f1)
    last_part = functools.partial(read_out, mean=mean, head_w=head_w, logits=logits)
    mine_slot = jnp.where((k == 0) & (c <= 4), c + 1, -1)
    pa_buf[...] = jnp.zeros_like(pa_buf)
    for s in range(1, 5):
        @pl.when(s != mine_slot)
        def _():
            pa_copy(r, c, s, 0).wait_recv()

        pa_buf[8 * s:8 * s + 8] = pa_land[s]
    row_parts(pa_buf, row_w, edge_w, a_mid, a_edge, ((4, 32),), r)
    for _ in first(list(range(4, 32, 2))):
        pass
    part1 = second(1)
    part2 = second(2)
    last_part(1, *part1)
    last_part(2, *part2)

    @pl.when(r > 0)
    def _():
        pa_copy(r, c, 0, 0).wait_recv()
        pa_buf[0:8] = pa_land[0]

    @pl.when((r < ROWS - 1) & (mine_slot != 5))
    def _():
        pa_copy(r, c, 5, 0).wait_recv()

    @pl.when(r < ROWS - 1)
    def _():
        pa_buf[40:48] = pa_land[5]

    row_parts(pa_buf, row_w, edge_w, a_mid, a_edge, ((0, 4), (32, 36)), r)
    for _ in first([0, 2, 32, 34]):
        pass
    part0 = second(0)
    part3 = second(3)
    last_part(0, *part0)
    last_part(3, *part3)
    out_ref[...] = side_by_side(logits)

    @pl.when(k == 0)
    def _():
        for n, (row, slot, on) in enumerate(targets):
            @pl.when(on & (row == r))
            def _():
                pa_whole(COLS - 1, n).wait_send()

            @pl.when(on & (row != r))
            def _():
                pa_whole(COLS, n).wait_send()


def gelu_twice(x):
    x = x.astype(BF16)
    inner = x * (BF16(0.7978845608028654) + BF16(0.035677408136300125) * (x * x))
    return x + x * jnp.tanh(inner)


def squared(x):
    x = x.astype(BF16)
    return x * x


def row_parts(pa_buf, row_w, edge_w, a_mid, a_edge, spans, r):
    place = iota((48, 128), 0) + (TILE_A * r - 8)
    pa = jnp.where((place >= 0) & (place < LA), pa_buf[...], 0.0)
    kinds = [[row_w[u:u + 1] for u in range(5)]]
    kinds += [[edge_w[n, u:u + 1] for u in range(5)] for n in range(2)]
    value = jnp.concatenate(
        [sum(w[u] * pa[4 + u:44 + u] for u in range(5)) for w in kinds], axis=0)
    value = value - near_dot(value, mean_matrix(128))
    for low, high in spans:
        a_mid[low:high] = value[low:high]
        a_edge[0, low:high] = value[40 + low:40 + high]
        a_edge[1, low:high] = value[80 + low:80 + high]


def first_blocks(rows, r, in_map, mean, pa_buf, pb_mid, b_part, a_mid, a_edge, point_w, f1):
    top, bottom = r == 0, r == ROWS - 1
    kinds = {2: jnp.where(top, 0, 2), 3: jnp.where(top, 1, 2),
             32: jnp.where(bottom, 3, 2), 33: jnp.where(bottom, 4, 2)}

    sub = iota((8, 128), 0)

    def part_of(w):
        part = b_part[kinds.get(w, 2)]
        row = a_mid[w:w + 1]
        return jnp.concatenate([
            part[:8] + jnp.where(sub == 1, a_edge[0, w:w + 1], row),
            part[8:HALF] + row,
            part[HALF:] + jnp.where(sub == 0, a_edge[1, w:w + 1], row)], axis=0)

    def start(u):
        x = jnp.concatenate([part_of(u), part_of(u + 1)], axis=1)
        return x, dot(squared(x), mean)

    def middle(x, var):
        return dot(gelu_twice(x * lax.rsqrt(var + 1e-5)), point_w[...])

    def end(u, update):
        for n in range(2):
            keep = in_map
            if u < 2:
                keep = keep & jnp.logical_not(top)
            if u >= 34:
                keep = keep & jnp.logical_not(bottom)
            field = pb_mid[...] + pa_buf[u + n + 6:u + n + 7] + update[:, 128 * n:128 * n + 128]
            f1[u + n] = jnp.where(keep, field, 0.0)

    started, updates = {}, {}
    count = len(rows)
    for n in range(count + 2):
        if n < count:
            started[n] = start(rows[n])
        if 1 <= n <= count:
            updates[n - 1] = middle(*started.pop(n - 1))
        if n >= 2:
            end(rows[n - 2], updates.pop(n - 2))
            yield rows[n - 2]


def correlate(step, conv_w, f1):
    pieces = {}
    for u in range(8 * step, 8 * step + 12):
        for q in range(3):
            pieces[u, q] = f1[u, q:q + HALF, :].astype(BF16)

    def tall(u, q):
        return jnp.concatenate([pieces[8 * step + 2 * n + u, q] for n in range(4)], axis=0)

    around = jnp.concatenate([tall(u, q) for u in range(6) for q in range(3)], axis=1)
    return dot(around, conv_w[...]), [tall(2, 1), tall(3, 1)]


def read_out(step, x, field, mean, head_w, logits):
    var = dot(squared(x), mean)
    g = gelu_twice(x * lax.rsqrt(var + 1e-5))
    found = dot(head_w[...], jnp.concatenate(field + [g], axis=1), NT)
    found = found[0:4] + found[4:8]
    for n in range(4):
        for o in range(2):
            for s in range(2):
                at = TILE_A * s + 8 * step + 2 * n + o
                logits[at:at + 1] = found[2 * o + s:2 * o + s + 1, HALF * n:HALF * n + HALF]


def side_by_side(logits):
    total = None
    for s in range(2):
        place = iota((HALF, TILE_B), 1) == 2 * iota((HALF, TILE_B), 0) + s
        place = jnp.where(place, 1.0, 0.0).astype(BF16)
        piece = near_dot(logits[TILE_A * s:TILE_A * s + TILE_A], place)
        total = piece if total is None else total + piece
    return total


def local(
    emb_a, emb_b, w_query, w_key, w_value, w_out, w_pair_a, w_pair_b, w_depth, w_point, w_logit
):
    hbm = pl.BlockSpec(memory_space=pltpu.HBM)
    vmem = pl.BlockSpec(memory_space=pltpu.VMEM)
    weight = pltpu.VMEM((E, E), BF16)
    dma = pltpu.SemaphoreType.DMA
    return pl.pallas_call(
        attention,
        out_shape=pltpu.VMEM((TILE_A, TILE_B), F32),
        in_specs=[hbm] * 11,
        out_specs=vmem,
        scratch_shapes=[
            pltpu.VMEM((48, 128), F32),
            pltpu.VMEM((QW, 128), F32),
            pltpu.VMEM((5, QW, 128), F32),
            pltpu.VMEM((8, 128), F32),
            pltpu.VMEM((2, 8, 128), F32),
            pltpu.VMEM((18 * 128, 256), BF16),
            pltpu.VMEM((256, 256), BF16),
            pltpu.VMEM((8, 512), BF16),
            pltpu.VMEM((40, 128), F32),
            pltpu.VMEM((2, 40, 128), F32),
            pltpu.VMEM((36, QW, 128), F32),
            pltpu.VMEM((2 * TILE_A, 128), F32),
            pltpu.VMEM((TILE_A, E // COLS), BF16),
            weight, weight, weight, weight,
            pltpu.VMEM((C, E), BF16),
            pltpu.VMEM((C, E), BF16),
            pltpu.VMEM((25, 2, C), F32),
            pltpu.VMEM((2, C, C), BF16),
            pltpu.VMEM((1, C), F32),
            pltpu.VMEM((2, D, HALF), BF16),
            pltpu.VMEM((ROWS, D, HALF), BF16),
            pltpu.VMEM((2, COLS, TILE_A, E // COLS), BF16),
            pltpu.VMEM((2 * TILE_A, E), F32),
            pltpu.VMEM((HALF, E), F32),
            pltpu.VMEM((HALF, E), F32),
            pltpu.VMEM((128, E), BF16),
            pltpu.VMEM((COLS, 96, 128), BF16),
            pltpu.VMEM((2 * COLS, 96, 128), BF16),
            pltpu.VMEM((HALF // 2, 128), F32),
            pltpu.VMEM((HALF // 2, 128), F32),
            pltpu.VMEM((8, 128), F32),
            pltpu.VMEM((8, 128), F32),
            pltpu.VMEM((152, 128), F32),
            pltpu.VMEM((8, 128), F32),
            pltpu.VMEM((6, 8, 128), F32),
            pltpu.VMEM((2, 32, 128), F32),
            dma((12,)),
            dma, dma((2,)),
            dma((2,)), dma((2,)),
            dma, dma,
            dma((3,)), dma((3,)),
            dma((4,)), dma((6,)),
        ],
        compiler_params=pltpu.CompilerParams(
            collective_id=0, has_side_effects=True, vmem_limit_bytes=48 * 2 ** 20),
        name="contact_map",
    )(*(pltpu.with_memory_space_constraint(a, pltpu.HBM) for a in (
        emb_a, emb_b.T, w_query, w_key, w_value, w_out, w_pair_a.T, w_pair_b.T,
        jnp.transpose(w_depth, (2, 0, 1)), w_point, w_logit.reshape(1, C))))


def solution(mesh):
    in_specs = (P("row", "col"), P("col", "row"), P(), P(), P(), P(), P(), P(), P(), P(), P())
    out_specs = P("row", "col")
    return jax.shard_map(local, mesh=mesh, in_specs=in_specs, out_specs=out_specs, check_vma=False)
```

```python
import functools
import math

import jax
import jax.numpy as jnp
from jax import lax
from jax.experimental import pallas as pl
from jax.experimental.pallas import tpu as pltpu
from jax.sharding import PartitionSpec as P

E = 1280
H = 16
D = E // H
C = 64
ROWS = 16
COLS = 8
LA = 512
LB = 2048
TILE_A = LA // ROWS
TILE_B = LB // COLS
HALF = TILE_B // 2
F32 = jnp.float32
BF16 = jnp.bfloat16
MESH = pl.DeviceIdType.MESH
NN = (((1,), (0,)), ((), ()))
NT = (((1,), (1,)), ((), ()))


def dot(a, b, dims=NN):
    return lax.dot_general(a, b, dims, preferred_element_type=F32)


def iota(shape, axis):
    return lax.broadcasted_iota(jnp.int32, shape, axis)


def eye(n):
    return jnp.where(iota((n, n), 0) == iota((n, n), 1), 1.0, 0.0).astype(BF16)


def doubled(n):
    lane = iota((n, 2 * n), 1)
    lane = jnp.where(lane >= n, lane - n, lane)
    return jnp.where(iota((n, 2 * n), 0) == lane, 1.0, 0.0).astype(BF16)


def split3(x):
    high = x.astype(BF16)
    rest = x - high.astype(F32)
    mid = rest.astype(BF16)
    low = (rest - mid.astype(F32)).astype(BF16)
    return high, mid, low


def exact_dot(x, ones, dims=NN):
    return sum(dot(part, ones, dims) for part in split3(x))


def near_dot(x, ones):
    high, mid, _ = split3(x)
    return dot(high, ones) + dot(mid, ones)


QW = 136


def prepare_weights(wd, wp, wl, taps, row_w, edge_w, conv_w, point_w, head_w, c):
    double = doubled(C)
    for s in range(2):
        taps[s, 0:25] = exact_dot(wd[:, s, :], double)

    def tap(u, v):
        return taps[0, 5 * u + v:5 * u + v + 1, :]

    for u in range(5):
        row_w[u:u + 1] = sum(tap(u, v) for v in range(5))
    for n, start in enumerate((1, HALF)):
        column = 2 * start + jnp.where(iota((1, 128), 1) < C, 0, 1) + TILE_B * c - 2
        for u in range(5):
            total = None
            for v in range(5):
                at = column + (v - 2)
                piece = jnp.where((at >= 0) & (at < LB), tap(u, v), 0.0)
                total = piece if total is None else total + piece
            edge_w[n, u:u + 1] = total

    a, b = iota((128, 128), 0), iota((128, 128), 1)
    upper, left = a < C, b < C
    same = upper == left
    rest = jnp.where((a & (C - 1)) == (b & (C - 1)), 1.0 - 1.0 / C, -1.0 / C)
    columns = sum(dot(jnp.concatenate([eye(C), eye(C)], axis=0), part, NT)
                  for part in split3(wd[:, 1, :]))

    def spread(u, v):
        if not 0 <= v < 5:
            return 0.0
        return columns[:, 5 * u + v:5 * u + v + 1]

    zero = jnp.zeros((128, 128), BF16)
    for q in range(3):
        blocks = []
        for u in range(5):
            block = jnp.where(same, spread(u, 2 * q),
                              jnp.where(upper, spread(u, 2 * q - 1), spread(u, 2 * q + 1)))
            blocks.append((block * rest).astype(BF16))
        for u in range(6):
            at = 128 * (3 * u + q)
            conv_w[at:at + 128, 0:128] = blocks[u] if u < 5 else zero
            conv_w[at:at + 128, 128:256] = blocks[u - 1] if u > 0 else zero

    point = dot(wp[0], double)
    point = jnp.concatenate([point, point], axis=1)
    point = jnp.concatenate([point] * 4, axis=0)
    fits = (iota((256, 256), 0) // C) == (iota((256, 256), 1) // C)
    point_w[...] = jnp.where(fits, 0.5 * point, 0.0).astype(BF16)

    read = jnp.broadcast_to(wl[...], (8, C))
    folded = 0.5 * sum(dot(part, wp[1], NT) for part in split3(read))
    row8, lane8 = iota((8, 256), 0), iota((8, 256), 1)
    fits8 = (row8 & 3) == (lane8 // C)
    for n, values in enumerate((read, folded)):
        both = exact_dot(values, double)
        both = jnp.concatenate([both, both], axis=1)
        high = both.astype(BF16).astype(F32)
        picked = jnp.where(row8 < 4, high, both - high)
        head_w[:, 256 * n:256 * n + 256] = jnp.where(fits8, picked, 0.0).astype(BF16)


def mean_matrix(n):
    fits = (iota((n, n), 0) // C) == (iota((n, n), 1) // C)
    return jnp.where(fits, 1.0 / C, 0.0).astype(BF16)


def column_part(pb_buf, taps, pb_mid, b_part):
    mean = mean_matrix(128)
    left = iota((1, 128), 1) < C
    plain = [pb_buf[6 + q:6 + q + QW] for q in range(3)]
    pb_mid[...] = plain[1]
    crossed = [pltpu.roll(x, C, 1) for x in plain]

    for n, (low, high) in enumerate(((2, 5), (1, 5), (0, 5), (0, 4), (0, 3))):
        w = [sum(taps[0, 5 * u + v:5 * u + v + 1, :] for u in range(low, high)) for v in range(5)]
        value = (w[0] * plain[0] + w[2] * plain[1] + w[4] * plain[2]
                 + jnp.where(left, w[1], 0.0) * crossed[0]
                 + jnp.where(left, w[3], w[1]) * crossed[1]
                 + jnp.where(left, 0.0, w[3]) * crossed[2])
        b_part[n] = value - near_dot(value, mean)


def attention(
    ea_h, eb_h, wq_h, wk_h, wv_h, wo_h, wpa_h, wpb_h, wd_h, wp_h, wl_h,
    out_ref,
    pa_buf, pb_mid, b_part, row_w, edge_w, conv_w, point_w, head_w, a_mid, a_edge, f1, logits,
    ea, wq, wk, wv, wo, wpa, wpb, wd, wp, wl,
    fb_src, fb_all, fa_all, fa_rows, keys, values, spread, msg, land,
    pb_own, pb_sib, pb_left, pb_right, pb_buf, pa_own, pa_land, taps,
    in_sem, fb_s, fb_r, fa_s, fa_r, rs_s, rs_r, pb_s, pb_r, pa_s, pa_r,
):
    r = lax.axis_index("row")
    c = lax.axis_index("col")
    k = lax.rem(r, 2)
    p = lax.div(r, 2)
    mine = k * COLS + c

    loads = [
        pltpu.make_async_copy(src, dst, in_sem.at[i])
        for i, (src, dst) in enumerate(
            [(eb_h.at[:, pl.ds(0, HALF)], fb_src.at[0]), (eb_h.at[:, pl.ds(HALF, HALF)], fb_src.at[1]),
             (ea_h, ea), (wd_h, wd), (wp_h, wp), (wl_h, wl), (wk_h, wk), (wv_h, wv),
             (wpb_h, wpb), (wq_h, wq), (wo_h, wo), (wpa_h, wpa)]
        )
    ]
    for load in loads[:3]:
        load.start()
    w_eb0, w_eb1, w_ea, w_d, w_p, w_l, w_k, w_v, w_pb, w_q, w_o, w_pa = loads

    x, y = lax.div(r, 8), lax.rem(p, 4)
    z, xl = lax.div(c, 2), lax.rem(c, 2)

    def row_peer(e):
        return (lax.rem(x + lax.div(e, 8), 2) * 8 + lax.rem(y + lax.rem(lax.div(e, 2), 4), 4) * 2
                + lax.rem(k + lax.rem(e, 2), 2))

    def col_peer(e):
        return lax.rem(z + lax.rem(lax.div(e, 2), 4), 4) * 2 + lax.rem(xl + lax.rem(e, 2), 2)

    barrier = pltpu.get_barrier_semaphore()

    def greet(row, col):
        pl.semaphore_signal(barrier, inc=1, device_id=(row, col), device_id_type=MESH)

    @pl.loop(1, ROWS)
    def _(n):
        e = ROWS - n
        greet(row_peer(e), c)
        greet(2 * p + lax.rem(k + lax.div(e, 8), 2), col_peer(e))

    @pl.when((k == 1) & (r < ROWS - 1))
    def _():
        greet(r + 1, 0)

    @pl.when((k == 0) & (r > 0))
    def _():
        greet(r - 2, COLS - 1)

    for load in loads[3:]:
        load.start()

    w_eb0.wait()
    w_eb1.wait()
    fb_all[pl.ds(r, 1)] = fb_src[pl.ds(k, 1)]
    w_ea.wait()
    fa_all[pl.ds(k, 1), pl.ds(c, 1)] = ea[...][None, None]

    first = (k == 0) & (c == 0) & (p > 0)
    last = (k == 0) & (c == COLS - 1) & (p < ROWS // 2 - 1)
    extra = jnp.where(first, COLS, 0) + jnp.where(last, COLS, 0)
    pl.semaphore_wait(barrier, 2 * (ROWS - 1) + extra)

    def fb_copy(e):
        to = row_peer(e)
        return pltpu.make_async_remote_copy(
            src_ref=fb_src.at[lax.rem(to, 2)], dst_ref=fb_all.at[r],
            send_sem=fb_s, recv_sem=fb_r.at[lax.div(e, 8)],
            device_id=(to, c), device_id_type=MESH)

    def fb_some(n, far):
        part = fb_all.at[pl.ds(0, n)]
        return pltpu.make_async_remote_copy(
            src_ref=part, dst_ref=part, send_sem=fb_s, recv_sem=fb_r.at[far],
            device_id=(2 * p + 1 - k, c), device_id_type=MESH)

    def fa_whole():
        part = fa_all.at[0, pl.ds(0, COLS - 1)]
        return pltpu.make_async_remote_copy(
            src_ref=part, dst_ref=part, send_sem=fa_s.at[1], recv_sem=fa_r.at[1],
            device_id=(2 * p + 1 - k, c), device_id_type=MESH)

    def fa_copy(e):
        return pltpu.make_async_remote_copy(
            src_ref=ea, dst_ref=fa_all.at[k, c],
            send_sem=fa_s.at[1], recv_sem=fa_r.at[1],
            device_id=(r, col_peer(e)), device_id_type=MESH)

    def fa_sibling():
        return pltpu.make_async_remote_copy(
            src_ref=fa_all.at[k], dst_ref=fa_all.at[k],
            send_sem=fa_s.at[0], recv_sem=fa_r.at[0],
            device_id=(2 * p + 1 - k, c), device_id_type=MESH)

    @pl.loop(1, COLS)
    def _(n):
        fa_copy(COLS - n).start()

    @pl.loop(1, ROWS)
    def _(n):
        fb_copy(ROWS - n).start()

    w_d.wait()
    w_p.wait()
    w_l.wait()
    prepare_weights(wd, wp, wl, taps, row_w, edge_w, conv_w, point_w, head_w, c)
    l, f = iota((128, E), 0), iota((128, E), 1)
    start = (l & (H - 1)) * D
    spread[...] = jnp.where((l < 2 * H) & (f >= start) & (f < start + D), 1.0, 0.0).astype(BF16)

    fa_whole().wait_recv()
    fa_sibling().start()

    n0, n1 = iota((HALF, HALF), 0), iota((HALF, HALF), 1)
    order = jnp.where(n0 < HALF // 2, 2 * n0, 2 * n0 - (HALF - 1))
    order = jnp.where(n1 == order, 1.0, 0.0).astype(BF16)

    def features(side):
        blocks = fb_all[pl.ds(8 * side, 8)].reshape(E // 2, HALF)
        return dot(order, blocks, NT).astype(BF16)

    def some_rows(side):
        return pl.ds(pl.multiple_of(side * (E // 2), 128), E // 2)

    def pair_weights(side):
        part = wpb[:, some_rows(side)]
        return jnp.concatenate([part, part], axis=0)

    fb_some(7, 0).wait_recv()
    w_k.wait()
    w_v.wait()
    w_pb.wait()
    near = features(x)
    for t in range(5):
        at = slice(256 * t, 256 * t + 256)
        keys[:, at] = dot(near, wk[some_rows(x), at])
        values[:, at] = dot(near, wv[some_rows(x), at])
    near_b = dot(near, pair_weights(x), NT)

    fa_sibling().wait_recv()
    fa = jnp.concatenate(
        [jnp.concatenate([fa_all[kk, cc].astype(F32) for cc in range(COLS)], axis=1)
         for kk in range(2)], axis=0)
    fa_rows[...] = fa
    w_q.wait()
    query = dot(fa.astype(BF16), wq[...]).astype(BF16).astype(F32)

    fb_some(8, 1).wait_recv()
    far = features(1 - x)
    rows = 2 * TILE_A
    lane256 = iota((rows, 256), 1)

    def heads_of(t):
        return range(3 * t, 3 * t + 4)

    def inside(h, t):
        return (lane256 >= D * h - 256 * t) & (lane256 < D * h + D - 256 * t)

    spans = [slice(256 * t, 256 * t + 256) for t in range(5)]
    masked = [jnp.concatenate([jnp.where(inside(h, t), query[:, spans[t]], 0.0)
                               for h in heads_of(t)], axis=0).astype(BF16) for t in range(5)]
    key_parts = [keys[:, at] + dot(far, wk[some_rows(1 - x), at]) for at in spans]
    founds = [dot(masked[t], key_parts[t].astype(BF16), NT) for t in range(5)]
    value_parts = [values[:, at] + dot(far, wv[some_rows(1 - x), at]) for at in spans]
    scores = [None] * H
    for t in range(5):
        for n, h in enumerate(heads_of(t)):
            piece = founds[t][rows * n:rows * n + rows]
            scores[h] = piece if scores[h] is None else scores[h] + piece

    lane = iota((rows, 128), 1)
    head_of = lane & (H - 1)
    tops = jnp.zeros((rows, 128), F32)
    totals = jnp.zeros((rows, 128), F32)
    weights = []
    for h in range(H):
        s = scores[h] * (1.0 / math.sqrt(D))
        top = jnp.max(s, axis=1, keepdims=True)
        w = jnp.exp(s - top)
        tops = jnp.where(head_of == h, top, tops)
        totals = jnp.where(head_of == h, jnp.sum(w, axis=1, keepdims=True), totals)
        weights.append(w.astype(BF16))
    founds = [dot(jnp.concatenate(weights[3 * t:3 * t + 4], axis=0), value_parts[t].astype(BF16))
              for t in range(5)]
    t1, t2, t3 = (x.astype(F32) for x in split3(tops))
    n1, n2, _ = (x.astype(F32) for x in split3(totals))
    stats = jnp.where(lane < 16, t1, jnp.where(lane < 32, t2, jnp.where(
        lane < 48, t3, jnp.where(lane < 64, n1, jnp.where(lane < 80, n2, 0.0)))))

    mixed = []
    for t in range(5):
        total = sum(jnp.where(inside(h, t), founds[t][rows * n:rows * n + rows], 0.0)
                    for n, h in enumerate(heads_of(t)))
        mixed += [total[:, :128], total[:, 128:]]
    for d in range(COLS):
        block = [m[8 * d:8 * d + 8] for m in mixed + [stats]] + [jnp.zeros((8, 128), F32)]
        msg[d] = jnp.concatenate(block, axis=0).astype(BF16)

    def rs_copy(d):
        to = col_peer(d)
        return pltpu.make_async_remote_copy(
            src_ref=msg.at[to], dst_ref=land.at[mine],
            send_sem=rs_s, recv_sem=rs_r,
            device_id=(2 * p, to), device_id_type=MESH)

    def rs_whole(n):
        return pltpu.make_async_remote_copy(
            src_ref=land.at[pl.ds(0, n)], dst_ref=land.at[pl.ds(0, n)],
            send_sem=rs_s, recv_sem=rs_r, device_id=(2 * p + 1 - k, c), device_id_type=MESH)

    @pl.loop(1, COLS)
    def _(n):
        rs_copy(COLS - n).start()

    @pl.when(k == 1)
    def _():
        rs_copy(0).start()

    found_b = near_b + dot(far, pair_weights(1 - x), NT)
    pb_own[...] = jnp.where(iota((HALF // 2, 128), 1) < C, found_b[:HALF // 2], found_b[HALF // 2:])

    def sib_copy():
        return pltpu.make_async_remote_copy(
            src_ref=pb_own, dst_ref=pb_sib, send_sem=pb_s.at[0], recv_sem=pb_r.at[0],
            device_id=(2 * p + 1 - k, c), device_id_type=MESH)

    def right_copy(kk):
        return pltpu.make_async_remote_copy(
            src_ref=pb_own.at[pl.ds(HALF // 2 - 8, 8)], dst_ref=pb_left,
            send_sem=pb_s.at[1 + kk], recv_sem=pb_r.at[1],
            device_id=(2 * p + kk, lax.rem(c + 1, COLS)), device_id_type=MESH)

    def left_copy(kk):
        return pltpu.make_async_remote_copy(
            src_ref=pb_own.at[pl.ds(0, 8)], dst_ref=pb_right,
            send_sem=pb_s.at[1 + kk], recv_sem=pb_r.at[2],
            device_id=(2 * p + kk, lax.rem(c + COLS - 1, COLS)), device_id_type=MESH)

    sends_right = (k == 1) & (c < COLS - 1)
    sends_left = (k == 0) & (c > 0)
    sib_copy().start()

    @pl.when(sends_right)
    def _():
        right_copy(0).start()
        right_copy(1).start()

    @pl.when(sends_left)
    def _():
        left_copy(0).start()
        left_copy(1).start()

    sib_copy().wait_recv()

    @pl.when(c > 0)
    def _():
        right_copy(0).wait_recv()

    @pl.when(c < COLS - 1)
    def _():
        left_copy(0).wait_recv()

    zero8 = jnp.zeros((8, 128), F32)
    own, sib = pb_own[...], pb_sib[...]
    even = k == 0
    pb_buf[0:8] = jnp.where(c > 0, pb_left[...], zero8)
    pb_buf[8:72] = jnp.where(even, own, sib)
    pb_buf[72:136] = jnp.where(even, sib, own)
    pb_buf[136:144] = jnp.where(c < COLS - 1, pb_right[...], zero8)
    pb_buf[144:152] = zero8
    column_part(pb_buf, taps, pb_mid, b_part)

    def pa_copy(row, col, slot, sem):
        return pltpu.make_async_remote_copy(
            src_ref=pa_own, dst_ref=pa_land.at[slot],
            send_sem=pa_s.at[sem], recv_sem=pa_r.at[slot],
            device_id=(row, col), device_id_type=MESH)

    def pa_whole(n, sem):
        part = pb_buf.at[pl.ds(0, 8 * n)]
        return pltpu.make_async_remote_copy(
            src_ref=part, dst_ref=part, send_sem=pa_s.at[sem], recv_sem=pa_r.at[0],
            device_id=(2 * p + 1 - k, c), device_id_type=MESH)

    targets = (
        (2 * p, c + 1, c <= 4),
        (2 * p + 1, c - 3, c >= 3),
        (2 * p - 1, 5, (c == 0) & (p > 0)),
        (2 * p + 2, 0, (c == COLS - 1) & (p < ROWS // 2 - 1)),
    )
    w_o.wait()
    w_pa.wait()

    @pl.when(k == 0)
    def _():
        land[pl.ds(c, 1)] = msg[pl.ds(c, 1)]

        rs_whole(2 * COLS - 1).wait_recv()
        got = [land[g].astype(F32) for g in range(2 * COLS)]
        stat = jnp.concatenate([x[80:88] for x in got], axis=0).astype(BF16)
        a, b = iota((128, 128), 0), iota((128, 128), 1)
        same = (a & (H - 1)) == (b & (H - 1))
        pick_top = jnp.where(same & (a < 48), 1.0, 0.0).astype(BF16)
        pick_total = jnp.where(same & (a >= 48) & (a < 80), 1.0, 0.0).astype(BF16)
        picked = dot(stat, jnp.concatenate([pick_top, pick_total], axis=1))
        top, total = picked[:, :128], picked[:, 128:]
        tops = [top[8 * g:8 * g + 8] for g in range(2 * COLS)]
        summit = functools.reduce(jnp.maximum, tops)
        scales = [jnp.exp(x - summit) for x in tops]
        whole = sum(s * total[8 * g:8 * g + 8] for g, s in enumerate(scales))
        factor = jnp.concatenate([s / whole for s in scales], axis=0)
        high = factor.astype(BF16).astype(F32)
        factor = jnp.where(b < H, high, jnp.where(b < 2 * H, factor - high, 0.0)).astype(BF16)
        factors = dot(factor, spread[...])
        attended = []
        for t in range(10):
            attended.append(sum(
                got[g][8 * t:8 * t + 8] * factors[8 * g:8 * g + 8, 128 * t:128 * t + 128]
                for g in range(2 * COLS)))
        attended = jnp.concatenate(attended, axis=1).astype(BF16)
        hidden = fa_rows[pl.ds(pl.multiple_of(8 * c, 8), 8), :] + dot(attended, wo[...])
        centre = hidden - jnp.mean(hidden, axis=1, keepdims=True)
        spread_h = jnp.mean(centre * centre, axis=1, keepdims=True)
        normed = (centre * lax.rsqrt(spread_h + 1e-5)).astype(BF16)
        pa_own[...] = dot(normed, jnp.concatenate([wpa[...], wpa[...]], axis=0), NT)
        for n, (row, slot, on) in enumerate(targets):
            @pl.when(on)
            def _():
                @pl.loop(0, COLS)
                def _(m):
                    col = col_peer(COLS - 1 - m)
                    local = (row == r) & (col == c)

                    @pl.when(local)
                    def _():
                        pa_land[pl.ds(slot, 1)] = pa_own[...][None]

                    @pl.when(jnp.logical_not(local))
                    def _():
                        pa_copy(row, col, slot, n).start()

    fb_some(ROWS - 1, 0).wait_send()
    fa_whole().wait_send()
    fa_sibling().wait_send()
    sib_copy().wait_send()

    @pl.when(sends_right)
    def _():
        right_copy(0).wait_send()
        right_copy(1).wait_send()

    @pl.when(sends_left)
    def _():
        left_copy(0).wait_send()
        left_copy(1).wait_send()

    @pl.when(k == 0)
    def _():
        rs_whole(COLS - 1).wait_send()

    @pl.when(k == 1)
    def _():
        rs_whole(COLS).wait_send()

    mean = mean_matrix(256)
    qq = iota((QW, 128), 0)
    in_map = ((qq > 0) | (c > 0)) & ((qq < HALF + 1) | (c < COLS - 1))
    first = functools.partial(
        first_blocks, r=r, in_map=in_map, mean=mean, pa_buf=pa_buf, pb_mid=pb_mid, b_part=b_part,
        a_mid=a_mid, a_edge=a_edge, point_w=point_w, f1=f1)
    second = functools.partial(correlate, conv_w=conv_w, f1=f1)
    last_part = functools.partial(read_out, mean=mean, head_w=head_w, logits=logits)
    mine_slot = jnp.where((k == 0) & (c <= 4), c + 1, -1)
    pa_buf[...] = jnp.zeros_like(pa_buf)
    for s in range(1, 5):
        @pl.when(s != mine_slot)
        def _():
            pa_copy(r, c, s, 0).wait_recv()

        pa_buf[8 * s:8 * s + 8] = pa_land[s]
    row_parts(pa_buf, row_w, edge_w, a_mid, a_edge, ((4, 32),), r)
    for _ in first(list(range(4, 32, 2))):
        pass
    part1 = second(1)
    part2 = second(2)
    last_part(1, *part1)
    last_part(2, *part2)

    @pl.when(r > 0)
    def _():
        pa_copy(r, c, 0, 0).wait_recv()
        pa_buf[0:8] = pa_land[0]

    @pl.when((r < ROWS - 1) & (mine_slot != 5))
    def _():
        pa_copy(r, c, 5, 0).wait_recv()

    @pl.when(r < ROWS - 1)
    def _():
        pa_buf[40:48] = pa_land[5]

    row_parts(pa_buf, row_w, edge_w, a_mid, a_edge, ((0, 4), (32, 36)), r)
    for _ in first([0, 2, 32, 34]):
        pass
    part0 = second(0)
    part3 = second(3)
    last_part(0, *part0)
    last_part(3, *part3)
    out_ref[...] = side_by_side(logits)

    @pl.when(k == 0)
    def _():
        for n, (row, slot, on) in enumerate(targets):
            @pl.when(on & (row == r))
            def _():
                pa_whole(COLS - 1, n).wait_send()

            @pl.when(on & (row != r))
            def _():
                pa_whole(COLS, n).wait_send()


def gelu_twice(x):
    x = x.astype(BF16)
    inner = x * (BF16(0.7978845608028654) + BF16(0.035677408136300125) * (x * x))
    return x + x * jnp.tanh(inner)


def squared(x):
    x = x.astype(BF16)
    return x * x


def row_parts(pa_buf, row_w, edge_w, a_mid, a_edge, spans, r):
    place = iota((48, 128), 0) + (TILE_A * r - 8)
    pa = jnp.where((place >= 0) & (place < LA), pa_buf[...], 0.0)
    kinds = [[row_w[u:u + 1] for u in range(5)]]
    kinds += [[edge_w[n, u:u + 1] for u in range(5)] for n in range(2)]
    value = jnp.concatenate(
        [sum(w[u] * pa[4 + u:44 + u] for u in range(5)) for w in kinds], axis=0)
    value = value - near_dot(value, mean_matrix(128))
    for low, high in spans:
        a_mid[low:high] = value[low:high]
        a_edge[0, low:high] = value[40 + low:40 + high]
        a_edge[1, low:high] = value[80 + low:80 + high]


def first_blocks(rows, r, in_map, mean, pa_buf, pb_mid, b_part, a_mid, a_edge, point_w, f1):
    top, bottom = r == 0, r == ROWS - 1
    kinds = {2: jnp.where(top, 0, 2), 3: jnp.where(top, 1, 2),
             32: jnp.where(bottom, 3, 2), 33: jnp.where(bottom, 4, 2)}

    sub = iota((8, 128), 0)

    def part_of(w):
        part = b_part[kinds.get(w, 2)]
        row = a_mid[w:w + 1]
        return jnp.concatenate([
            part[:8] + jnp.where(sub == 1, a_edge[0, w:w + 1], row),
            part[8:HALF] + row,
            part[HALF:] + jnp.where(sub == 0, a_edge[1, w:w + 1], row)], axis=0)

    def start(u):
        x = jnp.concatenate([part_of(u), part_of(u + 1)], axis=1)
        return x, dot(squared(x), mean)

    def middle(x, var):
        return dot(gelu_twice(x * lax.rsqrt(var + 1e-5)), point_w[...])

    def end(u, update):
        for n in range(2):
            keep = in_map
            if u < 2:
                keep = keep & jnp.logical_not(top)
            if u >= 34:
                keep = keep & jnp.logical_not(bottom)
            field = pb_mid[...] + pa_buf[u + n + 6:u + n + 7] + update[:, 128 * n:128 * n + 128]
            f1[u + n] = jnp.where(keep, field, 0.0)

    started, updates = {}, {}
    count = len(rows)
    for n in range(count + 2):
        if n < count:
            started[n] = start(rows[n])
        if 1 <= n <= count:
            updates[n - 1] = middle(*started.pop(n - 1))
        if n >= 2:
            end(rows[n - 2], updates.pop(n - 2))
            yield rows[n - 2]


def correlate(step, conv_w, f1):
    pieces = {}
    for u in range(8 * step, 8 * step + 12):
        for q in range(3):
            pieces[u, q] = f1[u, q:q + HALF, :].astype(BF16)

    def tall(u, q):
        return jnp.concatenate([pieces[8 * step + 2 * n + u, q] for n in range(4)], axis=0)

    around = jnp.concatenate([tall(u, q) for u in range(6) for q in range(3)], axis=1)
    return dot(around, conv_w[...]), [tall(2, 1), tall(3, 1)]


def read_out(step, x, field, mean, head_w, logits):
    var = dot(squared(x), mean)
    g = gelu_twice(x * lax.rsqrt(var + 1e-5))
    found = dot(head_w[...], jnp.concatenate(field + [g], axis=1), NT)
    found = found[0:4] + found[4:8]
    for n in range(4):
        for o in range(2):
            for s in range(2):
                at = TILE_A * s + 8 * step + 2 * n + o
                logits[at:at + 1] = found[2 * o + s:2 * o + s + 1, HALF * n:HALF * n + HALF]


def side_by_side(logits):
    total = None
    for s in range(2):
        place = iota((HALF, TILE_B), 1) == 2 * iota((HALF, TILE_B), 0) + s
        place = jnp.where(place, 1.0, 0.0).astype(BF16)
        piece = near_dot(logits[TILE_A * s:TILE_A * s + TILE_A], place)
        total = piece if total is None else total + piece
    return total


def local(
    emb_a, emb_b, w_query, w_key, w_value, w_out, w_pair_a, w_pair_b, w_depth, w_point, w_logit
):
    hbm = pl.BlockSpec(memory_space=pltpu.HBM)
    vmem = pl.BlockSpec(memory_space=pltpu.VMEM)
    weight = pltpu.VMEM((E, E), BF16)
    dma = pltpu.SemaphoreType.DMA
    return pl.pallas_call(
        attention,
        out_shape=pltpu.VMEM((TILE_A, TILE_B), F32),
        in_specs=[hbm] * 11,
        out_specs=vmem,
        scratch_shapes=[
            pltpu.VMEM((48, 128), F32),
            pltpu.VMEM((QW, 128), F32),
            pltpu.VMEM((5, QW, 128), F32),
            pltpu.VMEM((8, 128), F32),
            pltpu.VMEM((2, 8, 128), F32),
            pltpu.VMEM((18 * 128, 256), BF16),
            pltpu.VMEM((256, 256), BF16),
            pltpu.VMEM((8, 512), BF16),
            pltpu.VMEM((40, 128), F32),
            pltpu.VMEM((2, 40, 128), F32),
            pltpu.VMEM((36, QW, 128), F32),
            pltpu.VMEM((2 * TILE_A, 128), F32),
            pltpu.VMEM((TILE_A, E // COLS), BF16),
            weight, weight, weight, weight,
            pltpu.VMEM((C, E), BF16),
            pltpu.VMEM((C, E), BF16),
            pltpu.VMEM((25, 2, C), F32),
            pltpu.VMEM((2, C, C), BF16),
            pltpu.VMEM((1, C), F32),
            pltpu.VMEM((2, D, HALF), BF16),
            pltpu.VMEM((ROWS, D, HALF), BF16),
            pltpu.VMEM((2, COLS, TILE_A, E // COLS), BF16),
            pltpu.VMEM((2 * TILE_A, E), F32),
            pltpu.VMEM((HALF, E), F32),
            pltpu.VMEM((HALF, E), F32),
            pltpu.VMEM((128, E), BF16),
            pltpu.VMEM((COLS, 96, 128), BF16),
            pltpu.VMEM((2 * COLS, 96, 128), BF16),
            pltpu.VMEM((HALF // 2, 128), F32),
            pltpu.VMEM((HALF // 2, 128), F32),
            pltpu.VMEM((8, 128), F32),
            pltpu.VMEM((8, 128), F32),
            pltpu.VMEM((152, 128), F32),
            pltpu.VMEM((8, 128), F32),
            pltpu.VMEM((6, 8, 128), F32),
            pltpu.VMEM((2, 32, 128), F32),
            dma((12,)),
            dma, dma((2,)),
            dma((2,)), dma((2,)),
            dma, dma,
            dma((3,)), dma((3,)),
            dma((4,)), dma((6,)),
        ],
        compiler_params=pltpu.CompilerParams(
            collective_id=0, has_side_effects=True, vmem_limit_bytes=48 * 2 ** 20),
        name="contact_map",
    )(*(pltpu.with_memory_space_constraint(a, pltpu.HBM) for a in (
        emb_a, emb_b.T, w_query, w_key, w_value, w_out, w_pair_a.T, w_pair_b.T,
        jnp.transpose(w_depth, (2, 0, 1)), w_point, w_logit.reshape(1, C))))


def solution(mesh):
    in_specs = (P("row", "col"), P("col", "row"), P(), P(), P(), P(), P(), P(), P(), P(), P())
    out_specs = P("row", "col")
    return jax.shard_map(local, mesh=mesh, in_specs=in_specs, out_specs=out_specs, check_vma=False)
```

```python
import functools
import math

import jax
import jax.numpy as jnp
from jax import lax
from jax.experimental import pallas as pl
from jax.experimental.pallas import tpu as pltpu
from jax.sharding import PartitionSpec as P

E = 1280
H = 16
D = E // H
C = 64
ROWS = 16
COLS = 8
LA = 512
LB = 2048
TILE_A = LA // ROWS
TILE_B = LB // COLS
HALF = TILE_B // 2
F32 = jnp.float32
BF16 = jnp.bfloat16
MESH = pl.DeviceIdType.MESH
NN = (((1,), (0,)), ((), ()))
NT = (((1,), (1,)), ((), ()))


def dot(a, b, dims=NN):
    return lax.dot_general(a, b, dims, preferred_element_type=F32)


def iota(shape, axis):
    return lax.broadcasted_iota(jnp.int32, shape, axis)


def eye(n):
    return jnp.where(iota((n, n), 0) == iota((n, n), 1), 1.0, 0.0).astype(BF16)


def doubled(n):
    lane = iota((n, 2 * n), 1)
    lane = jnp.where(lane >= n, lane - n, lane)
    return jnp.where(iota((n, 2 * n), 0) == lane, 1.0, 0.0).astype(BF16)


def split3(x):
    high = x.astype(BF16)
    rest = x - high.astype(F32)
    mid = rest.astype(BF16)
    low = (rest - mid.astype(F32)).astype(BF16)
    return high, mid, low


def exact_dot(x, ones, dims=NN):
    return sum(dot(part, ones, dims) for part in split3(x))


def near_dot(x, ones):
    high, mid, _ = split3(x)
    return dot(high, ones) + dot(mid, ones)


QW = 136


def prepare_weights(wd, wp, wl, taps, row_w, edge_w, conv_w, point_w, head_w, c):
    double = doubled(C)
    for s in range(2):
        taps[s, 0:25] = exact_dot(wd[:, s, :], double)

    def tap(u, v):
        return taps[0, 5 * u + v:5 * u + v + 1, :]

    for u in range(5):
        row_w[u:u + 1] = sum(tap(u, v) for v in range(5))
    for n, start in enumerate((1, HALF)):
        column = 2 * start + jnp.where(iota((1, 128), 1) < C, 0, 1) + TILE_B * c - 2
        for u in range(5):
            total = None
            for v in range(5):
                at = column + (v - 2)
                piece = jnp.where((at >= 0) & (at < LB), tap(u, v), 0.0)
                total = piece if total is None else total + piece
            edge_w[n, u:u + 1] = total

    a, b = iota((128, 128), 0), iota((128, 128), 1)
    upper, left = a < C, b < C
    same = upper == left
    rest = jnp.where((a & (C - 1)) == (b & (C - 1)), 1.0 - 1.0 / C, -1.0 / C)
    columns = sum(dot(jnp.concatenate([eye(C), eye(C)], axis=0), part, NT)
                  for part in split3(wd[:, 1, :]))

    def spread(u, v):
        if not 0 <= v < 5:
            return 0.0
        return columns[:, 5 * u + v:5 * u + v + 1]

    zero = jnp.zeros((128, 128), BF16)
    for q in range(3):
        blocks = []
        for u in range(5):
            block = jnp.where(same, spread(u, 2 * q),
                              jnp.where(upper, spread(u, 2 * q - 1), spread(u, 2 * q + 1)))
            blocks.append((block * rest).astype(BF16))
        for u in range(6):
            at = 128 * (3 * u + q)
            conv_w[at:at + 128, 0:128] = blocks[u] if u < 5 else zero
            conv_w[at:at + 128, 128:256] = blocks[u - 1] if u > 0 else zero

    point = dot(wp[0], double)
    point = jnp.concatenate([point, point], axis=1)
    point = jnp.concatenate([point] * 4, axis=0)
    fits = (iota((256, 256), 0) // C) == (iota((256, 256), 1) // C)
    point_w[...] = jnp.where(fits, 0.5 * point, 0.0).astype(BF16)

    read = jnp.broadcast_to(wl[...], (8, C))
    folded = 0.5 * sum(dot(part, wp[1], NT) for part in split3(read))
    row8, lane8 = iota((8, 256), 0), iota((8, 256), 1)
    fits8 = (row8 & 3) == (lane8 // C)
    for n, values in enumerate((read, folded)):
        both = exact_dot(values, double)
        both = jnp.concatenate([both, both], axis=1)
        high = both.astype(BF16).astype(F32)
        picked = jnp.where(row8 < 4, high, both - high)
        head_w[:, 256 * n:256 * n + 256] = jnp.where(fits8, picked, 0.0).astype(BF16)


def mean_matrix(n):
    fits = (iota((n, n), 0) // C) == (iota((n, n), 1) // C)
    return jnp.where(fits, 1.0 / C, 0.0).astype(BF16)


def column_part(pb_buf, taps, pb_mid, b_part):
    mean = mean_matrix(128)
    left = iota((1, 128), 1) < C
    plain = [pb_buf[6 + q:6 + q + QW] for q in range(3)]
    pb_mid[...] = plain[1]
    crossed = [pltpu.roll(x, C, 1) for x in plain]

    for n, (low, high) in enumerate(((2, 5), (1, 5), (0, 5), (0, 4), (0, 3))):
        w = [sum(taps[0, 5 * u + v:5 * u + v + 1, :] for u in range(low, high)) for v in range(5)]
        value = (w[0] * plain[0] + w[2] * plain[1] + w[4] * plain[2]
                 + jnp.where(left, w[1], 0.0) * crossed[0]
                 + jnp.where(left, w[3], w[1]) * crossed[1]
                 + jnp.where(left, 0.0, w[3]) * crossed[2])
        b_part[n] = value - near_dot(value, mean)


def attention(
    ea_h, eb_h, wq_h, wk_h, wv_h, wo_h, wpa_h, wpb_h, wd_h, wp_h, wl_h,
    out_ref,
    pa_buf, pb_mid, b_part, row_w, edge_w, conv_w, point_w, head_w, a_mid, a_edge, f1, logits,
    ea, wq, wk, wv, wo, wpa, wpb, wd, wp, wl,
    fb_src, fb_all, fa_all, fa_rows, keys, values, masked, spread, msg, land,
    pb_own, pb_sib, pb_left, pb_right, pb_buf, pa_own, pa_land, taps,
    in_sem, fb_s, fb_r, fa_s, fa_r, rs_s, rs_r, pb_s, pb_r, pa_s, pa_r,
):
    r = lax.axis_index("row")
    c = lax.axis_index("col")
    k = lax.rem(r, 2)
    p = lax.div(r, 2)
    mine = k * COLS + c

    loads = [
        pltpu.make_async_copy(src, dst, in_sem.at[i])
        for i, (src, dst) in enumerate(
            [(eb_h.at[:, pl.ds(0, HALF)], fb_src.at[0]), (eb_h.at[:, pl.ds(HALF, HALF)], fb_src.at[1]),
             (ea_h, ea), (wd_h, wd), (wp_h, wp), (wl_h, wl), (wk_h, wk), (wv_h, wv),
             (wpb_h, wpb), (wq_h, wq), (wo_h, wo), (wpa_h, wpa)]
        )
    ]
    for load in loads[:3]:
        load.start()
    w_eb0, w_eb1, w_ea, w_d, w_p, w_l, w_k, w_v, w_pb, w_q, w_o, w_pa = loads

    x, y = lax.div(r, 8), lax.rem(p, 4)
    z, xl = lax.div(c, 2), lax.rem(c, 2)

    def row_peer(e):
        return (lax.rem(x + lax.div(e, 8), 2) * 8 + lax.rem(y + lax.rem(lax.div(e, 2), 4), 4) * 2
                + lax.rem(k + lax.rem(e, 2), 2))

    def col_peer(e):
        return lax.rem(z + lax.rem(lax.div(e, 2), 4), 4) * 2 + lax.rem(xl + lax.rem(e, 2), 2)

    barrier = pltpu.get_barrier_semaphore()

    def greet(row, col):
        pl.semaphore_signal(barrier, inc=1, device_id=(row, col), device_id_type=MESH)

    @pl.loop(1, ROWS)
    def _(n):
        e = ROWS - n
        greet(row_peer(e), c)
        greet(2 * p + lax.rem(k + lax.div(e, 8), 2), col_peer(e))

    @pl.when((k == 1) & (r < ROWS - 1))
    def _():
        greet(r + 1, 0)

    @pl.when((k == 0) & (r > 0))
    def _():
        greet(r - 2, COLS - 1)

    for load in loads[3:]:
        load.start()

    w_eb0.wait()
    w_eb1.wait()
    fb_all[pl.ds(r, 1)] = fb_src[pl.ds(k, 1)]
    w_ea.wait()
    fa_all[pl.ds(k, 1), pl.ds(c, 1)] = ea[...][None, None]

    first = (k == 0) & (c == 0) & (p > 0)
    last = (k == 0) & (c == COLS - 1) & (p < ROWS // 2 - 1)
    extra = jnp.where(first, COLS, 0) + jnp.where(last, COLS, 0)
    pl.semaphore_wait(barrier, 2 * (ROWS - 1) + extra)

    def fb_copy(e):
        to = row_peer(e)
        return pltpu.make_async_remote_copy(
            src_ref=fb_src.at[lax.rem(to, 2)], dst_ref=fb_all.at[r],
            send_sem=fb_s, recv_sem=fb_r.at[lax.div(e, 8)],
            device_id=(to, c), device_id_type=MESH)

    def fb_some(n, far):
        part = fb_all.at[pl.ds(0, n)]
        return pltpu.make_async_remote_copy(
            src_ref=part, dst_ref=part, send_sem=fb_s, recv_sem=fb_r.at[far],
            device_id=(2 * p + 1 - k, c), device_id_type=MESH)

    def fa_whole():
        part = fa_all.at[0, pl.ds(0, COLS - 1)]
        return pltpu.make_async_remote_copy(
            src_ref=part, dst_ref=part, send_sem=fa_s.at[1], recv_sem=fa_r.at[1],
            device_id=(2 * p + 1 - k, c), device_id_type=MESH)

    def fa_copy(e):
        return pltpu.make_async_remote_copy(
            src_ref=ea, dst_ref=fa_all.at[k, c],
            send_sem=fa_s.at[1], recv_sem=fa_r.at[1],
            device_id=(r, col_peer(e)), device_id_type=MESH)

    def fa_sibling():
        return pltpu.make_async_remote_copy(
            src_ref=fa_all.at[k], dst_ref=fa_all.at[k],
            send_sem=fa_s.at[0], recv_sem=fa_r.at[0],
            device_id=(2 * p + 1 - k, c), device_id_type=MESH)

    @pl.loop(1, COLS)
    def _(n):
        fa_copy(COLS - n).start()

    @pl.loop(1, ROWS)
    def _(n):
        fb_copy(ROWS - n).start()

    w_d.wait()
    w_p.wait()
    w_l.wait()
    prepare_weights(wd, wp, wl, taps, row_w, edge_w, conv_w, point_w, head_w, c)
    l, f = iota((128, E), 0), iota((128, E), 1)
    start = (l & (H - 1)) * D
    spread[...] = jnp.where((l < 2 * H) & (f >= start) & (f < start + D), 1.0, 0.0).astype(BF16)

    fa_whole().wait_recv()
    fa_sibling().start()

    n0, n1 = iota((HALF, HALF), 0), iota((HALF, HALF), 1)
    order = jnp.where(n0 < HALF // 2, 2 * n0, 2 * n0 - (HALF - 1))
    order = jnp.where(n1 == order, 1.0, 0.0).astype(BF16)

    def features(side):
        blocks = fb_all[pl.ds(8 * side, 8)].reshape(E // 2, HALF)
        return dot(order, blocks, NT).astype(BF16)

    def some_rows(side):
        return pl.ds(pl.multiple_of(side * (E // 2), 128), E // 2)

    def pair_weights(side):
        part = wpb[:, some_rows(side)]
        return jnp.concatenate([part, part], axis=0)

    fb_some(7, 0).wait_recv()
    w_k.wait()
    w_v.wait()
    w_pb.wait()
    near = features(x)
    for t in range(5):
        at = slice(256 * t, 256 * t + 256)
        keys[:, at] = dot(near, wk[some_rows(x), at])
        values[:, at] = dot(near, wv[some_rows(x), at])
    near_b = dot(near, pair_weights(x), NT)

    fa_sibling().wait_recv()
    fa = jnp.concatenate(
        [jnp.concatenate([fa_all[kk, cc].astype(F32) for cc in range(COLS)], axis=1)
         for kk in range(2)], axis=0)
    fa_rows[...] = fa
    w_q.wait()
    query = dot(fa.astype(BF16), wq[...]).astype(BF16).astype(F32)

    rows = 2 * TILE_A
    lane256 = iota((rows, 256), 1)

    def heads_of(t):
        return range(3 * t, 3 * t + 4)

    def inside(h, t):
        return (lane256 >= D * h - 256 * t) & (lane256 < D * h + D - 256 * t)

    spans = [slice(256 * t, 256 * t + 256) for t in range(5)]
    for t in range(5):
        masked[t] = jnp.concatenate([jnp.where(inside(h, t), query[:, spans[t]], 0.0)
                                     for h in heads_of(t)], axis=0).astype(BF16)

    fb_some(8, 1).wait_recv()
    far = features(1 - x)
    key_parts = [keys[:, at] + dot(far, wk[some_rows(1 - x), at]) for at in spans]
    founds = [dot(masked[t], key_parts[t].astype(BF16), NT) for t in range(5)]
    value_parts = [values[:, at] + dot(far, wv[some_rows(1 - x), at]) for at in spans]
    scores = [None] * H
    for t in range(5):
        for n, h in enumerate(heads_of(t)):
            piece = founds[t][rows * n:rows * n + rows]
            scores[h] = piece if scores[h] is None else scores[h] + piece

    lane = iota((rows, 128), 1)
    head_of = lane & (H - 1)
    tops = jnp.zeros((rows, 128), F32)
    totals = jnp.zeros((rows, 128), F32)
    weights = []
    for h in range(H):
        s = scores[h] * (1.0 / math.sqrt(D))
        top = jnp.max(s, axis=1, keepdims=True)
        w = jnp.exp(s - top)
        tops = jnp.where(head_of == h, top, tops)
        totals = jnp.where(head_of == h, jnp.sum(w, axis=1, keepdims=True), totals)
        weights.append(w.astype(BF16))
    founds = [dot(jnp.concatenate(weights[3 * t:3 * t + 4], axis=0), value_parts[t].astype(BF16))
              for t in range(5)]
    t1, t2, t3 = (x.astype(F32) for x in split3(tops))
    n1, n2, _ = (x.astype(F32) for x in split3(totals))
    stats = jnp.where(lane < 16, t1, jnp.where(lane < 32, t2, jnp.where(
        lane < 48, t3, jnp.where(lane < 64, n1, jnp.where(lane < 80, n2, 0.0)))))

    mixed = []
    for t in range(5):
        total = sum(jnp.where(inside(h, t), founds[t][rows * n:rows * n + rows], 0.0)
                    for n, h in enumerate(heads_of(t)))
        mixed += [total[:, :128], total[:, 128:]]
    for d in range(COLS):
        block = [m[8 * d:8 * d + 8] for m in mixed + [stats]] + [jnp.zeros((8, 128), F32)]
        msg[d] = jnp.concatenate(block, axis=0).astype(BF16)

    def rs_copy(d):
        to = col_peer(d)
        return pltpu.make_async_remote_copy(
            src_ref=msg.at[to], dst_ref=land.at[mine],
            send_sem=rs_s, recv_sem=rs_r,
            device_id=(2 * p, to), device_id_type=MESH)

    def rs_whole(n):
        return pltpu.make_async_remote_copy(
            src_ref=land.at[pl.ds(0, n)], dst_ref=land.at[pl.ds(0, n)],
            send_sem=rs_s, recv_sem=rs_r, device_id=(2 * p + 1 - k, c), device_id_type=MESH)

    @pl.loop(1, COLS)
    def _(n):
        rs_copy(COLS - n).start()

    @pl.when(k == 1)
    def _():
        rs_copy(0).start()

    found_b = near_b + dot(far, pair_weights(1 - x), NT)
    pb_own[...] = jnp.where(iota((HALF // 2, 128), 1) < C, found_b[:HALF // 2], found_b[HALF // 2:])

    def sib_copy():
        return pltpu.make_async_remote_copy(
            src_ref=pb_own, dst_ref=pb_sib, send_sem=pb_s.at[0], recv_sem=pb_r.at[0],
            device_id=(2 * p + 1 - k, c), device_id_type=MESH)

    def right_copy(kk):
        return pltpu.make_async_remote_copy(
            src_ref=pb_own.at[pl.ds(HALF // 2 - 8, 8)], dst_ref=pb_left,
            send_sem=pb_s.at[1 + kk], recv_sem=pb_r.at[1],
            device_id=(2 * p + kk, lax.rem(c + 1, COLS)), device_id_type=MESH)

    def left_copy(kk):
        return pltpu.make_async_remote_copy(
            src_ref=pb_own.at[pl.ds(0, 8)], dst_ref=pb_right,
            send_sem=pb_s.at[1 + kk], recv_sem=pb_r.at[2],
            device_id=(2 * p + kk, lax.rem(c + COLS - 1, COLS)), device_id_type=MESH)

    sends_right = (k == 1) & (c < COLS - 1)
    sends_left = (k == 0) & (c > 0)
    sib_copy().start()

    @pl.when(sends_right)
    def _():
        right_copy(0).start()
        right_copy(1).start()

    @pl.when(sends_left)
    def _():
        left_copy(0).start()
        left_copy(1).start()

    sib_copy().wait_recv()

    @pl.when(c > 0)
    def _():
        right_copy(0).wait_recv()

    @pl.when(c < COLS - 1)
    def _():
        left_copy(0).wait_recv()

    zero8 = jnp.zeros((8, 128), F32)
    own, sib = pb_own[...], pb_sib[...]
    even = k == 0
    pb_buf[0:8] = jnp.where(c > 0, pb_left[...], zero8)
    pb_buf[8:72] = jnp.where(even, own, sib)
    pb_buf[72:136] = jnp.where(even, sib, own)
    pb_buf[136:144] = jnp.where(c < COLS - 1, pb_right[...], zero8)
    pb_buf[144:152] = zero8
    column_part(pb_buf, taps, pb_mid, b_part)

    def pa_copy(row, col, slot, sem):
        return pltpu.make_async_remote_copy(
            src_ref=pa_own, dst_ref=pa_land.at[slot],
            send_sem=pa_s.at[sem], recv_sem=pa_r.at[slot],
            device_id=(row, col), device_id_type=MESH)

    def pa_whole(n, sem):
        part = pb_buf.at[pl.ds(0, 8 * n)]
        return pltpu.make_async_remote_copy(
            src_ref=part, dst_ref=part, send_sem=pa_s.at[sem], recv_sem=pa_r.at[0],
            device_id=(2 * p + 1 - k, c), device_id_type=MESH)

    targets = (
        (2 * p, c + 1, c <= 4),
        (2 * p + 1, c - 3, c >= 3),
        (2 * p - 1, 5, (c == 0) & (p > 0)),
        (2 * p + 2, 0, (c == COLS - 1) & (p < ROWS // 2 - 1)),
    )
    w_o.wait()
    w_pa.wait()

    @pl.when(k == 0)
    def _():
        land[pl.ds(c, 1)] = msg[pl.ds(c, 1)]

        rs_whole(2 * COLS - 1).wait_recv()
        got = [land[g].astype(F32) for g in range(2 * COLS)]
        stat = jnp.concatenate([x[80:88] for x in got], axis=0).astype(BF16)
        a, b = iota((128, 128), 0), iota((128, 128), 1)
        same = (a & (H - 1)) == (b & (H - 1))
        pick_top = jnp.where(same & (a < 48), 1.0, 0.0).astype(BF16)
        pick_total = jnp.where(same & (a >= 48) & (a < 80), 1.0, 0.0).astype(BF16)
        picked = dot(stat, jnp.concatenate([pick_top, pick_total], axis=1))
        top, total = picked[:, :128], picked[:, 128:]
        tops = [top[8 * g:8 * g + 8] for g in range(2 * COLS)]
        summit = functools.reduce(jnp.maximum, tops)
        scales = [jnp.exp(x - summit) for x in tops]
        whole = sum(s * total[8 * g:8 * g + 8] for g, s in enumerate(scales))
        factor = jnp.concatenate([s / whole for s in scales], axis=0)
        high = factor.astype(BF16).astype(F32)
        factor = jnp.where(b < H, high, jnp.where(b < 2 * H, factor - high, 0.0)).astype(BF16)
        factors = dot(factor, spread[...])
        attended = []
        for t in range(10):
            attended.append(sum(
                got[g][8 * t:8 * t + 8] * factors[8 * g:8 * g + 8, 128 * t:128 * t + 128]
                for g in range(2 * COLS)))
        attended = jnp.concatenate(attended, axis=1).astype(BF16)
        hidden = fa_rows[pl.ds(pl.multiple_of(8 * c, 8), 8), :] + dot(attended, wo[...])
        centre = hidden - jnp.mean(hidden, axis=1, keepdims=True)
        spread_h = jnp.mean(centre * centre, axis=1, keepdims=True)
        normed = (centre * lax.rsqrt(spread_h + 1e-5)).astype(BF16)
        pa_own[...] = dot(normed, jnp.concatenate([wpa[...], wpa[...]], axis=0), NT)
        for n, (row, slot, on) in enumerate(targets):
            @pl.when(on)
            def _():
                @pl.loop(0, COLS)
                def _(m):
                    col = col_peer(COLS - 1 - m)
                    local = (row == r) & (col == c)

                    @pl.when(local)
                    def _():
                        pa_land[pl.ds(slot, 1)] = pa_own[...][None]

                    @pl.when(jnp.logical_not(local))
                    def _():
                        pa_copy(row, col, slot, n).start()

    fb_some(ROWS - 1, 0).wait_send()
    fa_whole().wait_send()
    fa_sibling().wait_send()
    sib_copy().wait_send()

    @pl.when(sends_right)
    def _():
        right_copy(0).wait_send()
        right_copy(1).wait_send()

    @pl.when(sends_left)
    def _():
        left_copy(0).wait_send()
        left_copy(1).wait_send()

    @pl.when(k == 0)
    def _():
        rs_whole(COLS - 1).wait_send()

    @pl.when(k == 1)
    def _():
        rs_whole(COLS).wait_send()

    mean = mean_matrix(256)
    qq = iota((QW, 128), 0)
    in_map = ((qq > 0) | (c > 0)) & ((qq < HALF + 1) | (c < COLS - 1))
    first = functools.partial(
        first_blocks, r=r, in_map=in_map, mean=mean, pa_buf=pa_buf, pb_mid=pb_mid, b_part=b_part,
        a_mid=a_mid, a_edge=a_edge, point_w=point_w, f1=f1)
    second = functools.partial(correlate, conv_w=conv_w, f1=f1)
    last_part = functools.partial(read_out, mean=mean, head_w=head_w, logits=logits)
    mine_slot = jnp.where((k == 0) & (c <= 4), c + 1, -1)
    pa_buf[...] = jnp.zeros_like(pa_buf)
    for s in range(1, 5):
        @pl.when(s != mine_slot)
        def _():
            pa_copy(r, c, s, 0).wait_recv()

        pa_buf[8 * s:8 * s + 8] = pa_land[s]
    row_parts(pa_buf, row_w, edge_w, a_mid, a_edge, ((4, 32),), r)
    for _ in first(list(range(4, 32, 2))):
        pass
    part1 = second(1)
    part2 = second(2)
    last_part(1, *part1)
    last_part(2, *part2)

    @pl.when(r > 0)
    def _():
        pa_copy(r, c, 0, 0).wait_recv()
        pa_buf[0:8] = pa_land[0]

    @pl.when((r < ROWS - 1) & (mine_slot != 5))
    def _():
        pa_copy(r, c, 5, 0).wait_recv()

    @pl.when(r < ROWS - 1)
    def _():
        pa_buf[40:48] = pa_land[5]

    row_parts(pa_buf, row_w, edge_w, a_mid, a_edge, ((0, 4), (32, 36)), r)
    for _ in first([0, 2, 32, 34]):
        pass
    part0 = second(0)
    part3 = second(3)
    last_part(0, *part0)
    last_part(3, *part3)
    out_ref[...] = side_by_side(logits)

    @pl.when(k == 0)
    def _():
        for n, (row, slot, on) in enumerate(targets):
            @pl.when(on & (row == r))
            def _():
                pa_whole(COLS - 1, n).wait_send()

            @pl.when(on & (row != r))
            def _():
                pa_whole(COLS, n).wait_send()


def gelu_twice(x):
    x = x.astype(BF16)
    inner = x * (BF16(0.7978845608028654) + BF16(0.035677408136300125) * (x * x))
    return x + x * jnp.tanh(inner)


def squared(x):
    x = x.astype(BF16)
    return x * x


def row_parts(pa_buf, row_w, edge_w, a_mid, a_edge, spans, r):
    place = iota((48, 128), 0) + (TILE_A * r - 8)
    pa = jnp.where((place >= 0) & (place < LA), pa_buf[...], 0.0)
    kinds = [[row_w[u:u + 1] for u in range(5)]]
    kinds += [[edge_w[n, u:u + 1] for u in range(5)] for n in range(2)]
    value = jnp.concatenate(
        [sum(w[u] * pa[4 + u:44 + u] for u in range(5)) for w in kinds], axis=0)
    value = value - near_dot(value, mean_matrix(128))
    for low, high in spans:
        a_mid[low:high] = value[low:high]
        a_edge[0, low:high] = value[40 + low:40 + high]
        a_edge[1, low:high] = value[80 + low:80 + high]


def first_blocks(rows, r, in_map, mean, pa_buf, pb_mid, b_part, a_mid, a_edge, point_w, f1):
    top, bottom = r == 0, r == ROWS - 1
    kinds = {2: jnp.where(top, 0, 2), 3: jnp.where(top, 1, 2),
             32: jnp.where(bottom, 3, 2), 33: jnp.where(bottom, 4, 2)}

    sub = iota((8, 128), 0)

    def part_of(w):
        part = b_part[kinds.get(w, 2)]
        row = a_mid[w:w + 1]
        return jnp.concatenate([
            part[:8] + jnp.where(sub == 1, a_edge[0, w:w + 1], row),
            part[8:HALF] + row,
            part[HALF:] + jnp.where(sub == 0, a_edge[1, w:w + 1], row)], axis=0)

    def start(u):
        x = jnp.concatenate([part_of(u), part_of(u + 1)], axis=1)
        return x, dot(squared(x), mean)

    def middle(x, var):
        return dot(gelu_twice(x * lax.rsqrt(var + 1e-5)), point_w[...])

    def end(u, update):
        for n in range(2):
            keep = in_map
            if u < 2:
                keep = keep & jnp.logical_not(top)
            if u >= 34:
                keep = keep & jnp.logical_not(bottom)
            field = pb_mid[...] + pa_buf[u + n + 6:u + n + 7] + update[:, 128 * n:128 * n + 128]
            f1[u + n] = jnp.where(keep, field, 0.0)

    started, updates = {}, {}
    count = len(rows)
    for n in range(count + 2):
        if n < count:
            started[n] = start(rows[n])
        if 1 <= n <= count:
            updates[n - 1] = middle(*started.pop(n - 1))
        if n >= 2:
            end(rows[n - 2], updates.pop(n - 2))
            yield rows[n - 2]


def correlate(step, conv_w, f1):
    pieces = {}
    for u in range(8 * step, 8 * step + 12):
        for q in range(3):
            pieces[u, q] = f1[u, q:q + HALF, :].astype(BF16)

    def tall(u, q):
        return jnp.concatenate([pieces[8 * step + 2 * n + u, q] for n in range(4)], axis=0)

    around = jnp.concatenate([tall(u, q) for u in range(6) for q in range(3)], axis=1)
    return dot(around, conv_w[...]), [tall(2, 1), tall(3, 1)]


def read_out(step, x, field, mean, head_w, logits):
    var = dot(squared(x), mean)
    g = gelu_twice(x * lax.rsqrt(var + 1e-5))
    found = dot(head_w[...], jnp.concatenate(field + [g], axis=1), NT)
    found = found[0:4] + found[4:8]
    for n in range(4):
        for o in range(2):
            for s in range(2):
                at = TILE_A * s + 8 * step + 2 * n + o
                logits[at:at + 1] = found[2 * o + s:2 * o + s + 1, HALF * n:HALF * n + HALF]


def side_by_side(logits):
    total = None
    for s in range(2):
        place = iota((HALF, TILE_B), 1) == 2 * iota((HALF, TILE_B), 0) + s
        place = jnp.where(place, 1.0, 0.0).astype(BF16)
        piece = near_dot(logits[TILE_A * s:TILE_A * s + TILE_A], place)
        total = piece if total is None else total + piece
    return total


def local(
    emb_a, emb_b, w_query, w_key, w_value, w_out, w_pair_a, w_pair_b, w_depth, w_point, w_logit
):
    hbm = pl.BlockSpec(memory_space=pltpu.HBM)
    vmem = pl.BlockSpec(memory_space=pltpu.VMEM)
    weight = pltpu.VMEM((E, E), BF16)
    dma = pltpu.SemaphoreType.DMA
    return pl.pallas_call(
        attention,
        out_shape=pltpu.VMEM((TILE_A, TILE_B), F32),
        in_specs=[hbm] * 11,
        out_specs=vmem,
        scratch_shapes=[
            pltpu.VMEM((48, 128), F32),
            pltpu.VMEM((QW, 128), F32),
            pltpu.VMEM((5, QW, 128), F32),
            pltpu.VMEM((8, 128), F32),
            pltpu.VMEM((2, 8, 128), F32),
            pltpu.VMEM((18 * 128, 256), BF16),
            pltpu.VMEM((256, 256), BF16),
            pltpu.VMEM((8, 512), BF16),
            pltpu.VMEM((40, 128), F32),
            pltpu.VMEM((2, 40, 128), F32),
            pltpu.VMEM((36, QW, 128), F32),
            pltpu.VMEM((2 * TILE_A, 128), F32),
            pltpu.VMEM((TILE_A, E // COLS), BF16),
            weight, weight, weight, weight,
            pltpu.VMEM((C, E), BF16),
            pltpu.VMEM((C, E), BF16),
            pltpu.VMEM((25, 2, C), F32),
            pltpu.VMEM((2, C, C), BF16),
            pltpu.VMEM((1, C), F32),
            pltpu.VMEM((2, D, HALF), BF16),
            pltpu.VMEM((ROWS, D, HALF), BF16),
            pltpu.VMEM((2, COLS, TILE_A, E // COLS), BF16),
            pltpu.VMEM((2 * TILE_A, E), F32),
            pltpu.VMEM((HALF, E), F32),
            pltpu.VMEM((HALF, E), F32),
            pltpu.VMEM((5, 8 * TILE_A, 256), BF16),
            pltpu.VMEM((128, E), BF16),
            pltpu.VMEM((COLS, 96, 128), BF16),
            pltpu.VMEM((2 * COLS, 96, 128), BF16),
            pltpu.VMEM((HALF // 2, 128), F32),
            pltpu.VMEM((HALF // 2, 128), F32),
            pltpu.VMEM((8, 128), F32),
            pltpu.VMEM((8, 128), F32),
            pltpu.VMEM((152, 128), F32),
            pltpu.VMEM((8, 128), F32),
            pltpu.VMEM((6, 8, 128), F32),
            pltpu.VMEM((2, 32, 128), F32),
            dma((12,)),
            dma, dma((2,)),
            dma((2,)), dma((2,)),
            dma, dma,
            dma((3,)), dma((3,)),
            dma((4,)), dma((6,)),
        ],
        compiler_params=pltpu.CompilerParams(
            collective_id=0, has_side_effects=True, vmem_limit_bytes=48 * 2 ** 20),
        name="contact_map",
    )(*(pltpu.with_memory_space_constraint(a, pltpu.HBM) for a in (
        emb_a, emb_b.T, w_query, w_key, w_value, w_out, w_pair_a.T, w_pair_b.T,
        jnp.transpose(w_depth, (2, 0, 1)), w_point, w_logit.reshape(1, C))))


def solution(mesh):
    in_specs = (P("row", "col"), P("col", "row"), P(), P(), P(), P(), P(), P(), P(), P(), P())
    out_specs = P("row", "col")
    return jax.shard_map(local, mesh=mesh, in_specs=in_specs, out_specs=out_specs, check_vma=False)
```

```python
import functools
import math

import jax
import jax.numpy as jnp
from jax import lax
from jax.experimental import pallas as pl
from jax.experimental.pallas import tpu as pltpu
from jax.sharding import PartitionSpec as P

E = 1280
H = 16
D = E // H
C = 64
ROWS = 16
COLS = 8
LA = 512
LB = 2048
TILE_A = LA // ROWS
TILE_B = LB // COLS
HALF = TILE_B // 2
F32 = jnp.float32
BF16 = jnp.bfloat16
MESH = pl.DeviceIdType.MESH
NN = (((1,), (0,)), ((), ()))
NT = (((1,), (1,)), ((), ()))


def dot(a, b, dims=NN):
    return lax.dot_general(a, b, dims, preferred_element_type=F32)


def iota(shape, axis):
    return lax.broadcasted_iota(jnp.int32, shape, axis)


def eye(n):
    return jnp.where(iota((n, n), 0) == iota((n, n), 1), 1.0, 0.0).astype(BF16)


def doubled(n):
    lane = iota((n, 2 * n), 1)
    lane = jnp.where(lane >= n, lane - n, lane)
    return jnp.where(iota((n, 2 * n), 0) == lane, 1.0, 0.0).astype(BF16)


def split3(x):
    high = x.astype(BF16)
    rest = x - high.astype(F32)
    mid = rest.astype(BF16)
    low = (rest - mid.astype(F32)).astype(BF16)
    return high, mid, low


def exact_dot(x, ones, dims=NN):
    return sum(dot(part, ones, dims) for part in split3(x))


def near_dot(x, ones):
    high, mid, _ = split3(x)
    return dot(high, ones) + dot(mid, ones)


QW = 136


def prepare_weights(wd, wp, wl, taps, row_w, edge_w, conv_w, point_w, head_w, c):
    double = doubled(C)
    for s in range(2):
        taps[s, 0:25] = exact_dot(wd[:, s, :], double)

    def tap(u, v):
        return taps[0, 5 * u + v:5 * u + v + 1, :]

    for u in range(5):
        row_w[u:u + 1] = sum(tap(u, v) for v in range(5))
    for n, start in enumerate((1, HALF)):
        column = 2 * start + jnp.where(iota((1, 128), 1) < C, 0, 1) + TILE_B * c - 2
        for u in range(5):
            total = None
            for v in range(5):
                at = column + (v - 2)
                piece = jnp.where((at >= 0) & (at < LB), tap(u, v), 0.0)
                total = piece if total is None else total + piece
            edge_w[n, u:u + 1] = total

    a, b = iota((128, 128), 0), iota((128, 128), 1)
    upper, left = a < C, b < C
    same = upper == left
    rest = jnp.where((a & (C - 1)) == (b & (C - 1)), 1.0 - 1.0 / C, -1.0 / C)
    columns = sum(dot(jnp.concatenate([eye(C), eye(C)], axis=0), part, NT)
                  for part in split3(wd[:, 1, :]))

    def spread(u, v):
        if not 0 <= v < 5:
            return 0.0
        return columns[:, 5 * u + v:5 * u + v + 1]

    zero = jnp.zeros((128, 128), BF16)
    for q in range(3):
        blocks = []
        for u in range(5):
            block = jnp.where(same, spread(u, 2 * q),
                              jnp.where(upper, spread(u, 2 * q - 1), spread(u, 2 * q + 1)))
            blocks.append((block * rest).astype(BF16))
        for u in range(6):
            at = 128 * (3 * u + q)
            conv_w[at:at + 128, 0:128] = blocks[u] if u < 5 else zero
            conv_w[at:at + 128, 128:256] = blocks[u - 1] if u > 0 else zero

    point = dot(wp[0], double)
    point = jnp.concatenate([point, point], axis=1)
    point = jnp.concatenate([point] * 4, axis=0)
    fits = (iota((256, 256), 0) // C) == (iota((256, 256), 1) // C)
    point_w[...] = jnp.where(fits, 0.5 * point, 0.0).astype(BF16)

    read = jnp.broadcast_to(wl[...], (8, C))
    folded = 0.5 * sum(dot(part, wp[1], NT) for part in split3(read))
    row8, lane8 = iota((8, 256), 0), iota((8, 256), 1)
    fits8 = (row8 & 3) == (lane8 // C)
    for n, values in enumerate((read, folded)):
        both = exact_dot(values, double)
        both = jnp.concatenate([both, both], axis=1)
        high = both.astype(BF16).astype(F32)
        picked = jnp.where(row8 < 4, high, both - high)
        head_w[:, 256 * n:256 * n + 256] = jnp.where(fits8, picked, 0.0).astype(BF16)


def mean_matrix(n):
    fits = (iota((n, n), 0) // C) == (iota((n, n), 1) // C)
    return jnp.where(fits, 1.0 / C, 0.0).astype(BF16)


def column_part(pb_buf, taps, pb_mid, b_part):
    mean = mean_matrix(128)
    left = iota((1, 128), 1) < C
    plain = [pb_buf[6 + q:6 + q + QW] for q in range(3)]
    pb_mid[...] = plain[1]
    crossed = [pltpu.roll(x, C, 1) for x in plain]

    for n, (low, high) in enumerate(((2, 5), (1, 5), (0, 5), (0, 4), (0, 3))):
        w = [sum(taps[0, 5 * u + v:5 * u + v + 1, :] for u in range(low, high)) for v in range(5)]
        value = (w[0] * plain[0] + w[2] * plain[1] + w[4] * plain[2]
                 + jnp.where(left, w[1], 0.0) * crossed[0]
                 + jnp.where(left, w[3], w[1]) * crossed[1]
                 + jnp.where(left, 0.0, w[3]) * crossed[2])
        b_part[n] = value - near_dot(value, mean)


def attention(
    ea_h, eb_h, wq_h, wk_h, wv_h, wo_h, wpa_h, wpb_h, wd_h, wp_h, wl_h,
    out_ref,
    pa_buf, pb_mid, b_part, row_w, edge_w, conv_w, point_w, head_w, a_mid, a_edge, f1, logits,
    ea, wq, wk, wv, wo, wpa, wpb, wd, wp, wl,
    fb_src, fb_all, fa_all, fa_rows, keys, values, masked, spread, pick, wpa2, msg, land,
    pb_own, pb_sib, pb_left, pb_right, pb_buf, pa_own, pa_land, taps,
    in_sem, fb_s, fb_r, fa_s, fa_r, rs_s, rs_r, pb_s, pb_r, pa_s, pa_r,
):
    r = lax.axis_index("row")
    c = lax.axis_index("col")
    k = lax.rem(r, 2)
    p = lax.div(r, 2)
    mine = k * COLS + c

    loads = [
        pltpu.make_async_copy(src, dst, in_sem.at[i])
        for i, (src, dst) in enumerate(
            [(eb_h.at[:, pl.ds(0, HALF)], fb_src.at[0]), (eb_h.at[:, pl.ds(HALF, HALF)], fb_src.at[1]),
             (ea_h, ea), (wd_h, wd), (wp_h, wp), (wl_h, wl), (wk_h, wk), (wv_h, wv),
             (wpb_h, wpb), (wq_h, wq), (wo_h, wo), (wpa_h, wpa)]
        )
    ]
    for load in loads[:3]:
        load.start()
    w_eb0, w_eb1, w_ea, w_d, w_p, w_l, w_k, w_v, w_pb, w_q, w_o, w_pa = loads

    x, y = lax.div(r, 8), lax.rem(p, 4)
    z, xl = lax.div(c, 2), lax.rem(c, 2)

    def row_peer(e):
        return (lax.rem(x + lax.div(e, 8), 2) * 8 + lax.rem(y + lax.rem(lax.div(e, 2), 4), 4) * 2
                + lax.rem(k + lax.rem(e, 2), 2))

    def col_peer(e):
        return lax.rem(z + lax.rem(lax.div(e, 2), 4), 4) * 2 + lax.rem(xl + lax.rem(e, 2), 2)

    barrier = pltpu.get_barrier_semaphore()

    def greet(row, col):
        pl.semaphore_signal(barrier, inc=1, device_id=(row, col), device_id_type=MESH)

    @pl.loop(1, ROWS)
    def _(n):
        e = ROWS - n
        greet(row_peer(e), c)
        greet(2 * p + lax.rem(k + lax.div(e, 8), 2), col_peer(e))

    @pl.when((k == 1) & (r < ROWS - 1))
    def _():
        greet(r + 1, 0)

    @pl.when((k == 0) & (r > 0))
    def _():
        greet(r - 2, COLS - 1)

    for load in loads[3:]:
        load.start()

    w_eb0.wait()
    w_eb1.wait()
    fb_all[pl.ds(r, 1)] = fb_src[pl.ds(k, 1)]
    w_ea.wait()
    fa_all[pl.ds(k, 1), pl.ds(c, 1)] = ea[...][None, None]

    first = (k == 0) & (c == 0) & (p > 0)
    last = (k == 0) & (c == COLS - 1) & (p < ROWS // 2 - 1)
    extra = jnp.where(first, COLS, 0) + jnp.where(last, COLS, 0)
    pl.semaphore_wait(barrier, 2 * (ROWS - 1) + extra)

    def fb_copy(e):
        to = row_peer(e)
        return pltpu.make_async_remote_copy(
            src_ref=fb_src.at[lax.rem(to, 2)], dst_ref=fb_all.at[r],
            send_sem=fb_s, recv_sem=fb_r.at[lax.div(e, 8)],
            device_id=(to, c), device_id_type=MESH)

    def fb_some(n, far):
        part = fb_all.at[pl.ds(0, n)]
        return pltpu.make_async_remote_copy(
            src_ref=part, dst_ref=part, send_sem=fb_s, recv_sem=fb_r.at[far],
            device_id=(2 * p + 1 - k, c), device_id_type=MESH)

    def fa_whole():
        part = fa_all.at[0, pl.ds(0, COLS - 1)]
        return pltpu.make_async_remote_copy(
            src_ref=part, dst_ref=part, send_sem=fa_s.at[1], recv_sem=fa_r.at[1],
            device_id=(2 * p + 1 - k, c), device_id_type=MESH)

    def fa_copy(e):
        return pltpu.make_async_remote_copy(
            src_ref=ea, dst_ref=fa_all.at[k, c],
            send_sem=fa_s.at[1], recv_sem=fa_r.at[1],
            device_id=(r, col_peer(e)), device_id_type=MESH)

    def fa_sibling():
        return pltpu.make_async_remote_copy(
            src_ref=fa_all.at[k], dst_ref=fa_all.at[k],
            send_sem=fa_s.at[0], recv_sem=fa_r.at[0],
            device_id=(2 * p + 1 - k, c), device_id_type=MESH)

    @pl.loop(1, COLS)
    def _(n):
        fa_copy(COLS - n).start()

    @pl.loop(1, ROWS)
    def _(n):
        fb_copy(ROWS - n).start()

    w_d.wait()
    w_p.wait()
    w_l.wait()
    prepare_weights(wd, wp, wl, taps, row_w, edge_w, conv_w, point_w, head_w, c)
    l, f = iota((128, E), 0), iota((128, E), 1)
    start = (l & (H - 1)) * D
    spread[...] = jnp.where((l < 2 * H) & (f >= start) & (f < start + D), 1.0, 0.0).astype(BF16)

    fa_whole().wait_recv()
    fa_sibling().start()

    n0, n1 = iota((HALF, HALF), 0), iota((HALF, HALF), 1)
    order = jnp.where(n0 < HALF // 2, 2 * n0, 2 * n0 - (HALF - 1))
    order = jnp.where(n1 == order, 1.0, 0.0).astype(BF16)

    def features(side):
        blocks = fb_all[pl.ds(8 * side, 8)].reshape(E // 2, HALF)
        return dot(order, blocks, NT).astype(BF16)

    def some_rows(side):
        return pl.ds(pl.multiple_of(side * (E // 2), 128), E // 2)

    def pair_weights(side):
        part = wpb[:, some_rows(side)]
        return jnp.concatenate([part, part], axis=0)

    fb_some(7, 0).wait_recv()
    w_k.wait()
    w_v.wait()
    w_pb.wait()
    near = features(x)
    for t in range(5):
        at = slice(256 * t, 256 * t + 256)
        keys[:, at] = dot(near, wk[some_rows(x), at])
        values[:, at] = dot(near, wv[some_rows(x), at])
    near_b = dot(near, pair_weights(x), NT)

    fa_sibling().wait_recv()
    fa = jnp.concatenate(
        [jnp.concatenate([fa_all[kk, cc].astype(F32) for cc in range(COLS)], axis=1)
         for kk in range(2)], axis=0)
    fa_rows[...] = fa
    w_q.wait()
    query = dot(fa.astype(BF16), wq[...]).astype(BF16).astype(F32)

    rows = 2 * TILE_A
    lane256 = iota((rows, 256), 1)

    def heads_of(t):
        return range(3 * t, 3 * t + 4)

    def inside(h, t):
        return (lane256 >= D * h - 256 * t) & (lane256 < D * h + D - 256 * t)

    spans = [slice(256 * t, 256 * t + 256) for t in range(5)]
    for t in range(5):
        masked[t] = jnp.concatenate([jnp.where(inside(h, t), query[:, spans[t]], 0.0)
                                     for h in heads_of(t)], axis=0).astype(BF16)

    fb_some(8, 1).wait_recv()
    far = features(1 - x)
    key_parts = [keys[:, at] + dot(far, wk[some_rows(1 - x), at]) for at in spans]
    founds = [dot(masked[t], key_parts[t].astype(BF16), NT) for t in range(5)]
    value_parts = [values[:, at] + dot(far, wv[some_rows(1 - x), at]) for at in spans]
    scores = [None] * H
    for t in range(5):
        for n, h in enumerate(heads_of(t)):
            piece = founds[t][rows * n:rows * n + rows]
            scores[h] = piece if scores[h] is None else scores[h] + piece

    lane = iota((rows, 128), 1)
    head_of = lane & (H - 1)
    tops = jnp.zeros((rows, 128), F32)
    totals = jnp.zeros((rows, 128), F32)
    weights = []
    for h in range(H):
        s = scores[h] * (1.0 / math.sqrt(D))
        top = jnp.max(s, axis=1, keepdims=True)
        w = jnp.exp(s - top)
        tops = jnp.where(head_of == h, top, tops)
        totals = jnp.where(head_of == h, jnp.sum(w, axis=1, keepdims=True), totals)
        weights.append(w.astype(BF16))
    founds = [dot(jnp.concatenate(weights[3 * t:3 * t + 4], axis=0), value_parts[t].astype(BF16))
              for t in range(5)]
    t1, t2, t3 = (x.astype(F32) for x in split3(tops))
    n1, n2, _ = (x.astype(F32) for x in split3(totals))
    stats = jnp.where(lane < 16, t1, jnp.where(lane < 32, t2, jnp.where(
        lane < 48, t3, jnp.where(lane < 64, n1, jnp.where(lane < 80, n2, 0.0)))))

    mixed = []
    for t in range(5):
        total = sum(jnp.where(inside(h, t), founds[t][rows * n:rows * n + rows], 0.0)
                    for n, h in enumerate(heads_of(t)))
        mixed += [total[:, :128], total[:, 128:]]
    for d in range(COLS):
        block = [m[8 * d:8 * d + 8] for m in mixed + [stats]] + [jnp.zeros((8, 128), F32)]
        msg[d] = jnp.concatenate(block, axis=0).astype(BF16)

    def rs_copy(d):
        to = col_peer(d)
        return pltpu.make_async_remote_copy(
            src_ref=msg.at[to], dst_ref=land.at[mine],
            send_sem=rs_s, recv_sem=rs_r,
            device_id=(2 * p, to), device_id_type=MESH)

    def rs_whole(n):
        return pltpu.make_async_remote_copy(
            src_ref=land.at[pl.ds(0, n)], dst_ref=land.at[pl.ds(0, n)],
            send_sem=rs_s, recv_sem=rs_r, device_id=(2 * p + 1 - k, c), device_id_type=MESH)

    @pl.loop(1, COLS)
    def _(n):
        rs_copy(COLS - n).start()

    @pl.when(k == 1)
    def _():
        rs_copy(0).start()

    found_b = near_b + dot(far, pair_weights(1 - x), NT)
    pb_own[...] = jnp.where(iota((HALF // 2, 128), 1) < C, found_b[:HALF // 2], found_b[HALF // 2:])

    def sib_copy():
        return pltpu.make_async_remote_copy(
            src_ref=pb_own, dst_ref=pb_sib, send_sem=pb_s.at[0], recv_sem=pb_r.at[0],
            device_id=(2 * p + 1 - k, c), device_id_type=MESH)

    def right_copy(kk):
        return pltpu.make_async_remote_copy(
            src_ref=pb_own.at[pl.ds(HALF // 2 - 8, 8)], dst_ref=pb_left,
            send_sem=pb_s.at[1 + kk], recv_sem=pb_r.at[1],
            device_id=(2 * p + kk, lax.rem(c + 1, COLS)), device_id_type=MESH)

    def left_copy(kk):
        return pltpu.make_async_remote_copy(
            src_ref=pb_own.at[pl.ds(0, 8)], dst_ref=pb_right,
            send_sem=pb_s.at[1 + kk], recv_sem=pb_r.at[2],
            device_id=(2 * p + kk, lax.rem(c + COLS - 1, COLS)), device_id_type=MESH)

    sends_right = (k == 1) & (c < COLS - 1)
    sends_left = (k == 0) & (c > 0)
    sib_copy().start()

    @pl.when(sends_right)
    def _():
        right_copy(0).start()
        right_copy(1).start()

    @pl.when(sends_left)
    def _():
        left_copy(0).start()
        left_copy(1).start()

    sib_copy().wait_recv()

    @pl.when(c > 0)
    def _():
        right_copy(0).wait_recv()

    @pl.when(c < COLS - 1)
    def _():
        left_copy(0).wait_recv()

    zero8 = jnp.zeros((8, 128), F32)
    own, sib = pb_own[...], pb_sib[...]
    even = k == 0
    pb_buf[0:8] = jnp.where(c > 0, pb_left[...], zero8)
    pb_buf[8:72] = jnp.where(even, own, sib)
    pb_buf[72:136] = jnp.where(even, sib, own)
    pb_buf[136:144] = jnp.where(c < COLS - 1, pb_right[...], zero8)
    pb_buf[144:152] = zero8
    column_part(pb_buf, taps, pb_mid, b_part)

    def pa_copy(row, col, slot, sem):
        return pltpu.make_async_remote_copy(
            src_ref=pa_own, dst_ref=pa_land.at[slot],
            send_sem=pa_s.at[sem], recv_sem=pa_r.at[slot],
            device_id=(row, col), device_id_type=MESH)

    def pa_whole(n, sem):
        part = pb_buf.at[pl.ds(0, 8 * n)]
        return pltpu.make_async_remote_copy(
            src_ref=part, dst_ref=part, send_sem=pa_s.at[sem], recv_sem=pa_r.at[0],
            device_id=(2 * p + 1 - k, c), device_id_type=MESH)

    targets = (
        (2 * p, c + 1, c <= 4),
        (2 * p + 1, c - 3, c >= 3),
        (2 * p - 1, 5, (c == 0) & (p > 0)),
        (2 * p + 2, 0, (c == COLS - 1) & (p < ROWS // 2 - 1)),
    )
    w_o.wait()
    w_pa.wait()
    wpa2[0:C] = wpa[...]
    wpa2[C:2 * C] = wpa[...]
    l, f = iota((128, 256), 0), iota((128, 256), 1)
    wanted = (((f < 128) & (l < 48)) | ((f >= 128) & (l >= 48) & (l < 80))) & ((l & (H - 1)) == (f & (H - 1)))
    pick[...] = jnp.where(wanted, 1.0, 0.0).astype(BF16)

    @pl.when(k == 0)
    def _():
        land[pl.ds(c, 1)] = msg[pl.ds(c, 1)]

        rs_whole(2 * COLS - 1).wait_recv()
        got = [land[g].astype(F32) for g in range(2 * COLS)]
        stat = jnp.concatenate([x[80:88] for x in got], axis=0).astype(BF16)
        b = iota((128, 128), 1)
        picked = dot(stat, pick[...])
        top, total = picked[:, :128], picked[:, 128:]
        tops = [top[8 * g:8 * g + 8] for g in range(2 * COLS)]
        summit = functools.reduce(jnp.maximum, tops)
        scales = [jnp.exp(x - summit) for x in tops]
        whole = sum(s * total[8 * g:8 * g + 8] for g, s in enumerate(scales))
        factor = jnp.concatenate([s / whole for s in scales], axis=0)
        high = factor.astype(BF16).astype(F32)
        factor = jnp.where(b < H, high, jnp.where(b < 2 * H, factor - high, 0.0)).astype(BF16)
        factors = dot(factor, spread[...])
        attended = []
        for t in range(10):
            attended.append(sum(
                got[g][8 * t:8 * t + 8] * factors[8 * g:8 * g + 8, 128 * t:128 * t + 128]
                for g in range(2 * COLS)))
        attended = jnp.concatenate(attended, axis=1).astype(BF16)
        hidden = fa_rows[pl.ds(pl.multiple_of(8 * c, 8), 8), :] + dot(attended, wo[...])
        centre = hidden - jnp.mean(hidden, axis=1, keepdims=True)
        spread_h = jnp.mean(centre * centre, axis=1, keepdims=True)
        normed = (centre * lax.rsqrt(spread_h + 1e-5)).astype(BF16)
        pa_own[...] = dot(normed, wpa2[...], NT)
        for n, (row, slot, on) in enumerate(targets):
            @pl.when(on)
            def _():
                @pl.loop(0, COLS)
                def _(m):
                    col = col_peer(COLS - 1 - m)
                    local = (row == r) & (col == c)

                    @pl.when(local)
                    def _():
                        pa_land[pl.ds(slot, 1)] = pa_own[...][None]

                    @pl.when(jnp.logical_not(local))
                    def _():
                        pa_copy(row, col, slot, n).start()

    fb_some(ROWS - 1, 0).wait_send()
    fa_whole().wait_send()
    fa_sibling().wait_send()
    sib_copy().wait_send()

    @pl.when(sends_right)
    def _():
        right_copy(0).wait_send()
        right_copy(1).wait_send()

    @pl.when(sends_left)
    def _():
        left_copy(0).wait_send()
        left_copy(1).wait_send()

    @pl.when(k == 0)
    def _():
        rs_whole(COLS - 1).wait_send()

    @pl.when(k == 1)
    def _():
        rs_whole(COLS).wait_send()

    mean = mean_matrix(256)
    qq = iota((QW, 128), 0)
    in_map = ((qq > 0) | (c > 0)) & ((qq < HALF + 1) | (c < COLS - 1))
    first = functools.partial(
        first_blocks, r=r, in_map=in_map, mean=mean, pa_buf=pa_buf, pb_mid=pb_mid, b_part=b_part,
        a_mid=a_mid, a_edge=a_edge, point_w=point_w, f1=f1)
    second = functools.partial(correlate, conv_w=conv_w, f1=f1)
    last_part = functools.partial(read_out, mean=mean, head_w=head_w, logits=logits)
    mine_slot = jnp.where((k == 0) & (c <= 4), c + 1, -1)
    pa_buf[...] = jnp.zeros_like(pa_buf)
    for s in range(1, 5):
        @pl.when(s != mine_slot)
        def _():
            pa_copy(r, c, s, 0).wait_recv()

        pa_buf[8 * s:8 * s + 8] = pa_land[s]
    row_parts(pa_buf, row_w, edge_w, a_mid, a_edge, ((4, 32),), r)
    for _ in first(list(range(4, 32, 2))):
        pass
    part1 = second(1)
    part2 = second(2)
    last_part(1, *part1)
    last_part(2, *part2)

    @pl.when(r > 0)
    def _():
        pa_copy(r, c, 0, 0).wait_recv()
        pa_buf[0:8] = pa_land[0]

    @pl.when((r < ROWS - 1) & (mine_slot != 5))
    def _():
        pa_copy(r, c, 5, 0).wait_recv()

    @pl.when(r < ROWS - 1)
    def _():
        pa_buf[40:48] = pa_land[5]

    row_parts(pa_buf, row_w, edge_w, a_mid, a_edge, ((0, 4), (32, 36)), r)
    for _ in first([0, 2, 32, 34]):
        pass
    part0 = second(0)
    part3 = second(3)
    last_part(0, *part0)
    last_part(3, *part3)
    out_ref[...] = side_by_side(logits)

    @pl.when(k == 0)
    def _():
        for n, (row, slot, on) in enumerate(targets):
            @pl.when(on & (row == r))
            def _():
                pa_whole(COLS - 1, n).wait_send()

            @pl.when(on & (row != r))
            def _():
                pa_whole(COLS, n).wait_send()


def gelu_twice(x):
    x = x.astype(BF16)
    inner = x * (BF16(0.7978845608028654) + BF16(0.035677408136300125) * (x * x))
    return x + x * jnp.tanh(inner)


def squared(x):
    x = x.astype(BF16)
    return x * x


def row_parts(pa_buf, row_w, edge_w, a_mid, a_edge, spans, r):
    place = iota((48, 128), 0) + (TILE_A * r - 8)
    pa = jnp.where((place >= 0) & (place < LA), pa_buf[...], 0.0)
    kinds = [[row_w[u:u + 1] for u in range(5)]]
    kinds += [[edge_w[n, u:u + 1] for u in range(5)] for n in range(2)]
    value = jnp.concatenate(
        [sum(w[u] * pa[4 + u:44 + u] for u in range(5)) for w in kinds], axis=0)
    value = value - near_dot(value, mean_matrix(128))
    for low, high in spans:
        a_mid[low:high] = value[low:high]
        a_edge[0, low:high] = value[40 + low:40 + high]
        a_edge[1, low:high] = value[80 + low:80 + high]


def first_blocks(rows, r, in_map, mean, pa_buf, pb_mid, b_part, a_mid, a_edge, point_w, f1):
    top, bottom = r == 0, r == ROWS - 1
    kinds = {2: jnp.where(top, 0, 2), 3: jnp.where(top, 1, 2),
             32: jnp.where(bottom, 3, 2), 33: jnp.where(bottom, 4, 2)}

    sub = iota((8, 128), 0)

    def part_of(w):
        part = b_part[kinds.get(w, 2)]
        row = a_mid[w:w + 1]
        return jnp.concatenate([
            part[:8] + jnp.where(sub == 1, a_edge[0, w:w + 1], row),
            part[8:HALF] + row,
            part[HALF:] + jnp.where(sub == 0, a_edge[1, w:w + 1], row)], axis=0)

    def start(u):
        x = jnp.concatenate([part_of(u), part_of(u + 1)], axis=1)
        return x, dot(squared(x), mean)

    def middle(x, var):
        return dot(gelu_twice(x * lax.rsqrt(var + 1e-5)), point_w[...])

    def end(u, update):
        for n in range(2):
            keep = in_map
            if u < 2:
                keep = keep & jnp.logical_not(top)
            if u >= 34:
                keep = keep & jnp.logical_not(bottom)
            field = pb_mid[...] + pa_buf[u + n + 6:u + n + 7] + update[:, 128 * n:128 * n + 128]
            f1[u + n] = jnp.where(keep, field, 0.0)

    started, updates = {}, {}
    count = len(rows)
    for n in range(count + 2):
        if n < count:
            started[n] = start(rows[n])
        if 1 <= n <= count:
            updates[n - 1] = middle(*started.pop(n - 1))
        if n >= 2:
            end(rows[n - 2], updates.pop(n - 2))
            yield rows[n - 2]


def correlate(step, conv_w, f1):
    pieces = {}
    for u in range(8 * step, 8 * step + 12):
        for q in range(3):
            pieces[u, q] = f1[u, q:q + HALF, :].astype(BF16)

    def tall(u, q):
        return jnp.concatenate([pieces[8 * step + 2 * n + u, q] for n in range(4)], axis=0)

    around = jnp.concatenate([tall(u, q) for u in range(6) for q in range(3)], axis=1)
    return dot(around, conv_w[...]), [tall(2, 1), tall(3, 1)]


def read_out(step, x, field, mean, head_w, logits):
    var = dot(squared(x), mean)
    g = gelu_twice(x * lax.rsqrt(var + 1e-5))
    found = dot(head_w[...], jnp.concatenate(field + [g], axis=1), NT)
    found = found[0:4] + found[4:8]
    for n in range(4):
        for o in range(2):
            for s in range(2):
                at = TILE_A * s + 8 * step + 2 * n + o
                logits[at:at + 1] = found[2 * o + s:2 * o + s + 1, HALF * n:HALF * n + HALF]


def side_by_side(logits):
    total = None
    for s in range(2):
        place = iota((HALF, TILE_B), 1) == 2 * iota((HALF, TILE_B), 0) + s
        place = jnp.where(place, 1.0, 0.0).astype(BF16)
        piece = near_dot(logits[TILE_A * s:TILE_A * s + TILE_A], place)
        total = piece if total is None else total + piece
    return total


def local(
    emb_a, emb_b, w_query, w_key, w_value, w_out, w_pair_a, w_pair_b, w_depth, w_point, w_logit
):
    hbm = pl.BlockSpec(memory_space=pltpu.HBM)
    vmem = pl.BlockSpec(memory_space=pltpu.VMEM)
    weight = pltpu.VMEM((E, E), BF16)
    dma = pltpu.SemaphoreType.DMA
    return pl.pallas_call(
        attention,
        out_shape=pltpu.VMEM((TILE_A, TILE_B), F32),
        in_specs=[hbm] * 11,
        out_specs=vmem,
        scratch_shapes=[
            pltpu.VMEM((48, 128), F32),
            pltpu.VMEM((QW, 128), F32),
            pltpu.VMEM((5, QW, 128), F32),
            pltpu.VMEM((8, 128), F32),
            pltpu.VMEM((2, 8, 128), F32),
            pltpu.VMEM((18 * 128, 256), BF16),
            pltpu.VMEM((256, 256), BF16),
            pltpu.VMEM((8, 512), BF16),
            pltpu.VMEM((40, 128), F32),
            pltpu.VMEM((2, 40, 128), F32),
            pltpu.VMEM((36, QW, 128), F32),
            pltpu.VMEM((2 * TILE_A, 128), F32),
            pltpu.VMEM((TILE_A, E // COLS), BF16),
            weight, weight, weight, weight,
            pltpu.VMEM((C, E), BF16),
            pltpu.VMEM((C, E), BF16),
            pltpu.VMEM((25, 2, C), F32),
            pltpu.VMEM((2, C, C), BF16),
            pltpu.VMEM((1, C), F32),
            pltpu.VMEM((2, D, HALF), BF16),
            pltpu.VMEM((ROWS, D, HALF), BF16),
            pltpu.VMEM((2, COLS, TILE_A, E // COLS), BF16),
            pltpu.VMEM((2 * TILE_A, E), F32),
            pltpu.VMEM((HALF, E), F32),
            pltpu.VMEM((HALF, E), F32),
            pltpu.VMEM((5, 8 * TILE_A, 256), BF16),
            pltpu.VMEM((128, E), BF16),
            pltpu.VMEM((128, 256), BF16),
            pltpu.VMEM((2 * C, E), BF16),
            pltpu.VMEM((COLS, 96, 128), BF16),
            pltpu.VMEM((2 * COLS, 96, 128), BF16),
            pltpu.VMEM((HALF // 2, 128), F32),
            pltpu.VMEM((HALF // 2, 128), F32),
            pltpu.VMEM((8, 128), F32),
            pltpu.VMEM((8, 128), F32),
            pltpu.VMEM((152, 128), F32),
            pltpu.VMEM((8, 128), F32),
            pltpu.VMEM((6, 8, 128), F32),
            pltpu.VMEM((2, 32, 128), F32),
            dma((12,)),
            dma, dma((2,)),
            dma((2,)), dma((2,)),
            dma, dma,
            dma((3,)), dma((3,)),
            dma((4,)), dma((6,)),
        ],
        compiler_params=pltpu.CompilerParams(
            collective_id=0, has_side_effects=True, vmem_limit_bytes=48 * 2 ** 20),
        name="contact_map",
    )(*(pltpu.with_memory_space_constraint(a, pltpu.HBM) for a in (
        emb_a, emb_b.T, w_query, w_key, w_value, w_out, w_pair_a.T, w_pair_b.T,
        jnp.transpose(w_depth, (2, 0, 1)), w_point, w_logit.reshape(1, C))))


def solution(mesh):
    in_specs = (P("row", "col"), P("col", "row"), P(), P(), P(), P(), P(), P(), P(), P(), P())
    out_specs = P("row", "col")
    return jax.shard_map(local, mesh=mesh, in_specs=in_specs, out_specs=out_specs, check_vma=False)
```
